32 devices in a mesh: dp: 8 (over y, x, core), expert: 4 (over z).
Axes of the slice: x: 2, y: 2, z: 4, core: 2. Of those that a mesh axis runs over, the one named last changes fastest.
Arguments:
- grad_out: bfloat16 [4096, 2048], P(('dp', 'expert')), may hold values from -6 to 6
- expert_ids: int32 [4096, 8], P(('dp', 'expert')), may hold values from 0 to 15, all different within a row; in each aligned block of 128 rows (0 to 127, 128 to 255, ...) at most 72 rows name the same one
- route_weights: bfloat16 [4096, 8], P(('dp', 'expert')), may hold values from 0.049804688 to 0.5
- hidden_cache: bfloat16 [8, 16, 4, 72, 768], P('dp', 'expert'), may hold values from -0.29882812 to 0.29882812
- w_down: bfloat16 [16, 768, 2048], P('expert', 'dp'), may hold values from -0.21875 to 0.21875
Outputs:
- grad_hidden: bfloat16 [8, 16, 4, 72, 768], P('dp', 'expert')
- grad_down: bfloat16 [16, 768, 2048], P('expert', 'dp')
- grad_probs: float32 [4096, 8], P(('dp', 'expert'))
The draws below stay inside these ranges and needn't reach their ends.
Inputs may be any that keep to these rules, and one draw needn't show every extreme that they name: `expert_ids`: in each aligned block of 128 rows (the rows of one device) every row names 8 different experts and no expert is named by more than 72 rows; some expert is named by exactly 72 rows in some blocks.
All inputs are finite; a program needn't handle non-finite values.
Results may differ from the reference program's by a relative error of at most 0.012.
Values may be sent and summed in bfloat16 or wider, within the bound.
No kernel may reach another device: no remote copies, remote signals or barrier semaphores. Data moves between devices by JAX's collectives and lax.ppermute only.
A program may use at most 128 MiB of HBM per device.

```python
import math
import jax
import jax.numpy as jnp
import numpy as np
from jax import lax

D = 2048
FF = 768
EXPERTS = 16
TOP = 8
TOK_DEV = 128
CAP = 72
SOURCES = 4
TOKENS = 4096
N_DP = 8


def strengthened(entries, key, source, target, shards_of, factor):
    owner, partner = [(jnp.arange(entries.shape[dim]) // (entries.shape[dim] // shards_of)).reshape([-1 if axis == dim else 1 for axis in range(entries.ndim)]) for dim in (source, target)]
    chosen = jax.random.permutation(key, shards_of)[partner]
    strong = (owner == chosen) | (owner == (partner + shards_of // 2) % shards_of)
    return jnp.where(strong, factor * entries, entries)


def shard_levels(stream_key, extent, pieces, smallest, high):
    loudness = 1.0
    for axis_at, blocks in pieces:
        draws = jax.random.uniform(jax.random.fold_in(jax.random.fold_in(stream_key, 6), axis_at), (blocks,), jnp.float32, smallest / len(pieces), high / len(pieces))
        loudness = loudness * jnp.repeat(jnp.exp(draws), extent[axis_at] // blocks).reshape((-1,) + (1,) * (len(extent) - 1 - axis_at))
    return loudness


def routed_block(stream_key, own, number, rows, count, top, reach, skew):
    sequence = jax.random.permutation(stream_key, count)
    packed, usual = shares(count, rows * top, reach, skew, True), shares(count, rows * top, reach, skew, False)
    places = jnp.arange(count)

    def named(sizes, rotation):
        used = int((sizes > 0).sum())
        fixed = max(1, used // 4)
        shifted = fixed + (places - fixed + rotation * (used - fixed)) % max(1, count - fixed)
        return jnp.zeros((count,), jnp.int32).at[sequence[jnp.where(places < fixed, places, shifted)]].set(jnp.asarray(sizes, jnp.int32))

    sizes = jnp.where(number % 4 == 0, named(packed, number // 4), named(usual, number - number // 4 - 1))
    mixed = jax.random.permutation(jax.random.fold_in(own, 3), count)
    donor, receiver = mixed[0:count // 2 * 2:2], mixed[1:count // 2 * 2:2]
    room = jnp.minimum(sizes[donor] - 1, reach - sizes[receiver]) // 2
    room = jnp.where((donor == sequence[0]) | (receiver == sequence[0]) | (sizes[receiver] == 0), 0, jnp.maximum(room, 0))
    shifted = jax.random.randint(jax.random.fold_in(own, 4), (count // 2,), 0, 1 << 20) % (room + 1)
    sizes = sizes.at[donor].add(-shifted).at[receiver].add(shifted)
    items = jnp.searchsorted(jnp.cumsum(sizes), jnp.arange(rows * top), side="right").astype(jnp.int32)
    listing = items.reshape(top, rows).T
    listing = listing[jax.random.permutation(jax.random.fold_in(own, 1), rows)]
    rotation = jax.random.randint(jax.random.fold_in(own, 2), (rows, 1), 0, top)
    return jnp.take_along_axis(listing, (jnp.arange(top)[None, :] + rotation) % top, axis=1)


def shares(amount, total, reach, lean, full):
    portions = [(1 << 20) // math.isqrt(standing ** lean) + 1 for standing in range(1, amount + 1)]
    largest = reach if full else min(reach, max(-(-total // amount), total * portions[0] // sum(portions)))
    least = 1 if total - largest >= amount - 1 else 0
    holding, surplus = [largest] + [least] * (amount - 1), total - largest - least * (amount - 1)
    while surplus > 0:
        candidates = [i for i in range(1, amount) if holding[i] < largest] or [i for i in range(1, amount) if holding[i] < reach]
        pool, budget = sum([portions[i] for i in candidates]), surplus
        for i in candidates:
            more = min(reach - holding[i], max(1, budget * portions[i] // pool), surplus)
            holding[i] = holding[i] + more
            surplus = surplus - more
    return np.array(holding)


def centred(key, shape, width, limit, pieces=(), held_as=jnp.bfloat16):
    values = width * jax.random.normal(key, shape, jnp.float32)
    if pieces:
        values = values * shard_levels(key, shape, pieces, -0.22, 0.18)
    return jnp.clip(values, -limit, limit).astype(held_as)


def noise_with(stream_key, extent, spread, most, split, heavy, held_as=jnp.bfloat16):
    entries = spread * jax.random.normal(stream_key, extent, jnp.float32)
    if split:
        entries = entries * shard_levels(stream_key, extent, split, -0.22, 0.18)
    return jnp.clip(strengthened(entries, jax.random.fold_in(stream_key, 3), *heavy), -most, most).astype(held_as)


def setup_inputs(seed: int = 0) -> dict:
    seeds = jax.random.split(jax.random.key(seed), 6)
    grad_out = centred(seeds[0], (TOKENS, D), 1.0, 6.0, ((0, 32),))
    expert_ids_keys = jax.random.split(jax.random.fold_in(seeds[1], 1), TOKENS // TOK_DEV)
    expert_ids_turns = jax.random.permutation(jax.random.fold_in(seeds[1], 3), TOKENS // TOK_DEV)
    expert_ids = jax.vmap(lambda own, number: routed_block(jax.random.fold_in(seeds[1], 2), own, number, TOK_DEV, EXPERTS, TOP, CAP, 1))(expert_ids_keys, expert_ids_turns).reshape((TOKENS, TOP))
    route_weights = jnp.clip(jnp.exp(math.log(0.5) - 2.306499 * jax.random.uniform(seeds[2], (TOKENS, TOP), jnp.float32) ** shard_levels(seeds[2], (TOKENS, TOP), ((0, 32),), -0.2, 0.2)), 0.049804688, 0.5).astype(jnp.bfloat16)
    hidden_cache = noise_with(seeds[3], (N_DP, EXPERTS, SOURCES, CAP, FF), 0.05, 0.29882812, ((0, 8), (1, 4)), (0, 4, 8, 2.0))
    w_down = centred(seeds[4], (EXPERTS, FF, D), FF ** -0.5, 0.21875, ((0, 4), (1, 8)))
    return {"grad_out": grad_out, "expert_ids": expert_ids, "route_weights": route_weights, "hidden_cache": hidden_cache, "w_down": w_down}


def route_table(expert_ids):
    routed = expert_ids.reshape(-1).astype(jnp.int32)
    total_routes = routed.shape[0]
    onehot = (routed[:, None] == jnp.arange(EXPERTS, dtype=jnp.int32)[None, :]).astype(jnp.int32)
    before = (jnp.cumsum(onehot, axis=0) - onehot).astype(jnp.int32)
    slot_rank = jnp.sum(before * onehot, axis=1).astype(jnp.int32)
    target = (routed * CAP + slot_rank).astype(jnp.int32)
    route_of = jnp.zeros((EXPERTS * CAP,), jnp.int32).at[target].set(jnp.arange(total_routes, dtype=jnp.int32))
    filled = jnp.zeros((EXPERTS * CAP,), jnp.int32).at[target].set(1)
    return target, route_of, filled


def reference(grad_out, expert_ids, route_weights, hidden_cache, w_down):
    groups = hidden_cache.shape[0]
    sources = hidden_cache.shape[2]
    grad_blocks = grad_out.reshape(groups, sources, TOK_DEV, D)
    id_blocks = expert_ids.reshape(groups, sources, TOK_DEV, TOP)
    weight_blocks = route_weights.reshape(groups, sources, TOK_DEV * TOP)
    down_f = w_down.astype(jnp.float32)

    def one_group(carry, inputs):
        grads, ids_here, routing, cache = inputs
        target, route_of, filled = jax.vmap(route_table)(ids_here)
        token_rows = (route_of // TOP).astype(jnp.int32)
        received = jnp.take_along_axis(grads, token_rows[:, :, None], axis=1)
        received = jnp.where(filled[:, :, None] > 0, received, jnp.zeros_like(received))
        weights_in = jnp.take_along_axis(routing, route_of, axis=1)
        weights_in = jnp.where(filled > 0, weights_in, jnp.zeros_like(weights_in))
        received = received.reshape(sources, EXPERTS, CAP, D).transpose(1, 0, 2, 3)
        weights_in = weights_in.reshape(sources, EXPERTS, CAP).transpose(1, 0, 2)
        back = jnp.einsum("escd,efd->escf", received.astype(jnp.float32), down_f)
        hidden = cache.astype(jnp.float32)
        weight_f = weights_in.astype(jnp.float32)[..., None]
        grad_hidden = (weight_f * back).astype(jnp.bfloat16)
        slot_grads = jnp.sum(back * hidden, axis=-1)
        scaled = (weight_f * received.astype(jnp.float32)).astype(jnp.bfloat16)
        part = jnp.einsum("escf,escd->efd", hidden, scaled.astype(jnp.float32)).astype(jnp.bfloat16)
        carry = carry + part.astype(jnp.float32)
        per_source = slot_grads.transpose(1, 0, 2).reshape(sources, EXPERTS * CAP)
        grad_probs = jnp.take_along_axis(per_source, target, axis=1)
        return carry, (grad_hidden, grad_probs)

    start = jnp.zeros((EXPERTS, FF, D), jnp.float32)
    total, outputs = lax.scan(one_group, start, (grad_blocks, id_blocks, weight_blocks, hidden_cache))
    grad_hidden, grad_probs = outputs
    return grad_hidden, total.astype(jnp.bfloat16), grad_probs.reshape(-1, TOP)
```

```python
import functools

import jax
import jax.numpy as jnp
from jax import lax
from jax.experimental import pallas as pl
from jax.experimental.pallas import tpu as pltpu
from jax.sharding import PartitionSpec as P

EXPERTS = 16
CAP = 72
BF = jnp.bfloat16
F32 = jnp.float32


def iota(shape, dim):
    return lax.broadcasted_iota(jnp.int32, shape, dim)


def hidden_kernel(n, sc_ref, tab_ref, hid_ref, hst_ref, wt_ref, rank_ref):
    experts, toks = tab_ref.shape[2], tab_ref.shape[3]
    wt = tab_ref[0, 0].astype(F32)
    named = wt > 0
    earlier = (iota((toks, toks), 0) < iota((toks, toks), 1)).astype(BF)
    rank = jnp.dot(named.astype(F32).astype(BF), earlier, preferred_element_type=F32)
    slots = iota((CAP, toks), 0).astype(F32)
    for e in range(experts):
        w_row, r_row = wt[e : e + 1], rank[e : e + 1]
        place = jnp.where(slots == r_row, w_row, 0.0).astype(BF)
        moved = lax.dot_general(
            hid_ref[0, e, 0], place, (((0,), (0,)), ((), ())), preferred_element_type=F32
        )
        hst_ref[e] = moved.astype(BF)
        wt_ref[0, e] = w_row
        rank_ref[0, e] = r_row


def hidden_to_tokens(n, scalars, table, hid, f):
    experts, toks = table.shape[2], table.shape[3]
    src = lambda k, sc: lax.rem(sc[0] + n - k, n)
    row = jax.ShapeDtypeStruct((n, experts, 1, toks), F32)
    row_spec = pl.BlockSpec((1, experts, 1, toks), lambda k, sc: (k, 0, 0, 0))
    return pl.pallas_call(
        functools.partial(hidden_kernel, n),
        out_shape=(jax.ShapeDtypeStruct((experts, f, n * toks), BF), row, row),
        grid_spec=pltpu.PrefetchScalarGridSpec(
            num_scalar_prefetch=1,
            grid=(n,),
            in_specs=[
                pl.BlockSpec((1, 1, experts, toks), lambda k, sc: (sc[2] * n + src(k, sc), sc[0], 0, 0)),
                pl.BlockSpec((1, experts, 1, CAP, f), lambda k, sc: (0, 0, src(k, sc), 0, sc[1])),
            ],
            out_specs=(
                pl.BlockSpec((experts, f, toks), lambda k, sc: (0, 0, k)),
                row_spec,
                row_spec,
            ),
        ),
        cost_estimate=pl.CostEstimate(
            flops=2 * n * experts * CAP * f * toks, bytes_accessed=4 * n * experts * f * toks, transcendentals=0
        ),
    )(scalars, table, hid)


def back_kernel(n, sc_ref, tok0_ref, tok1_ref, w_ref, hid_ref, wt_ref, rank_ref, gh_ref, sg_ref):
    toks = wt_ref.shape[3]
    half = tok0_ref.shape[1]
    over_d = (((1,), (1,)), ((), ()))
    z = lax.dot_general(tok0_ref[...], w_ref[0, :, :half], over_d, preferred_element_type=F32)
    z = z + lax.dot_general(tok1_ref[...], w_ref[0, :, half:], over_d, preferred_element_type=F32)
    eye = iota((toks, toks), 0) == iota((toks, toks), 1)
    slots = iota((CAP, toks), 0).astype(F32)
    for k in range(n):
        s = lax.rem(sc_ref[0] + n - k, n)
        w_row, r_row = wt_ref[k, 0], rank_ref[k, 0]
        pick = jnp.where((slots == r_row) & (w_row > 0), 1.0, 0.0).astype(BF)
        w_col = jnp.sum(jnp.where(eye, w_row, 0.0), axis=1, keepdims=True)
        zk = z[k * toks : (k + 1) * toks]
        weighted = (zk * w_col).astype(BF)
        gh_ref[0, s] = jnp.dot(pick, weighted, preferred_element_type=F32).astype(BF)
        hid = lax.dot_general(
            pick, hid_ref[0, 0, s], (((0,), (0,)), ((), ())), preferred_element_type=F32
        )
        sg_col = jnp.sum(zk * hid, axis=1, keepdims=True)
        sg_ref[s, 0] = jnp.sum(jnp.where(eye, sg_col, 0.0), axis=0, keepdims=True)


def backward(n, scalars, tok0, tok1, w, hid, wt, rank):
    experts, f, d = w.shape
    rows, half = tok0.shape
    toks = wt.shape[3]
    row_spec = pl.BlockSpec((n, 1, 1, toks), lambda e, sc: (0, e, 0, 0))
    whole = pl.BlockSpec((rows, half), lambda e, sc: (0, 0))
    return pl.pallas_call(
        functools.partial(back_kernel, n),
        out_shape=(
            jax.ShapeDtypeStruct((experts, n, CAP, f), BF),
            jax.ShapeDtypeStruct((n, experts, 1, toks), F32),
        ),
        grid_spec=pltpu.PrefetchScalarGridSpec(
            num_scalar_prefetch=1,
            grid=(experts,),
            in_specs=[
                whole,
                whole,
                pl.BlockSpec((1, f, d), lambda e, sc: (e, 0, 0)),
                pl.BlockSpec((1, 1, n, CAP, f), lambda e, sc: (0, e, 0, 0, sc[1])),
                row_spec,
                row_spec,
            ],
            out_specs=(pl.BlockSpec((1, n, CAP, f), lambda e, sc: (e, 0, 0, 0)), row_spec),
        ),
        compiler_params=pltpu.CompilerParams(vmem_limit_bytes=48 << 20),
        cost_estimate=pl.CostEstimate(
            flops=2 * rows * d * experts * f,
            bytes_accessed=2 * (rows * d + experts * f * d + experts * n * CAP * f * 2),
            transcendentals=0,
        ),
    )(scalars, tok0, tok1, w, hid, wt, rank)


def part_kernel(bands, sc_ref, own_ref, nb_ref, tok_own_ref, tok_nb_ref, send_ref, keep_ref):
    total = jnp.dot(own_ref[...], tok_own_ref[...], preferred_element_type=F32)
    total = total + jnp.dot(nb_ref[...], tok_nb_ref[...], preferred_element_type=F32)
    _, experts, band, cols = send_ref.shape
    total = total.reshape(experts, bands, band, cols).astype(BF)
    for a in range(bands):
        rel = sc_ref[0] ^ a
        for ref, bit in ((send_ref, 1), (keep_ref, 0)):

            @pl.when(rel % 2 == bit)
            def _():
                ref[rel // 2] = total[:, a]


def partial_grad(bands, band, scalars, own, nb, tok_own, tok_nb):
    rows, k = own.shape
    cols = tok_own.shape[1]
    block = min(256, cols)
    experts = rows // (bands * band)
    out = jax.ShapeDtypeStruct((bands // 2, experts, band, cols), BF)
    out_spec = pl.BlockSpec((bands // 2, experts, band, block), lambda c, sc: (0, 0, 0, c))
    hs_spec = pl.BlockSpec((rows, k), lambda c, sc: (0, 0))
    tok_spec = pl.BlockSpec((k, block), lambda c, sc: (0, c))
    return pl.pallas_call(
        functools.partial(part_kernel, bands),
        out_shape=(out, out),
        grid_spec=pltpu.PrefetchScalarGridSpec(
            num_scalar_prefetch=1,
            grid=(cols // block,),
            in_specs=[hs_spec, hs_spec, tok_spec, tok_spec],
            out_specs=(out_spec, out_spec),
        ),
        compiler_params=pltpu.CompilerParams(vmem_limit_bytes=48 << 20),
        cost_estimate=pl.CostEstimate(
            flops=4 * rows * k * cols, bytes_accessed=2 * (rows * cols + 2 * k * cols + 2 * rows * k), transcendentals=0
        ),
    )(scalars, own, nb, tok_own, tok_nb)


def per_device(n_dp, n, grad_out, expert_ids, route_weights, hidden_cache, w_down):
    dp, z = lax.axis_index("dp"), lax.axis_index("expert")
    bands = n_dp // 2
    upper, j = dp // bands, dp % bands
    experts, band, d = w_down.shape
    toks = grad_out.shape[0]
    f = bands * band

    def swap(x, bit):
        return lax.ppermute(x, "dp", [(i, i ^ bit) for i in range(n_dp)])

    ids = expert_ids[None] == jnp.arange(EXPERTS, dtype=jnp.int32)[:, None, None]
    table = jnp.sum(jnp.where(ids, route_weights.astype(F32)[None], 0.0), axis=2).astype(BF)
    tables = lax.all_gather(table, ("dp", "expert"), axis=0, tiled=False)
    tables = tables.reshape(n_dp * n, n, experts, toks)

    half = d // 2
    tok_own, tok_nb = [], []
    for h in range(2):
        mine = grad_out[:, h * half : (h + 1) * half]
        blocks = [mine] + [
            lax.ppermute(mine, "expert", [(i, (i + k) % n) for i in range(n)]) for k in range(1, n)
        ]
        tok_own.append(jnp.concatenate(blocks, axis=0))
        tok_nb.append(swap(tok_own[h], bands))

    outgoing = lax.dynamic_slice_in_dim(hidden_cache, (1 - upper) * f, f, axis=4)
    hid_nb = swap(outgoing, bands)

    pieces = {0: w_down}
    bit = bands // 2
    while bit:
        for r in list(pieces):
            pieces[r ^ bit] = swap(pieces[r], bit)
        bit //= 2
    w = jnp.zeros((experts, f, d), BF)
    for r, piece in pieces.items():
        w = lax.dynamic_update_slice(w, piece, (0, (j ^ r) * band, 0))

    sc_own = jnp.stack([z, upper, dp]).astype(jnp.int32)
    sc_nb = jnp.stack([z, 0 * z, dp ^ bands]).astype(jnp.int32)
    hs_own, wt_own, rank_own = hidden_to_tokens(n, sc_own, tables, hidden_cache, f)
    hs_nb, wt_nb, rank_nb = hidden_to_tokens(n, sc_nb, tables, hid_nb, f)
    hs_own, hs_nb = hs_own.reshape(experts * f, -1), hs_nb.reshape(experts * f, -1)

    sc_j = jnp.stack([j]).astype(jnp.int32)
    halves = []
    for h in range(2):
        send, keep = partial_grad(bands, band, sc_j, hs_own, hs_nb, tok_own[h], tok_nb[h])
        terms = [keep, swap(send, 1)]
        bit = bands // 2
        while bit > 1:
            mid = bit // 2
            going = sum(t[mid:].astype(F32) for t in terms).astype(BF)
            terms = [t[:mid] for t in terms] + [swap(going, bit)]
            bit //= 2
        halves.append(sum(t[0].astype(F32) for t in terms).astype(BF))
    grad_down = jnp.concatenate(halves, axis=2)

    gh_own, sg_own = backward(n, sc_own, tok_own[0], tok_own[1], w, hidden_cache, wt_own, rank_own)
    gh_nb, sg_nb = backward(n, sc_nb, tok_nb[0], tok_nb[1], w, hid_nb, wt_nb, rank_nb)
    gh_in = swap(gh_nb, bands)
    grad_hidden = jnp.where(
        upper == 0,
        jnp.concatenate([gh_own, gh_in], axis=3),
        jnp.concatenate([gh_in, gh_own], axis=3),
    )
    sg = sg_own.reshape(n, experts, toks) + swap(sg_nb.reshape(n, experts, toks), bands)
    by_expert = lax.all_to_all(sg, "expert", split_axis=0, concat_axis=0, tiled=True)
    by_expert = by_expert.reshape(EXPERTS, 1, toks)
    chosen = expert_ids.T[None] == jnp.arange(EXPERTS, dtype=jnp.int32)[:, None, None]
    grad_probs = jnp.sum(jnp.where(chosen, by_expert, 0.0), axis=0).T
    return grad_hidden[None], grad_down, grad_probs


def solution(mesh):
    tokens = P(("dp", "expert"), None)
    cache = P("dp", "expert", None, None, None)
    weights = P("expert", "dp", None)
    return jax.shard_map(
        functools.partial(per_device, mesh.shape["dp"], mesh.shape["expert"]),
        mesh=mesh,
        in_specs=(tokens, tokens, tokens, cache, weights),
        out_specs=(cache, weights, tokens),
        check_vma=False,
    )
```

```python
import functools

import jax
import jax.numpy as jnp
from jax import lax
from jax.experimental import pallas as pl
from jax.experimental.pallas import tpu as pltpu
from jax.sharding import PartitionSpec as P

EXPERTS = 16
CAP = 72
BF = jnp.bfloat16
F32 = jnp.float32


def iota(shape, dim):
    return lax.broadcasted_iota(jnp.int32, shape, dim)


def hidden_kernel(n, sc_ref, tab_ref, hid_ref, hst_ref, wt_ref, rank_ref):
    experts, toks = tab_ref.shape[1], tab_ref.shape[2]
    wt = tab_ref[0]
    named = wt > 0
    earlier = (iota((toks, toks), 0) < iota((toks, toks), 1)).astype(BF)
    rank = jnp.dot(named.astype(F32).astype(BF), earlier, preferred_element_type=F32)
    slots = iota((CAP, toks), 0).astype(F32)
    for e in range(experts):
        w_row, r_row = wt[e : e + 1], rank[e : e + 1]
        place = jnp.where(slots == r_row, w_row, 0.0).astype(BF)
        moved = lax.dot_general(
            hid_ref[0, e, 0], place, (((0,), (0,)), ((), ())), preferred_element_type=F32
        )
        hst_ref[e] = moved.astype(BF)
        wt_ref[0, e] = w_row
        rank_ref[0, e] = r_row


def hidden_to_tokens(n, scalars, table, hid, f):
    experts, toks = table.shape[1], table.shape[2]
    src = lambda k, sc: lax.rem(sc[0] + n - k, n)
    row = jax.ShapeDtypeStruct((n, experts, 1, toks), F32)
    row_spec = pl.BlockSpec((1, experts, 1, toks), lambda k, sc: (k, 0, 0, 0))
    return pl.pallas_call(
        functools.partial(hidden_kernel, n),
        out_shape=(jax.ShapeDtypeStruct((experts, f, n * toks), BF), row, row),
        grid_spec=pltpu.PrefetchScalarGridSpec(
            num_scalar_prefetch=1,
            grid=(n,),
            in_specs=[
                pl.BlockSpec((1, experts, toks), lambda k, sc: (src(k, sc), 0, 0)),
                pl.BlockSpec((1, experts, 1, CAP, f), lambda k, sc: (0, 0, src(k, sc), 0, sc[1])),
            ],
            out_specs=(
                pl.BlockSpec((experts, f, toks), lambda k, sc: (0, 0, k)),
                row_spec,
                row_spec,
            ),
        ),
        cost_estimate=pl.CostEstimate(
            flops=2 * n * experts * CAP * f * toks, bytes_accessed=4 * n * experts * f * toks, transcendentals=0
        ),
    )(scalars, table, hid)


def back_kernel(n, sc_ref, tok0_ref, tok1_ref, w_ref, hid_ref, wt_ref, rank_ref, gh_ref, sg_ref):
    toks = wt_ref.shape[3]
    half = tok0_ref.shape[1]
    over_d = (((1,), (1,)), ((), ()))
    z = lax.dot_general(tok0_ref[...], w_ref[0, :, :half], over_d, preferred_element_type=F32)
    z = z + lax.dot_general(tok1_ref[...], w_ref[0, :, half:], over_d, preferred_element_type=F32)
    eye = iota((toks, toks), 0) == iota((toks, toks), 1)
    slots = iota((CAP, toks), 0).astype(F32)
    for k in range(n):
        s = lax.rem(sc_ref[0] + n - k, n)
        w_row, r_row = wt_ref[k, 0], rank_ref[k, 0]
        pick = jnp.where((slots == r_row) & (w_row > 0), 1.0, 0.0).astype(BF)
        w_col = jnp.sum(jnp.where(eye, w_row, 0.0), axis=1, keepdims=True)
        zk = z[k * toks : (k + 1) * toks]
        weighted = (zk * w_col).astype(BF)
        gh_ref[0, s] = jnp.dot(pick, weighted, preferred_element_type=F32).astype(BF)
        hid = lax.dot_general(
            pick, hid_ref[0, 0, s], (((0,), (0,)), ((), ())), preferred_element_type=F32
        )
        sg_col = jnp.sum(zk * hid, axis=1, keepdims=True)
        sg_ref[s, 0] = jnp.sum(jnp.where(eye, sg_col, 0.0), axis=0, keepdims=True)


def backward(n, scalars, tok0, tok1, w, hid, wt, rank):
    experts, f, d = w.shape
    rows, half = tok0.shape
    toks = wt.shape[3]
    row_spec = pl.BlockSpec((n, 1, 1, toks), lambda e, sc: (0, e, 0, 0))
    whole = pl.BlockSpec((rows, half), lambda e, sc: (0, 0))
    return pl.pallas_call(
        functools.partial(back_kernel, n),
        out_shape=(
            jax.ShapeDtypeStruct((experts, n, CAP, f), BF),
            jax.ShapeDtypeStruct((n, experts, 1, toks), F32),
        ),
        grid_spec=pltpu.PrefetchScalarGridSpec(
            num_scalar_prefetch=1,
            grid=(experts,),
            in_specs=[
                whole,
                whole,
                pl.BlockSpec((1, f, d), lambda e, sc: (e, 0, 0)),
                pl.BlockSpec((1, 1, n, CAP, f), lambda e, sc: (0, e, 0, 0, sc[1])),
                row_spec,
                row_spec,
            ],
            out_specs=(pl.BlockSpec((1, n, CAP, f), lambda e, sc: (e, 0, 0, 0)), row_spec),
        ),
        compiler_params=pltpu.CompilerParams(vmem_limit_bytes=48 << 20),
        cost_estimate=pl.CostEstimate(
            flops=2 * rows * d * experts * f,
            bytes_accessed=2 * (rows * d + experts * f * d + experts * n * CAP * f * 2),
            transcendentals=0,
        ),
    )(scalars, tok0, tok1, w, hid, wt, rank)


def part_kernel(bands, sc_ref, own_ref, nb_ref, tok_own_ref, tok_nb_ref, send_ref, keep_ref):
    hidden = jnp.concatenate([own_ref[...], nb_ref[...]], axis=1)
    toks = jnp.concatenate([tok_own_ref[...], tok_nb_ref[...]], axis=0)
    total = jnp.dot(hidden, toks, preferred_element_type=F32)
    _, experts, band, cols = send_ref.shape
    total = total.reshape(experts, bands, band, cols).astype(BF)
    for a in range(bands):
        rel = sc_ref[0] ^ a
        for ref, bit in ((send_ref, 1), (keep_ref, 0)):

            @pl.when(rel % 2 == bit)
            def _():
                ref[rel // 2] = total[:, a]


def partial_grad(bands, band, scalars, own, nb, tok_own, tok_nb):
    rows, k = own.shape
    cols = tok_own.shape[1]
    block = min(256, cols)
    experts = rows // (bands * band)
    out = jax.ShapeDtypeStruct((bands // 2, experts, band, cols), BF)
    out_spec = pl.BlockSpec((bands // 2, experts, band, block), lambda c, sc: (0, 0, 0, c))
    hs_spec = pl.BlockSpec((rows, k), lambda c, sc: (0, 0))
    tok_spec = pl.BlockSpec((k, block), lambda c, sc: (0, c))
    return pl.pallas_call(
        functools.partial(part_kernel, bands),
        out_shape=(out, out),
        grid_spec=pltpu.PrefetchScalarGridSpec(
            num_scalar_prefetch=1,
            grid=(cols // block,),
            in_specs=[hs_spec, hs_spec, tok_spec, tok_spec],
            out_specs=(out_spec, out_spec),
        ),
        compiler_params=pltpu.CompilerParams(vmem_limit_bytes=48 << 20),
        cost_estimate=pl.CostEstimate(
            flops=4 * rows * k * cols, bytes_accessed=2 * (rows * cols + 2 * k * cols + 2 * rows * k), transcendentals=0
        ),
    )(scalars, own, nb, tok_own, tok_nb)


def per_device(n_dp, n, grad_out, expert_ids, route_weights, hidden_cache, w_down):
    dp, z = lax.axis_index("dp"), lax.axis_index("expert")
    bands = n_dp // 2
    upper, j = dp // bands, dp % bands
    experts, band, d = w_down.shape
    toks = grad_out.shape[0]
    f = bands * band

    def swap(x, bit):
        return lax.ppermute(x, "dp", [(i, i ^ bit) for i in range(n_dp)])

    ids = expert_ids[None] == jnp.arange(EXPERTS, dtype=jnp.int32)[:, None, None]
    table = jnp.sum(jnp.where(ids, route_weights.astype(F32)[None], 0.0), axis=2)
    tab_own = lax.all_to_all(table.reshape(n, experts, toks), "expert", 0, 0, tiled=True)
    tab_nb = swap(tab_own, bands)

    half = d // 2
    tok_own, tok_nb = [], []
    for h in range(2):
        mine = grad_out[:, h * half : (h + 1) * half]
        blocks = [mine] + [
            lax.ppermute(mine, "expert", [(i, (i + k) % n) for i in range(n)]) for k in range(1, n)
        ]
        tok_own.append(jnp.concatenate(blocks, axis=0))
        tok_nb.append(swap(tok_own[h], bands))

    outgoing = lax.dynamic_slice_in_dim(hidden_cache, (1 - upper) * f, f, axis=4)
    hid_nb = swap(outgoing, bands)

    pieces = {0: w_down}
    bit = bands // 2
    while bit:
        for r in list(pieces):
            pieces[r ^ bit] = swap(pieces[r], bit)
        bit //= 2
    w = jnp.zeros((experts, f, d), BF)
    for r, piece in pieces.items():
        w = lax.dynamic_update_slice(w, piece, (0, (j ^ r) * band, 0))

    sc_own = jnp.stack([z, upper]).astype(jnp.int32)
    sc_nb = jnp.stack([z, 0 * z]).astype(jnp.int32)
    hs_own, wt_own, rank_own = hidden_to_tokens(n, sc_own, tab_own, hidden_cache, f)
    hs_nb, wt_nb, rank_nb = hidden_to_tokens(n, sc_nb, tab_nb, hid_nb, f)
    hs_own, hs_nb = hs_own.reshape(experts * f, -1), hs_nb.reshape(experts * f, -1)

    sc_j = jnp.stack([j]).astype(jnp.int32)
    halves = []
    for h in range(2):
        send, keep = partial_grad(bands, band, sc_j, hs_own, hs_nb, tok_own[h], tok_nb[h])
        terms = [keep, swap(send, 1)]
        bit = bands // 2
        while bit > 1:
            mid = bit // 2
            going = sum(t[mid:].astype(F32) for t in terms).astype(BF)
            terms = [t[:mid] for t in terms] + [swap(going, bit)]
            bit //= 2
        halves.append(sum(t[0].astype(F32) for t in terms).astype(BF))
    grad_down = jnp.concatenate(halves, axis=2)

    gh_own, sg_own = backward(n, sc_own, tok_own[0], tok_own[1], w, hidden_cache, wt_own, rank_own)
    gh_nb, sg_nb = backward(n, sc_nb, tok_nb[0], tok_nb[1], w, hid_nb, wt_nb, rank_nb)
    gh_in = swap(gh_nb, bands)
    grad_hidden = jnp.where(
        upper == 0,
        jnp.concatenate([gh_own, gh_in], axis=3),
        jnp.concatenate([gh_in, gh_own], axis=3),
    )
    sg = sg_own.reshape(n, experts, toks) + swap(sg_nb.reshape(n, experts, toks), bands)
    by_expert = lax.all_to_all(sg, "expert", split_axis=0, concat_axis=0, tiled=True)
    by_expert = by_expert.reshape(EXPERTS, 1, toks)
    chosen = expert_ids.T[None] == jnp.arange(EXPERTS, dtype=jnp.int32)[:, None, None]
    grad_probs = jnp.sum(jnp.where(chosen, by_expert, 0.0), axis=0).T
    return grad_hidden[None], grad_down, grad_probs


def solution(mesh):
    tokens = P(("dp", "expert"), None)
    cache = P("dp", "expert", None, None, None)
    weights = P("expert", "dp", None)
    return jax.shard_map(
        functools.partial(per_device, mesh.shape["dp"], mesh.shape["expert"]),
        mesh=mesh,
        in_specs=(tokens, tokens, tokens, cache, weights),
        out_specs=(cache, weights, tokens),
        check_vma=False,
    )
```

```python
import functools

import jax
import jax.numpy as jnp
from jax import lax
from jax.experimental import pallas as pl
from jax.experimental.pallas import tpu as pltpu
from jax.sharding import PartitionSpec as P

EXPERTS = 16
CAP = 72
BF = jnp.bfloat16
F32 = jnp.float32
CHUNKS = ((0, 8, False), (8, 12, False), (12, 16, True))
REDUCTIONS = ((0,), (1, 2))


SHORT = pl.CostEstimate(flops=1, bytes_accessed=1, transcendentals=0)


def iota(shape, dim):
    return lax.broadcasted_iota(jnp.int32, shape, dim)


def after(x, *others):
    return lax.optimization_barrier((x, *others))[0]


def hidden_kernel(n, sc_ref, tab_ref, hid_ref, hst_ref, wt_ref, rank_ref):
    experts, toks = tab_ref.shape[1], tab_ref.shape[2]
    earlier = (iota((toks, toks), 0) < iota((toks, toks), 1)).astype(BF)
    slots = iota((CAP, toks), 0).astype(F32)
    for k in range(n):
        s = lax.rem(sc_ref[0] + n - k, n)
        wt = tab_ref[k]
        named = (wt > 0).astype(F32).astype(BF)
        rank = jnp.dot(named, earlier, preferred_element_type=F32)
        for e in range(experts):
            w_row, r_row = wt[e : e + 1], rank[e : e + 1]
            place = jnp.where(slots == r_row, w_row, 0.0).astype(BF)
            moved = lax.dot_general(
                hid_ref[0, e, s], place, (((0,), (0,)), ((), ())), preferred_element_type=F32
            )
            hst_ref[e, :, k * toks : (k + 1) * toks] = moved.astype(BF)
            wt_ref[k, e] = w_row
            rank_ref[k, e] = r_row


def hidden_to_tokens(n, scalars, table, hid, f):
    experts, toks = table.shape[1], table.shape[2]
    row = jax.ShapeDtypeStruct((n, experts, 1, toks), F32)
    row_spec = pl.BlockSpec((n, experts, 1, toks), lambda i, sc: (0, 0, 0, 0))
    return pl.pallas_call(
        functools.partial(hidden_kernel, n),
        out_shape=(jax.ShapeDtypeStruct((experts, f, n * toks), BF), row, row),
        grid_spec=pltpu.PrefetchScalarGridSpec(
            num_scalar_prefetch=1,
            grid=(1,),
            in_specs=[
                pl.BlockSpec((n, experts, toks), lambda i, sc: (0, 0, 0)),
                pl.BlockSpec((1, experts, n, CAP, f), lambda i, sc: (0, 0, 0, 0, sc[1])),
            ],
            out_specs=(
                pl.BlockSpec((experts, f, n * toks), lambda i, sc: (0, 0, 0)),
                row_spec,
                row_spec,
            ),
        ),
        compiler_params=pltpu.CompilerParams(vmem_limit_bytes=16 << 20),
        cost_estimate=SHORT,
    )(scalars, table, hid)


def flat(pieces):
    arrays = [a for chunk in pieces for a, _, _ in chunk]
    specs = [
        pl.BlockSpec((rows, a.shape[1]), functools.partial(lambda g, i, sc: (g, 0), g))
        for chunk in pieces
        for a, rows, g in chunk
    ]
    return arrays, specs, [len(chunk) for chunk in pieces]


def gathered(refs, counts):
    chunks, at = [], 0
    for count in counts:
        refs_here = [refs[at + i][...] for i in range(count)]
        chunks.append(refs_here[0] if count == 1 else jnp.concatenate(refs_here, axis=0))
        at += count
    return chunks, at


def back_kernel(n, counts, group, rels, sc_ref, *refs):
    chunks, at = gathered(refs, counts)
    w_refs, refs = refs[at : at + len(rels)], refs[at + len(rels) :]
    hid_ref, wt_ref, rank_ref, gh_ref, sg_ref, w_all = refs
    toks, (f, d) = wt_ref.shape[3], w_all.shape[1:]
    for rel, ref in zip(rels, w_refs):
        rows = ref.shape[1]
        start = 0 if rel is None else pl.multiple_of((sc_ref[2] ^ rel) * rows, rows)
        for e in range(group):
            w_all[e, pl.ds(start, rows), :] = ref[e]
    tokens = chunks[0] if len(chunks) == 1 else jnp.concatenate(chunks, axis=1)
    z = lax.dot_general(
        tokens, w_all[...].reshape(group * f, d), (((1,), (1,)), ((), ())), preferred_element_type=F32
    )
    eye = iota((toks, toks), 0) == iota((toks, toks), 1)
    slots = iota((CAP, toks), 0).astype(F32)
    for e in range(group):
        for k in range(n):
            s = lax.rem(sc_ref[0] + n - k, n)
            w_row, r_row = wt_ref[k, e], rank_ref[k, e]
            here = (slots == r_row) & (w_row > 0)
            pick = jnp.where(here, 1.0, 0.0).astype(BF)
            weigh = jnp.where(here, w_row, 0.0).astype(BF)
            zk = z[k * toks : (k + 1) * toks, e * f : (e + 1) * f]
            gh_ref[e, s] = jnp.dot(weigh, zk.astype(BF), preferred_element_type=F32).astype(BF)
            hid = lax.dot_general(
                pick, hid_ref[0, e, s], (((0,), (0,)), ((), ())), preferred_element_type=F32
            )
            sg_col = jnp.sum(zk * hid, axis=1, keepdims=True)
            sg_ref[s, e] = jnp.sum(jnp.where(eye, sg_col, 0.0), axis=0, keepdims=True)


def backward(n, scalars, pieces, w_pieces, f, hid, wt, rank, width):
    experts, band, d = w_pieces[0][1].shape
    toks = wt.shape[3]
    rels = [rel for rel, _ in w_pieces]
    group = 2 if experts % 2 == 0 else 1
    arrays, specs, counts = flat(pieces)
    row_spec = pl.BlockSpec((n, group, 1, toks), lambda e, sc: (0, e, 0, 0))
    return pl.pallas_call(
        functools.partial(back_kernel, n, counts, group, rels),
        out_shape=(
            jax.ShapeDtypeStruct((experts, n, CAP, width), BF),
            jax.ShapeDtypeStruct((n, experts, 1, toks), F32),
        ),
        grid_spec=pltpu.PrefetchScalarGridSpec(
            num_scalar_prefetch=1,
            grid=(experts // group,),
            in_specs=specs
            + [pl.BlockSpec((group, band, d), lambda e, sc: (e, 0, 0))] * len(rels)
            + [
                pl.BlockSpec((1, group, n, CAP, f), lambda e, sc: (0, e, 0, 0, sc[1])),
                row_spec,
                row_spec,
            ],
            out_specs=(pl.BlockSpec((group, n, CAP, f), lambda e, sc: (e, 0, 0, sc[1])), row_spec),
            scratch_shapes=[pltpu.VMEM((group, f, d), BF)],
        ),
        compiler_params=pltpu.CompilerParams(vmem_limit_bytes=32 << 20),
        cost_estimate=SHORT,
    )(scalars, *arrays, *[w for _, w in w_pieces], hid, wt, rank)


def insert_kernel(sc_ref, new_ref, old_ref, out_ref):
    out_ref[...] = new_ref[...]


def insert(scalars, new, whole):
    experts, n, cap, f = new.shape
    return pl.pallas_call(
        insert_kernel,
        out_shape=jax.ShapeDtypeStruct(whole.shape, BF),
        grid_spec=pltpu.PrefetchScalarGridSpec(
            num_scalar_prefetch=1,
            grid=(1,),
            in_specs=[
                pl.BlockSpec((experts, n, cap, f), lambda i, sc: (0, 0, 0, 0)),
                pl.BlockSpec(memory_space=pl.ANY),
            ],
            out_specs=pl.BlockSpec((experts, n, cap, f), lambda i, sc: (0, 0, 0, 1 - sc[1])),
        ),
        input_output_aliases={2: 0},
        cost_estimate=SHORT,
    )(scalars, new, whole)


def part_kernel(bands, counts, sc_ref, *refs):
    own, at_own = gathered(refs, counts[0])
    nb, at_nb = gathered(refs[at_own:], counts[1])
    own_ref, nb_ref, send_ref, keep_ref = refs[at_own + at_nb :]
    tokens = jnp.concatenate(
        [jnp.concatenate(c, axis=1) if len(c) > 1 else c[0] for c in (own, nb)], axis=0
    )
    hidden = jnp.concatenate([own_ref[0], nb_ref[0]], axis=1)
    total = jnp.dot(hidden, tokens, preferred_element_type=F32)
    band, cols = send_ref.shape[2:]
    total = total.reshape(bands, band, cols).astype(BF)
    for a in range(bands):
        rel = sc_ref[0] ^ a
        for ref, bit in ((send_ref, 1), (keep_ref, 0)):

            @pl.when(rel % 2 == bit)
            def _():
                ref[rel // 2, 0] = total[a]


def partial_grad(bands, band, scalars, own, nb, pieces_own, pieces_nb):
    experts, f, k = own.shape
    arrays, specs, counts = flat(pieces_own)
    arrays_nb, specs_nb, counts_nb = flat(pieces_nb)
    cols = sum(chunk[0][0].shape[1] for chunk in pieces_own)
    out = jax.ShapeDtypeStruct((bands // 2, experts, band, cols), BF)
    out_spec = pl.BlockSpec((bands // 2, 1, band, cols), lambda e, sc: (0, e, 0, 0))
    hs_spec = pl.BlockSpec((1, f, k), lambda e, sc: (e, 0, 0))
    return pl.pallas_call(
        functools.partial(part_kernel, bands, (counts, counts_nb)),
        out_shape=(out, out),
        grid_spec=pltpu.PrefetchScalarGridSpec(
            num_scalar_prefetch=1,
            grid=(experts,),
            in_specs=specs + specs_nb + [hs_spec, hs_spec],
            out_specs=(out_spec, out_spec),
        ),
        compiler_params=pltpu.CompilerParams(vmem_limit_bytes=32 << 20),
        cost_estimate=SHORT,
    )(scalars, *arrays, *arrays_nb, own, nb)


def per_device(n_dp, n, grad_out, expert_ids, route_weights, hidden_cache, w_down):
    dp, z = lax.axis_index("dp"), lax.axis_index("expert")
    bands = n_dp // 2
    upper, j = dp // bands, dp % bands
    experts, band, d = w_down.shape
    toks = grad_out.shape[0]
    f = bands * band

    def swap(x, bit):
        return lax.ppermute(x, "dp", [(i, i ^ bit) for i in range(n_dp)])

    def spread(x):
        return [x] + [
            lax.ppermute(x, "expert", [(i, (i + k) % n) for i in range(n)]) for k in range(1, n)
        ]

    ids = expert_ids[None] == jnp.arange(EXPERTS, dtype=jnp.int32)[:, None, None]
    table = jnp.sum(jnp.where(ids, route_weights.astype(F32)[None], 0.0), axis=2).astype(BF)

    mine = [grad_out[:, a * d // 16 : b * d // 16] for a, b, _ in CHUNKS]

    def with_table(x, t):
        return jnp.concatenate([x, jnp.pad(t, ((0, 0), (0, x.shape[1] - toks)))], axis=0)

    def tables(blocks):
        rows = [lax.dynamic_slice(b, (toks + z * experts, 0), (experts, toks)) for b in blocks]
        return jnp.stack(rows).astype(F32)

    pieces = {0: w_down}
    bit = bands // 2
    while bit:
        for r in list(pieces):
            pieces[r ^ bit] = swap(pieces[r], bit)
        bit //= 2
    blocks0 = spread(with_table(mine[0], table))
    pair = swap(with_table(mine[2], table), bands)
    outgoing = lax.dynamic_slice_in_dim(hidden_cache, (1 - upper) * f, f, axis=4)
    hid_nb = swap(after(outgoing, pair), bands)
    sc_own = jnp.stack([z, upper, j]).astype(jnp.int32)
    sc_nb = jnp.stack([z, 0 * z, j]).astype(jnp.int32)
    sc_j = jnp.stack([j]).astype(jnp.int32)
    hs_own, wt_own, rank_own = hidden_to_tokens(n, sc_own, tables(blocks0), hidden_cache, f)

    nb0 = swap(jnp.concatenate([b[:toks] for b in blocks0], axis=0), bands)
    blocks1 = spread(after(with_table(mine[1], pair[toks:, :toks]), *blocks0))
    hs_nb, wt_nb, rank_nb = hidden_to_tokens(n, sc_nb, tables(blocks1), hid_nb, f)
    blocks2 = spread(after(jnp.concatenate([mine[2], pair[:toks]], axis=0), *blocks1))
    ready = jnp.concatenate([b[:toks] for b in blocks1], axis=0)
    nb1 = swap(after(ready, hs_own, hs_nb, pieces[bands // 2]), bands)

    own_pieces = [[(b, toks, 0) for b in blocks] for blocks in (blocks0, blocks1, blocks2)]
    nb_pieces = [[(nb0, n * toks, 0)], [(nb1, n * toks, 0)], [(b, toks, 1) for b in blocks2]]

    w_pieces = list(pieces.items())
    if band % 16:
        w = jnp.zeros((experts, f, d), BF)
        for r, piece in w_pieces:
            w = lax.dynamic_update_slice(w, piece, (0, (j ^ r) * band, 0))
        w_pieces = [(None, w)]

    grad_down, partials, at = jnp.zeros((experts, band, d), BF), [], 0
    for members in REDUCTIONS:
        send, keep = partial_grad(
            bands, band, after(sc_j, *partials), hs_own, hs_nb, [own_pieces[i] for i in members], [nb_pieces[i] for i in members]
        )
        if not partials:
            send = after(send, *blocks2[1 : (n + 2) // 2])
        terms = [keep, swap(send, 1)]
        bit = bands // 2
        while bit > 1:
            mid = bit // 2
            going = sum(t[mid:].astype(F32) for t in terms).astype(BF)
            partials.append(going)
            terms = [t[:mid] for t in terms] + [swap(going, bit)]
            bit //= 2
        total = sum(t[0].astype(F32) for t in terms).astype(BF)
        grad_down = lax.dynamic_update_slice(grad_down, total, (0, 0, at))
        at += total.shape[2]

    gh_nb, sg_nb = backward(
        n, after(sc_nb, send), nb_pieces, w_pieces, f, hid_nb, wt_nb, rank_nb, f
    )
    sg_in = swap(sg_nb.reshape(n, experts, toks), bands)
    gh_own, sg_own = backward(
        n, after(sc_own, sg_in), own_pieces, w_pieces, f, hidden_cache, wt_own, rank_own, 2 * f
    )
    grad_hidden = insert(sc_own, swap(after(gh_nb, sg_in), bands), gh_own)
    sg = sg_own.reshape(n, experts, toks) + sg_in
    by_expert = lax.all_to_all(sg, "expert", split_axis=0, concat_axis=0, tiled=True)
    by_expert = by_expert.reshape(EXPERTS, 1, toks)
    chosen = expert_ids.T[None] == jnp.arange(EXPERTS, dtype=jnp.int32)[:, None, None]
    grad_probs = jnp.sum(jnp.where(chosen, by_expert, 0.0), axis=0).T
    return grad_hidden[None], grad_down, grad_probs


def solution(mesh):
    tokens = P(("dp", "expert"), None)
    cache = P("dp", "expert", None, None, None)
    weights = P("expert", "dp", None)
    return jax.shard_map(
        functools.partial(per_device, mesh.shape["dp"], mesh.shape["expert"]),
        mesh=mesh,
        in_specs=(tokens, tokens, tokens, cache, weights),
        out_specs=(cache, weights, tokens),
        check_vma=False,
    )
```

```python
import functools

import jax
import jax.numpy as jnp
from jax import lax
from jax.experimental import pallas as pl
from jax.experimental.pallas import tpu as pltpu
from jax.sharding import PartitionSpec as P

EXPERTS = 16
CAP = 72
BF = jnp.bfloat16
F32 = jnp.float32
SHORT = pl.CostEstimate(flops=1, bytes_accessed=1, transcendentals=0)


def iota(shape, dim):
    return lax.broadcasted_iota(jnp.int32, shape, dim)


def after(x, *others):
    return lax.optimization_barrier((x, *others))[0]


def hidden_kernel(n, experts, sc_ref, tab_ref, hid_ref, hst_ref, wt_ref, rank_ref):
    toks = tab_ref.shape[1]
    earlier = (iota((toks, toks), 0) < iota((toks, toks), 1)).astype(BF)
    slots = iota((CAP, toks), 0).astype(F32)
    table = tab_ref[...].astype(F32)
    rank = jnp.dot((table > 0).astype(F32).astype(BF), earlier, preferred_element_type=F32)
    for k in range(n):
        s = lax.rem(sc_ref[0] + n - k, n)
        for e in range(experts):
            at = k * experts + e
            w_row, r_row = table[at : at + 1], rank[at : at + 1]
            place = jnp.where(slots == r_row, w_row, 0.0).astype(BF)
            moved = lax.dot_general(
                hid_ref[0, e, s], place, (((0,), (0,)), ((), ())), preferred_element_type=F32
            )
            hst_ref[e, :, k * toks : (k + 1) * toks] = moved.astype(BF)
            wt_ref[k, e] = w_row
            rank_ref[k, e] = r_row


def hidden_to_tokens(n, experts, toks, scalars, tokens, hid, f, whole):
    row = jax.ShapeDtypeStruct((n, experts, 1, toks), F32)
    row_spec = pl.BlockSpec((n, experts, 1, toks), lambda i, sc: (0, 0, 0, 0))
    lines = n * experts
    return pl.pallas_call(
        functools.partial(hidden_kernel, n, experts),
        out_shape=(jax.ShapeDtypeStruct((experts, f, n * toks), BF), row, row),
        grid_spec=pltpu.PrefetchScalarGridSpec(
            num_scalar_prefetch=1,
            grid=(1,),
            in_specs=[
                pl.BlockSpec((lines, toks), lambda i, sc: (n * toks // lines, 0)),
                pl.BlockSpec((1, experts, n, CAP, f), lambda i, sc: (0, 0, 0, 0, sc[1] if whole else 0)),
            ],
            out_specs=(
                pl.BlockSpec((experts, f, n * toks), lambda i, sc: (0, 0, 0)),
                row_spec,
                row_spec,
            ),
        ),
        compiler_params=pltpu.CompilerParams(vmem_limit_bytes=16 << 20),
        cost_estimate=SHORT,
    )(scalars, tokens, hid)


def below_kernel(n, experts, sc_ref, *refs):
    *blocks, out_ref = refs
    z = sc_ref[0]
    toks = blocks[0].shape[0] - EXPERTS
    line = iota((EXPERTS, toks), 0)

    def put(k, ref):
        out_ref[k * toks : (k + 1) * toks] = ref[:toks]
        table = ref[toks:, :toks].astype(F32)
        rows = [
            jnp.sum(jnp.where(line == z * experts + e, table, 0.0), axis=0, keepdims=True)
            for e in range(experts)
        ]
        return rows

    tables = [put(k, blocks[k]) for k in range(n)]
    if len(blocks) > n:
        passed = blocks[n]
        rows = [
            jnp.sum(jnp.where(line == z * experts + e, passed[toks:, :toks].astype(F32), 0.0), axis=0, keepdims=True)
            for e in range(experts)
        ]
        for k, place in ((1, 0), (n - 1, n - 1)):
            tables[k] = [jnp.where(z == place, new, old) for new, old in zip(rows, tables[k])]

            @pl.when(z == place)
            def _():
                out_ref[k * toks : (k + 1) * toks] = passed[:toks]

    rows = [row for table in tables for row in table]
    out_ref[n * toks :, :toks] = jnp.concatenate(rows, axis=0).astype(BF)


def below(n, experts, scalars, blocks):
    rows, cols = blocks[0].shape
    toks = rows - EXPERTS
    return pl.pallas_call(
        functools.partial(below_kernel, n, experts),
        out_shape=jax.ShapeDtypeStruct((n * (toks + experts), cols), BF),
        grid_spec=pltpu.PrefetchScalarGridSpec(
            num_scalar_prefetch=1,
            grid=(1,),
            in_specs=[pl.BlockSpec((rows, cols), lambda i, sc: (0, 0))] * len(blocks),
            out_specs=pl.BlockSpec((n * (toks + experts), cols), lambda i, sc: (0, 0)),
        ),
        compiler_params=pltpu.CompilerParams(vmem_limit_bytes=24 << 20),
        cost_estimate=SHORT,
    )(scalars, *blocks)


def flat(pieces):
    arrays = [a for chunk in pieces for a, _, _ in chunk]
    specs = [
        pl.BlockSpec(shape, functools.partial(lambda at, i, sc: at, at))
        for chunk in pieces
        for _, shape, at in chunk
    ]
    return arrays, specs, [len(chunk) for chunk in pieces]


def gathered(refs, counts, n, z, spans=None):
    chunks, at = [], 0
    for i, count in enumerate(counts):
        cols = slice(*spans[i]) if spans else slice(None)
        pieces = [refs[at + k][:, cols] for k in range(count)]
        if count > n:
            passed = pieces.pop()
            for k, place in ((1, 0), (n - 1, n - 1)):
                pieces[k] = jnp.where(z == place, passed, pieces[k])
        chunks.append(pieces[0] if len(pieces) == 1 else jnp.concatenate(pieces, axis=0))
        at += count
    return chunks, at


def back_kernel(n, counts, group, rels, sc_ref, *refs):
    chunks, at = gathered(refs, counts, n, sc_ref[0])
    w_refs, refs = refs[at : at + len(rels)], refs[at + len(rels) :]
    hid_ref, wt_ref, rank_ref, gh_ref, sg_ref, w_all = refs
    toks, (f, d) = wt_ref.shape[3], w_all.shape[1:]
    for rel, ref in zip(rels, w_refs):
        rows = ref.shape[2]
        start = 0 if rel is None else pl.multiple_of((sc_ref[2] ^ rel) * rows, rows)
        for e in range(group):
            w_all[e, pl.ds(start, rows), :] = ref[0, e]
    tokens = chunks[0] if len(chunks) == 1 else jnp.concatenate(chunks, axis=1)
    z = lax.dot_general(
        tokens, w_all[...].reshape(group * f, d), (((1,), (1,)), ((), ())), preferred_element_type=F32
    )
    eye = iota((toks, toks), 0) == iota((toks, toks), 1)
    slots = iota((CAP, toks), 0).astype(F32)
    for e in range(group):
        for k in range(n):
            s = lax.rem(sc_ref[0] + n - k, n)
            w_row, r_row = wt_ref[k, e], rank_ref[k, e]
            here = (slots == r_row) & (w_row > 0)
            pick = jnp.where(here, 1.0, 0.0).astype(BF)
            weigh = jnp.where(here, w_row, 0.0).astype(BF)
            zk = z[k * toks : (k + 1) * toks, e * f : (e + 1) * f]
            gh_ref[e, s] = jnp.dot(weigh, zk.astype(BF), preferred_element_type=F32).astype(BF)
            hid = lax.dot_general(
                pick, hid_ref[0, e, s], (((0,), (0,)), ((), ())), preferred_element_type=F32
            )
            sg_col = jnp.sum(zk * hid, axis=1, keepdims=True)
            sg_ref[s, e] = jnp.sum(jnp.where(eye, sg_col, 0.0), axis=0, keepdims=True)


def backward(n, scalars, pieces, w_pieces, f, hid, wt, rank, whole):
    _, experts, band, d = w_pieces[0][1].shape
    toks = wt.shape[3]
    rels = [rel for rel, _, _ in w_pieces]
    group = 2 if experts % 2 == 0 else 1
    arrays, specs, counts = flat(pieces)
    row_spec = pl.BlockSpec((n, group, 1, toks), lambda e, sc: (0, e, 0, 0))
    return pl.pallas_call(
        functools.partial(back_kernel, n, counts, group, rels),
        out_shape=(
            jax.ShapeDtypeStruct((experts, n, CAP, 2 * f if whole else f), BF),
            jax.ShapeDtypeStruct((n, experts, 1, toks), F32),
        ),
        grid_spec=pltpu.PrefetchScalarGridSpec(
            num_scalar_prefetch=1,
            grid=(experts // group,),
            in_specs=specs
            + [
                pl.BlockSpec((1, group, band, d), functools.partial(lambda i, e, sc: (i, e, 0, 0), i))
                for _, _, i in w_pieces
            ]
            + [
                pl.BlockSpec((1, group, n, CAP, f), lambda e, sc: (0, e, 0, 0, sc[1] if whole else 0)),
                row_spec,
                row_spec,
            ],
            out_specs=(pl.BlockSpec((group, n, CAP, f), lambda e, sc: (e, 0, 0, sc[1] if whole else 0)), row_spec),
            scratch_shapes=[pltpu.VMEM((group, f, d), BF)],
        ),
        compiler_params=pltpu.CompilerParams(vmem_limit_bytes=32 << 20),
        cost_estimate=SHORT,
    )(scalars, *arrays, *[w for _, w, _ in w_pieces], hid, wt, rank)


def insert_kernel(sc_ref, new_ref, old_ref, out_ref, sems):
    experts, n, _, f = new_ref.shape
    at = pl.multiple_of((1 - sc_ref[1]) * f, f)
    copies = [
        pltpu.make_async_copy(new_ref.at[e, s], out_ref.at[e, s, :, pl.ds(at, f)], sems.at[e, s])
        for e in range(experts)
        for s in range(n)
    ]
    for copy in copies:
        copy.start()
    for copy in copies:
        copy.wait()


def insert(scalars, new, whole):
    return pl.pallas_call(
        insert_kernel,
        out_shape=jax.ShapeDtypeStruct(whole.shape, BF),
        in_specs=[
            pl.BlockSpec(memory_space=pltpu.SMEM),
            pl.BlockSpec(memory_space=pltpu.VMEM),
            pl.BlockSpec(memory_space=pl.ANY),
        ],
        out_specs=pl.BlockSpec(memory_space=pl.ANY),
        scratch_shapes=[pltpu.SemaphoreType.DMA(new.shape[:2])],
        input_output_aliases={2: 0},
        cost_estimate=SHORT,
    )(scalars, new, whole)


def part_kernel(n, bands, counts, spans, sc_ref, *refs):
    own, at_own = gathered(refs, counts[0], n, sc_ref[0], spans)
    nb, at_nb = gathered(refs[at_own:], counts[1], n, sc_ref[0], spans)
    own_ref, nb_ref, *send_refs, keep_ref = refs[at_own + at_nb :]
    tokens = jnp.concatenate(
        [jnp.concatenate(c, axis=1) if len(c) > 1 else c[0] for c in (own, nb)], axis=0
    )
    hidden = jnp.concatenate([own_ref[0], nb_ref[0]], axis=1)
    total = jnp.dot(hidden, tokens, preferred_element_type=F32)
    quarter, _, band, cols = keep_ref.shape
    total = total.reshape(bands // 2, band, cols).astype(BF)
    for a in range(bands // 2):
        rel = (sc_ref[2] % (bands // 2)) ^ a
        at = rel // 2

        @pl.when(rel % 2 == 1)
        def _():
            done = 0
            for ref in send_refs:
                width = ref.shape[3]
                ref[at, 0] = total[a, :, done : done + width]
                done += width

        @pl.when(rel % 2 == 0)
        def _():
            keep_ref[at, 0] = total[a]


def partial_grad(n, bands, band, far, parts, scalars, own, nb, pieces_own, pieces_nb, spans):
    experts, f, k = own.shape
    arrays, specs, counts = flat(pieces_own)
    arrays_nb, specs_nb, counts_nb = flat(pieces_nb)
    cols = sum(stop - start for start, stop in spans)
    widths = (*parts, cols)
    half = bands // 2
    hs_spec = pl.BlockSpec((1, f // 2, k), lambda e, sc: (e, (sc[2] // half) ^ int(far), 0))
    return pl.pallas_call(
        functools.partial(part_kernel, n, bands, (counts, counts_nb), spans),
        out_shape=[jax.ShapeDtypeStruct((bands // 4, experts, band, width), BF) for width in widths],
        grid_spec=pltpu.PrefetchScalarGridSpec(
            num_scalar_prefetch=1,
            grid=(experts,),
            in_specs=specs + specs_nb + [hs_spec, hs_spec],
            out_specs=[pl.BlockSpec((bands // 4, 1, band, width), lambda e, sc: (0, e, 0, 0)) for width in widths],
        ),
        compiler_params=pltpu.CompilerParams(vmem_limit_bytes=32 << 20),
        cost_estimate=SHORT,
    )(scalars, *arrays, *arrays_nb, own, nb)


def joined_kernel(widths, *refs):
    out_ref, at = refs[-1], 0
    count = len(widths)
    for i, width in enumerate(widths):
        keep, parts = refs[i], refs[count + 2 * i : count + 2 * i + 2]
        there = jnp.concatenate([x[...] for x in parts], axis=3)
        out_ref[:, :, :, at : at + width] = (keep[...].astype(F32) + there.astype(F32)).astype(BF)
        at += width


def joined(keeps, parts):
    widths = [keep.shape[3] for keep in keeps]
    arrays = [*keeps, *[part for two in parts for part in two]]
    block = lambda x: pl.BlockSpec((x.shape[0], 1, *x.shape[2:]), lambda e: (0, e, 0, 0))
    out = jax.ShapeDtypeStruct((*keeps[0].shape[:3], sum(widths)), BF)
    return pl.pallas_call(
        functools.partial(joined_kernel, widths),
        out_shape=out,
        grid=(out.shape[1],),
        in_specs=[block(x) for x in arrays],
        out_specs=block(out),
        compiler_params=pltpu.CompilerParams(vmem_limit_bytes=16 << 20),
        cost_estimate=SHORT,
    )(*arrays)


def finish_kernel(keep_ref, left_ref, right_ref, there_ref, out_ref):
    near = jnp.concatenate([left_ref[0], right_ref[0]], axis=2).astype(F32)
    out_ref[...] = (keep_ref[0].astype(F32) + near + there_ref[0].astype(F32)).astype(BF)


def finish(keep, near, there):
    _, experts, band, d = keep.shape
    block = lambda x: pl.BlockSpec((1, 1, *x.shape[2:]), lambda e: (0, e, 0, 0))
    return pl.pallas_call(
        finish_kernel,
        out_shape=jax.ShapeDtypeStruct((experts, band, d), BF),
        grid=(experts,),
        in_specs=[block(x) for x in (keep, *near, there)],
        out_specs=pl.BlockSpec((1, band, d), lambda e: (e, 0, 0)),
        compiler_params=pltpu.CompilerParams(vmem_limit_bytes=16 << 20),
        cost_estimate=SHORT,
    )(keep, *near, there)


def per_device(n_dp, n, grad_out, expert_ids, route_weights, hidden_cache, w_down):
    dp, z = lax.axis_index("dp"), lax.axis_index("expert")
    bands = n_dp // 2
    upper, j = dp // bands, dp % bands
    experts, band, d = w_down.shape
    toks = grad_out.shape[0]
    f = bands * band

    def swap(x, bit):
        return lax.ppermute(x, "dp", [(i, i ^ bit) for i in range(n_dp)])

    def spread(x):
        if n != 4:
            return [x] + [
                lax.ppermute(x, "expert", [(i, (i + k) % n) for i in range(n)]) for k in range(1, n)
            ]
        two = lax.ppermute(x, "expert", [(i, (i + 2) % n) for i in range(n)])
        one = lax.ppermute(x, "expert", [(i, i + 1) for i in range(n - 1)])
        three = lax.ppermute(x, "expert", [(i + 1, i) for i in range(n - 1)])
        passed = lax.ppermute(two, "expert", [(2, 3), (1, 0)])
        return [x, one, two, three, passed]

    ids = expert_ids[None] == jnp.arange(EXPERTS, dtype=jnp.int32)[:, None, None]
    table = jnp.sum(jnp.where(ids, route_weights.astype(F32)[None], 0.0), axis=2).astype(BF)

    cut = 10 * d // 16
    table = jnp.pad(table, ((0, 0), (0, cut - toks)))
    blocks = spread(jnp.concatenate([grad_out[:, :cut], table], axis=0))
    w_core = swap(w_down[None], 1)
    outgoing = lax.dynamic_slice_in_dim(hidden_cache, (1 - upper) * f, f, axis=4).reshape(-1, f)
    lefts = [min(left, d - f) for left in range(cut, d, f)]
    outgoing = [outgoing] + [grad_out[:, left : left + f] for left in lefts]
    incoming = swap(after(jnp.concatenate(outgoing, axis=0), w_core), bands)
    count = hidden_cache.size // (2 * f)
    hid_nb = incoming[:count].reshape(1, experts, n, CAP, f)
    pair = [
        incoming[count + i * toks : count + (i + 1) * toks, cut + i * f - left :] for i, left in enumerate(lefts)
    ]
    w_pieces = [(0, w_down[None], 0), (1, w_core, 0)]
    bit = 2
    while bit < bands:
        far = swap(w_down[None] if bit == 2 else jnp.concatenate([a for _, a, _ in w_pieces[::2]]), bit)
        there = swap(far, 1)
        for i in range(far.shape[0]):
            w_pieces += [(w_pieces[2 * i][0] ^ bit, far, i), (w_pieces[2 * i][0] ^ bit ^ 1, there, i)]
        bit *= 2

    scalars = jnp.stack([z, upper, j]).astype(jnp.int32)
    mine = below(n, experts, scalars, blocks)
    hs_own, wt_own, rank_own = hidden_to_tokens(n, experts, toks, scalars, mine, hidden_cache, f, True)
    rest = jnp.concatenate([grad_out[:, cut:], jnp.concatenate(pair, axis=1)], axis=0)
    rests = spread(after(rest, *blocks))
    nb_a = swap(after(mine, incoming), bands)
    hs_nb, wt_nb, rank_nb = hidden_to_tokens(n, experts, toks, scalars, nb_a, hid_nb, f, False)

    own_pieces = [[(mine, (n * toks, cut), (0, 0))], [(b, (toks, d - cut), (0, 0)) for b in rests]]
    nb_pieces = [[(nb_a, (n * toks, cut), (0, 0))], [(b, (toks, d - cut), (1, 0)) for b in rests]]

    if band % 16:
        w = jnp.zeros((experts, f, d), BF)
        for r, array, i in w_pieces:
            w = lax.dynamic_update_slice(w, array[i], (0, (j ^ r) * band, 0))
        w_pieces = [(None, w[None], 0)]

    half = d // 2
    groups = (
        (slice(0, 1), ((0, half),)),
        (slice(0, 2), ((half, cut), (0, d - cut))),
    )
    order, keeps, parts = scalars, [], []
    for chunks, spans in groups:
        tokens = own_pieces[chunks], nb_pieces[chunks], spans
        *far, keep_far = partial_grad(
            n, bands, band, True, (half // 2, half // 2), order, hs_own, hs_nb, *tokens
        )
        order = after(scalars, far[0])
        keeps.append(keep_far)
        parts.append([swap(x, 1) for x in far])
    going = joined(keeps, parts)
    there = swap(going, bands // 2)
    gh_nb, sg_nb = backward(
        n, after(scalars, going), nb_pieces, w_pieces, f, hid_nb, wt_nb, rank_nb, False
    )
    sg_in = swap(sg_nb.reshape(n, experts, toks), bands)
    gh_own, sg_own = backward(
        n, after(scalars, sg_in), own_pieces, w_pieces, f, hidden_cache, wt_own, rank_own, True
    )
    spans = ((0, cut), (0, d - cut))
    *near, keep = partial_grad(
        n, bands, band, False, (half, half), after(scalars, sg_own), hs_own, hs_nb, own_pieces, nb_pieces, spans
    )
    near = [swap(x, 1) for x in near]
    if bands == 4:
        grad_down = finish(keep, near, there)
    else:
        total = keep.astype(F32) + jnp.concatenate(near, axis=3).astype(F32) + there.astype(F32)
        mid = bands // 8
        while mid:
            total, mid = total[:mid] + swap(total[mid:].astype(BF), 4 * mid).astype(F32), mid // 2
        grad_down = total[0].astype(BF)

    grad_hidden = insert(scalars, swap(after(gh_nb, sg_in), bands), gh_own)
    sg = sg_own.reshape(n, experts, toks) + sg_in
    by_expert = lax.all_to_all(sg, "expert", split_axis=0, concat_axis=0, tiled=True)
    by_expert = by_expert.reshape(EXPERTS, 1, toks)
    chosen = expert_ids.T[None] == jnp.arange(EXPERTS, dtype=jnp.int32)[:, None, None]
    grad_probs = jnp.sum(jnp.where(chosen, by_expert, 0.0), axis=0).T
    return grad_hidden[None], grad_down, grad_probs


def solution(mesh):
    tokens = P(("dp", "expert"), None)
    cache = P("dp", "expert", None, None, None)
    weights = P("expert", "dp", None)
    return jax.shard_map(
        functools.partial(per_device, mesh.shape["dp"], mesh.shape["expert"]),
        mesh=mesh,
        in_specs=(tokens, tokens, tokens, cache, weights),
        out_specs=(cache, weights, tokens),
        check_vma=False,
    )
```

```python
import functools

import jax
import jax.numpy as jnp
from jax import lax
from jax.experimental import pallas as pl
from jax.experimental.pallas import tpu as pltpu
from jax.sharding import PartitionSpec as P

EXPERTS = 16
CAP = 72
BF = jnp.bfloat16
F32 = jnp.float32
SHORT = pl.CostEstimate(flops=1, bytes_accessed=1, transcendentals=0)


def iota(shape, dim):
    return lax.broadcasted_iota(jnp.int32, shape, dim)


def after(x, *others):
    return lax.optimization_barrier((x, *others))[0]


def hidden_kernel(n, experts, sc_ref, tab_ref, hid_ref, hst_ref, wt_ref, rank_ref):
    toks = tab_ref.shape[1]
    earlier = (iota((toks, toks), 0) < iota((toks, toks), 1)).astype(BF)
    slots = iota((CAP, toks), 0).astype(F32)
    table = tab_ref[...].astype(F32)
    rank = jnp.dot((table > 0).astype(F32).astype(BF), earlier, preferred_element_type=F32)
    for k in range(n):
        s = lax.rem(sc_ref[0] + n - k, n)
        for e in range(experts):
            at = k * experts + e
            w_row, r_row = table[at : at + 1], rank[at : at + 1]
            place = jnp.where(slots == r_row, w_row, 0.0).astype(BF)
            moved = lax.dot_general(
                hid_ref[0, e, s], place, (((0,), (0,)), ((), ())), preferred_element_type=F32
            )
            hst_ref[e, :, k * toks : (k + 1) * toks] = moved.astype(BF)
            wt_ref[k, e] = w_row
            rank_ref[k, e] = r_row


def hidden_to_tokens(n, experts, toks, scalars, tokens, hid, f, whole):
    row = jax.ShapeDtypeStruct((n, experts, 1, toks), F32)
    row_spec = pl.BlockSpec((n, experts, 1, toks), lambda i, sc: (0, 0, 0, 0))
    lines = n * experts
    return pl.pallas_call(
        functools.partial(hidden_kernel, n, experts),
        out_shape=(jax.ShapeDtypeStruct((experts, f, n * toks), BF), row, row),
        grid_spec=pltpu.PrefetchScalarGridSpec(
            num_scalar_prefetch=1,
            grid=(1,),
            in_specs=[
                pl.BlockSpec((lines, toks), lambda i, sc: (n * toks // lines, 0)),
                pl.BlockSpec((1, experts, n, CAP, f), lambda i, sc: (0, 0, 0, 0, sc[1] if whole else 0)),
            ],
            out_specs=(
                pl.BlockSpec((experts, f, n * toks), lambda i, sc: (0, 0, 0)),
                row_spec,
                row_spec,
            ),
        ),
        compiler_params=pltpu.CompilerParams(vmem_limit_bytes=12 << 20),
        cost_estimate=SHORT,
    )(scalars, tokens, hid)


def below_kernel(n, experts, sc_ref, *refs):
    *blocks, out_ref = refs
    z = sc_ref[0]
    toks = blocks[0].shape[0] - EXPERTS
    line = iota((EXPERTS, toks), 0)

    def put(k, ref):
        out_ref[k * toks : (k + 1) * toks] = ref[:toks]
        table = ref[toks:, :toks].astype(F32)
        rows = [
            jnp.sum(jnp.where(line == z * experts + e, table, 0.0), axis=0, keepdims=True)
            for e in range(experts)
        ]
        return rows

    tables = [put(k, blocks[k]) for k in range(n)]
    if len(blocks) > n:
        passed = blocks[n]
        rows = [
            jnp.sum(jnp.where(line == z * experts + e, passed[toks:, :toks].astype(F32), 0.0), axis=0, keepdims=True)
            for e in range(experts)
        ]
        for k, place in ((1, 0), (n - 1, n - 1)):
            tables[k] = [jnp.where(z == place, new, old) for new, old in zip(rows, tables[k])]

            @pl.when(z == place)
            def _():
                out_ref[k * toks : (k + 1) * toks] = passed[:toks]

    rows = [row for table in tables for row in table]
    out_ref[n * toks :, :toks] = jnp.concatenate(rows, axis=0).astype(BF)


def below(n, experts, scalars, blocks):
    rows, cols = blocks[0].shape
    toks = rows - EXPERTS
    return pl.pallas_call(
        functools.partial(below_kernel, n, experts),
        out_shape=jax.ShapeDtypeStruct((n * (toks + experts), cols), BF),
        grid_spec=pltpu.PrefetchScalarGridSpec(
            num_scalar_prefetch=1,
            grid=(1,),
            in_specs=[pl.BlockSpec((rows, cols), lambda i, sc: (0, 0))] * len(blocks),
            out_specs=pl.BlockSpec((n * (toks + experts), cols), lambda i, sc: (0, 0)),
        ),
        compiler_params=pltpu.CompilerParams(vmem_limit_bytes=12 << 20),
        cost_estimate=SHORT,
    )(scalars, *blocks)


def flat(pieces):
    arrays = [a for chunk in pieces for a, _, _ in chunk]
    specs = [
        pl.BlockSpec(shape, functools.partial(lambda at, i, sc: at, at))
        for chunk in pieces
        for _, shape, at in chunk
    ]
    return arrays, specs, [len(chunk) for chunk in pieces]


def gathered(refs, counts, n, z, spans=None):
    chunks, at = [], 0
    for i, count in enumerate(counts):
        cols = slice(*spans[i]) if spans else slice(None)
        pieces = [refs[at + k][:, cols] for k in range(count)]
        if count > n:
            passed = pieces.pop()
            for k, place in ((1, 0), (n - 1, n - 1)):
                pieces[k] = jnp.where(z == place, passed, pieces[k])
        chunks.append(pieces[0] if len(pieces) == 1 else jnp.concatenate(pieces, axis=0))
        at += count
    return chunks, at


def back_kernel(n, counts, group, rels, sc_ref, *refs):
    chunks, at = gathered(refs, counts, n, sc_ref[0])
    w_refs, refs = refs[at : at + len(rels)], refs[at + len(rels) :]
    hid_ref, wt_ref, rank_ref, gh_ref, sg_ref, w_all = refs
    toks, (f, d) = wt_ref.shape[3], w_all.shape[1:]
    for rel, ref in zip(rels, w_refs):
        rows = ref.shape[2]
        start = 0 if rel is None else pl.multiple_of((sc_ref[2] ^ rel) * rows, rows)
        for e in range(group):
            w_all[e, pl.ds(start, rows), :] = ref[0, e]
    tokens = chunks[0] if len(chunks) == 1 else jnp.concatenate(chunks, axis=1)
    z = lax.dot_general(
        tokens, w_all[...].reshape(group * f, d), (((1,), (1,)), ((), ())), preferred_element_type=F32
    )
    eye = iota((toks, toks), 0) == iota((toks, toks), 1)
    slots = iota((CAP, toks), 0).astype(F32)
    for e in range(group):
        for k in range(n):
            s = lax.rem(sc_ref[0] + n - k, n)
            w_row, r_row = wt_ref[k, e], rank_ref[k, e]
            here = (slots == r_row) & (w_row > 0)
            pick = jnp.where(here, 1.0, 0.0).astype(BF)
            weigh = jnp.where(here, w_row, 0.0).astype(BF)
            zk = z[k * toks : (k + 1) * toks, e * f : (e + 1) * f]
            gh_ref[e, s] = jnp.dot(weigh, zk.astype(BF), preferred_element_type=F32).astype(BF)
            hid = lax.dot_general(
                pick, hid_ref[0, e, s], (((0,), (0,)), ((), ())), preferred_element_type=F32
            )
            sg_col = jnp.sum(zk * hid, axis=1, keepdims=True)
            sg_ref[s, e] = jnp.sum(jnp.where(eye, sg_col, 0.0), axis=0, keepdims=True)


def backward(n, scalars, pieces, w_pieces, f, hid, wt, rank, whole):
    _, experts, band, d = w_pieces[0][1].shape
    toks = wt.shape[3]
    rels = [rel for rel, _, _ in w_pieces]
    group = 2 if experts % 2 == 0 else 1
    arrays, specs, counts = flat(pieces)
    row_spec = pl.BlockSpec((n, group, 1, toks), lambda e, sc: (0, e, 0, 0))
    return pl.pallas_call(
        functools.partial(back_kernel, n, counts, group, rels),
        out_shape=(
            jax.ShapeDtypeStruct((experts, n, CAP, 2 * f if whole else f), BF),
            jax.ShapeDtypeStruct((n, experts, 1, toks), F32),
        ),
        grid_spec=pltpu.PrefetchScalarGridSpec(
            num_scalar_prefetch=1,
            grid=(experts // group,),
            in_specs=specs
            + [
                pl.BlockSpec((1, group, band, d), functools.partial(lambda i, e, sc: (i, e, 0, 0), i))
                for _, _, i in w_pieces
            ]
            + [
                pl.BlockSpec((1, group, n, CAP, f), lambda e, sc: (0, e, 0, 0, sc[1] if whole else 0)),
                row_spec,
                row_spec,
            ],
            out_specs=(pl.BlockSpec((group, n, CAP, f), lambda e, sc: (e, 0, 0, sc[1] if whole else 0)), row_spec),
            scratch_shapes=[pltpu.VMEM((group, f, d), BF)],
        ),
        compiler_params=pltpu.CompilerParams(vmem_limit_bytes=24 << 20),
        cost_estimate=SHORT,
    )(scalars, *arrays, *[w for _, w, _ in w_pieces], hid, wt, rank)


def part_kernel(n, bands, counts, spans, sc_ref, *refs):
    own, at_own = gathered(refs, counts[0], n, sc_ref[0], spans)
    nb, at_nb = gathered(refs[at_own:], counts[1], n, sc_ref[0], spans)
    own_ref, nb_ref, *send_refs, keep_ref = refs[at_own + at_nb :]
    tokens = jnp.concatenate(
        [jnp.concatenate(c, axis=1) if len(c) > 1 else c[0] for c in (own, nb)], axis=0
    )
    hidden = jnp.concatenate([own_ref[0], nb_ref[0]], axis=1)
    total = jnp.dot(hidden, tokens, preferred_element_type=F32)
    quarter, _, band, cols = keep_ref.shape
    total = total.reshape(bands // 2, band, cols).astype(BF)
    for a in range(bands // 2):
        rel = (sc_ref[2] % (bands // 2)) ^ a
        at = rel // 2

        @pl.when(rel % 2 == 1)
        def _():
            done = 0
            for ref in send_refs:
                width = ref.shape[3]
                ref[at, 0] = total[a, :, done : done + width]
                done += width

        @pl.when(rel % 2 == 0)
        def _():
            keep_ref[at, 0] = total[a]


def partial_grad(n, bands, band, far, parts, scalars, own, nb, pieces_own, pieces_nb, spans):
    experts, f, k = own.shape
    arrays, specs, counts = flat(pieces_own)
    arrays_nb, specs_nb, counts_nb = flat(pieces_nb)
    cols = sum(stop - start for start, stop in spans)
    widths = (*parts, cols)
    half = bands // 2
    hs_spec = pl.BlockSpec((1, f // 2, k), lambda e, sc: (e, (sc[2] // half) ^ int(far), 0))
    return pl.pallas_call(
        functools.partial(part_kernel, n, bands, (counts, counts_nb), spans),
        out_shape=[jax.ShapeDtypeStruct((bands // 4, experts, band, width), BF) for width in widths],
        grid_spec=pltpu.PrefetchScalarGridSpec(
            num_scalar_prefetch=1,
            grid=(experts,),
            in_specs=specs + specs_nb + [hs_spec, hs_spec],
            out_specs=[pl.BlockSpec((bands // 4, 1, band, width), lambda e, sc: (0, e, 0, 0)) for width in widths],
        ),
        compiler_params=pltpu.CompilerParams(vmem_limit_bytes=20 << 20),
        cost_estimate=SHORT,
    )(scalars, *arrays, *arrays_nb, own, nb)


def joined_kernel(groups, *refs):
    total, at = None, 0
    for count in groups:
        parts = [ref[...].astype(F32) for ref in refs[at : at + count]]
        term = parts[0] if count == 1 else jnp.concatenate(parts, axis=3)
        total = term if total is None else total + term
        at += count
    refs[-1][...] = total.astype(BF)


def joined(terms):
    arrays = [part for term in terms for part in term]
    lead, experts, band, _ = arrays[0].shape
    d = sum(part.shape[3] for part in terms[0])
    block = lambda x: pl.BlockSpec((x.shape[0], 1, *x.shape[2:]), lambda e: (0, e, 0, 0))
    out, spec = (lead, experts, band, d), pl.BlockSpec((lead, 1, band, d), lambda e: (0, e, 0, 0))
    return pl.pallas_call(
        functools.partial(joined_kernel, [len(term) for term in terms]),
        out_shape=jax.ShapeDtypeStruct(out, BF),
        grid=(experts,),
        in_specs=[block(x) for x in arrays],
        out_specs=spec,
        compiler_params=pltpu.CompilerParams(vmem_limit_bytes=8 << 20),
        cost_estimate=SHORT,
    )(*arrays)


def finish_kernel(sc_ref, base_ref, there_ref, new_ref, old_ref, down_ref, hidden_ref):
    down_ref[0] = (base_ref[0, 0].astype(F32) + there_ref[0, 0].astype(F32)).astype(BF)
    hidden_ref[...] = new_ref[...]


def finish(scalars, base, there, new, whole):
    _, experts, band, d = base.shape
    _, n, cap, f = new.shape
    sums = pl.BlockSpec((1, 1, band, d), lambda e, sc: (0, e, 0, 0))
    return pl.pallas_call(
        finish_kernel,
        out_shape=(jax.ShapeDtypeStruct((experts, band, d), BF), jax.ShapeDtypeStruct(whole.shape, BF)),
        grid_spec=pltpu.PrefetchScalarGridSpec(
            num_scalar_prefetch=1,
            grid=(experts,),
            in_specs=[
                sums,
                sums,
                pl.BlockSpec((1, n, cap, f), lambda e, sc: (e, 0, 0, 0)),
                pl.BlockSpec(memory_space=pl.ANY),
            ],
            out_specs=(
                pl.BlockSpec((1, band, d), lambda e, sc: (e, 0, 0)),
                pl.BlockSpec((1, n, cap, f), lambda e, sc: (e, 0, 0, 1 - sc[1])),
            ),
        ),
        input_output_aliases={4: 1},
        compiler_params=pltpu.CompilerParams(vmem_limit_bytes=12 << 20),
        cost_estimate=SHORT,
    )(scalars, base, there, new, whole)


def per_device(n_dp, n, grad_out, expert_ids, route_weights, hidden_cache, w_down):
    dp, z = lax.axis_index("dp"), lax.axis_index("expert")
    bands = n_dp // 2
    upper, j = dp // bands, dp % bands
    experts, band, d = w_down.shape
    toks = grad_out.shape[0]
    f = bands * band

    def swap(x, bit):
        return lax.ppermute(x, "dp", [(i, i ^ bit) for i in range(n_dp)])

    def spread(x):
        if n != 4:
            return [x] + [
                lax.ppermute(x, "expert", [(i, (i + k) % n) for i in range(n)]) for k in range(1, n)
            ]
        two = lax.ppermute(x, "expert", [(i, (i + 2) % n) for i in range(n)])
        one = lax.ppermute(x, "expert", [(i, i + 1) for i in range(n - 1)])
        three = lax.ppermute(x, "expert", [(i + 1, i) for i in range(n - 1)])
        passed = lax.ppermute(two, "expert", [(2, 3), (1, 0)])
        return [x, one, two, three, passed]

    ids = expert_ids[None] == jnp.arange(EXPERTS, dtype=jnp.int32)[:, None, None]
    table = jnp.sum(jnp.where(ids, route_weights.astype(F32)[None], 0.0), axis=2).astype(BF)

    cut = 10 * d // 16
    table = jnp.pad(table, ((0, 0), (0, cut - toks)))
    blocks = spread(jnp.concatenate([grad_out[:, :cut], table], axis=0))
    w_core = swap(w_down[None], 1)
    outgoing = lax.dynamic_slice_in_dim(hidden_cache, (1 - upper) * f, f, axis=4).reshape(-1, f)
    lefts = [min(left, d - f) for left in range(cut, d, f)]
    outgoing = [outgoing] + [grad_out[:, left : left + f] for left in lefts]
    incoming = swap(after(jnp.concatenate(outgoing, axis=0), w_core), bands)
    count = hidden_cache.size // (2 * f)
    hid_nb = incoming[:count].reshape(1, experts, n, CAP, f)
    pair = [
        incoming[count + i * toks : count + (i + 1) * toks, cut + i * f - left :] for i, left in enumerate(lefts)
    ]
    w_pieces = [(0, w_down[None], 0), (1, w_core, 0)]
    bit = 2
    while bit < bands:
        far = swap(w_down[None] if bit == 2 else jnp.concatenate([a for _, a, _ in w_pieces[::2]]), bit)
        there = swap(far, 1)
        for i in range(far.shape[0]):
            w_pieces += [(w_pieces[2 * i][0] ^ bit, far, i), (w_pieces[2 * i][0] ^ bit ^ 1, there, i)]
        bit *= 2

    scalars = jnp.stack([z, upper, j]).astype(jnp.int32)
    mine = below(n, experts, scalars, blocks)
    hs_own, wt_own, rank_own = hidden_to_tokens(n, experts, toks, scalars, mine, hidden_cache, f, True)
    rest = jnp.concatenate([grad_out[:, cut:], jnp.concatenate(pair, axis=1)], axis=0)
    rests = spread(after(rest, *blocks))
    nb_a = swap(after(mine, incoming), bands)
    hs_nb, wt_nb, rank_nb = hidden_to_tokens(n, experts, toks, scalars, nb_a, hid_nb, f, False)

    own_pieces = [[(mine, (n * toks, cut), (0, 0))], [(b, (toks, d - cut), (0, 0)) for b in rests]]
    nb_pieces = [[(nb_a, (n * toks, cut), (0, 0))], [(b, (toks, d - cut), (1, 0)) for b in rests]]

    if band % 16:
        w = jnp.zeros((experts, f, d), BF)
        for r, array, i in w_pieces:
            w = lax.dynamic_update_slice(w, array[i], (0, (j ^ r) * band, 0))
        w_pieces = [(None, w[None], 0)]

    half = d // 2
    groups = (
        (slice(0, 1), ((0, half),)),
        (slice(0, 2), ((half, cut), (0, d - cut))),
    )
    order, sums = scalars, []
    for chunks, spans in groups:
        tokens = own_pieces[chunks], nb_pieces[chunks], spans
        width = sum(stop - start for start, stop in spans) // 2
        *far, keep_far = partial_grad(n, bands, band, True, (width, width), order, hs_own, hs_nb, *tokens)
        order = after(scalars, far[0])
        sums.append([[keep_far], [swap(x, 1) for x in far]])
    going = joined([[x[i][k] for x in sums for k in ks] for i, ks in ((0, (0,)), (1, (0, 1)))])
    there = [swap(going, bands // 2)]
    gh_nb, sg_nb = backward(
        n, after(scalars, going), nb_pieces, w_pieces, f, hid_nb, wt_nb, rank_nb, False
    )
    sg_in = swap(sg_nb.reshape(n, experts, toks), bands)
    gh_own, sg_own = backward(
        n, after(scalars, sg_in), own_pieces, w_pieces, f, hidden_cache, wt_own, rank_own, True
    )
    sg = sg_own.reshape(n, experts, toks) + sg_in
    by_expert = lax.all_to_all(sg, "expert", split_axis=0, concat_axis=0, tiled=True)
    spans = ((0, cut), (0, d - cut))
    *near, keep = partial_grad(
        n, bands, band, False, (half, half), after(scalars, sg_own), hs_own, hs_nb, own_pieces, nb_pieces, spans
    )
    base = joined([[keep], [swap(x, 1) for x in near]])
    mid = bands // 8
    there = there[0]
    while mid:
        total = base.astype(F32) + there.astype(F32)
        base, there, mid = total[:mid].astype(BF), swap(total[mid:].astype(BF), 4 * mid), mid // 2
    gh_in = swap(after(gh_nb, sg_in), bands)
    grad_down, grad_hidden = finish(scalars, base, there, gh_in, gh_own)
    by_expert = by_expert.reshape(EXPERTS, 1, toks)
    chosen = expert_ids.T[None] == jnp.arange(EXPERTS, dtype=jnp.int32)[:, None, None]
    grad_probs = jnp.sum(jnp.where(chosen, by_expert, 0.0), axis=0).T
    return grad_hidden[None], grad_down, grad_probs


def solution(mesh):
    tokens = P(("dp", "expert"), None)
    cache = P("dp", "expert", None, None, None)
    weights = P("expert", "dp", None)
    return jax.shard_map(
        functools.partial(per_device, mesh.shape["dp"], mesh.shape["expert"]),
        mesh=mesh,
        in_specs=(tokens, tokens, tokens, cache, weights),
        out_specs=(cache, weights, tokens),
        check_vma=False,
    )
```

```python
import functools

import jax
import jax.numpy as jnp
from jax import lax
from jax.experimental import pallas as pl
from jax.experimental.pallas import tpu as pltpu
from jax.sharding import PartitionSpec as P

EXPERTS = 16
CAP = 72
PADDED = 80
BF = jnp.bfloat16
F32 = jnp.float32
SHORT = pl.CostEstimate(flops=1, bytes_accessed=1, transcendentals=0)


def iota(shape, dim):
    return lax.broadcasted_iota(jnp.int32, shape, dim)


def after(x, *others):
    return lax.optimization_barrier((x, *others))[0]


def hidden_kernel(n, experts, sc_ref, tab_ref, hid_ref, hst_ref, wt_ref, rank_ref):
    toks = tab_ref.shape[1]
    earlier = (iota((toks, toks), 0) < iota((toks, toks), 1)).astype(BF)
    slots = iota((CAP, toks), 0).astype(F32)
    table = tab_ref[...].astype(F32)
    rank = jnp.dot((table > 0).astype(F32).astype(BF), earlier, preferred_element_type=F32)
    for k in range(n):
        s = lax.rem(sc_ref[0] + n - k, n)
        for e in range(experts):
            at = k * experts + e
            w_row, r_row = table[at : at + 1], rank[at : at + 1]
            place = jnp.where(slots == r_row, w_row, 0.0).astype(BF)
            moved = lax.dot_general(
                hid_ref[0, e, s, :CAP], place, (((0,), (0,)), ((), ())), preferred_element_type=F32
            )
            hst_ref[e, :, k * toks : (k + 1) * toks] = moved.astype(BF)
            wt_ref[k, e] = w_row
            rank_ref[k, e] = r_row


def hidden_to_tokens(n, experts, toks, scalars, tokens, hid, f, whole):
    row = jax.ShapeDtypeStruct((n, experts, 1, toks), F32)
    row_spec = pl.BlockSpec((n, experts, 1, toks), lambda i, sc: (0, 0, 0, 0))
    lines = n * experts
    return pl.pallas_call(
        functools.partial(hidden_kernel, n, experts),
        out_shape=(jax.ShapeDtypeStruct((experts, f, n * toks), BF), row, row),
        grid_spec=pltpu.PrefetchScalarGridSpec(
            num_scalar_prefetch=1,
            grid=(1,),
            in_specs=[
                pl.BlockSpec((lines, toks), lambda i, sc: ((n - 1) * toks // lines, 0)),
                pl.BlockSpec((1, experts, n, hid.shape[3], f), lambda i, sc: (0, 0, 0, 0, sc[1] if whole else 0)),
            ],
            out_specs=(
                pl.BlockSpec((experts, f, n * toks), lambda i, sc: (0, 0, 0)),
                row_spec,
                row_spec,
            ),
        ),
        compiler_params=pltpu.CompilerParams(vmem_limit_bytes=12 << 20),
        cost_estimate=SHORT,
    )(scalars, tokens, hid)


def pack_kernel(lefts, sc_ref, hid_ref, tok_ref, out_ref):
    _, experts, n, cap, f = hid_ref.shape
    toks = tok_ref.shape[0]
    for e in range(experts):
        for s in range(n):
            at = (e * n + s) * PADDED
            out_ref[at : at + cap] = hid_ref[0, e, s]
            out_ref[at + cap : at + PADDED] = jnp.zeros((PADDED - cap, f), BF)
    for i, left in enumerate(lefts):
        at = experts * n * PADDED + i * toks
        out_ref[at : at + toks] = tok_ref[:, left : left + f]


def pack(scalars, hid, tok, lefts, f):
    _, experts, n, cap, _ = hid.shape
    rows = experts * n * PADDED + len(lefts) * tok.shape[0]
    return pl.pallas_call(
        functools.partial(pack_kernel, lefts),
        out_shape=jax.ShapeDtypeStruct((rows, f), BF),
        grid_spec=pltpu.PrefetchScalarGridSpec(
            num_scalar_prefetch=1,
            grid=(1,),
            in_specs=[
                pl.BlockSpec((1, experts, n, cap, f), lambda i, sc: (0, 0, 0, 0, 1 - sc[1])),
                pl.BlockSpec(tok.shape, lambda i, sc: (0, 0)),
            ],
            out_specs=pl.BlockSpec((rows, f), lambda i, sc: (0, 0)),
        ),
        compiler_params=pltpu.CompilerParams(vmem_limit_bytes=12 << 20),
        cost_estimate=SHORT,
    )(scalars, hid, tok)


def below_kernel(n, experts, sc_ref, *refs):
    *blocks, out_ref = refs
    z = sc_ref[0]
    toks = blocks[0].shape[0] - EXPERTS // 2
    line = iota((EXPERTS, toks), 0)

    def local(ref):
        table = ref[toks:, : 2 * toks].astype(F32)
        table = jnp.concatenate([table[:, :toks], table[:, toks:]], axis=0)
        return [
            jnp.sum(jnp.where(line == z * experts + e, table, 0.0), axis=0, keepdims=True)
            for e in range(experts)
        ]

    tables = [local(blocks[k]) for k in range(n)]
    for k in range(1, n):
        out_ref[(k - 1) * toks : k * toks] = blocks[k][:toks]
    if len(blocks) > n:
        passed = blocks[n]
        rows = local(passed)
        for k, place in ((1, 0), (n - 1, n - 1)):
            tables[k] = [jnp.where(z == place, new, old) for new, old in zip(rows, tables[k])]

            @pl.when(z == place)
            def _():
                out_ref[(k - 1) * toks : k * toks] = passed[:toks]

    rows = [row for table in tables for row in table]
    out_ref[(n - 1) * toks :, :toks] = jnp.concatenate(rows, axis=0).astype(BF)


def below(n, experts, scalars, blocks):
    rows, cols = blocks[0].shape
    toks = rows - EXPERTS // 2
    height = (n - 1) * toks + n * experts
    return pl.pallas_call(
        functools.partial(below_kernel, n, experts),
        out_shape=jax.ShapeDtypeStruct((height, cols), BF),
        grid_spec=pltpu.PrefetchScalarGridSpec(
            num_scalar_prefetch=1,
            grid=(1,),
            in_specs=[pl.BlockSpec((rows, cols), lambda i, sc: (0, 0))] * len(blocks),
            out_specs=pl.BlockSpec((height, cols), lambda i, sc: (0, 0)),
        ),
        compiler_params=pltpu.CompilerParams(vmem_limit_bytes=24 << 20),
        cost_estimate=SHORT,
    )(scalars, *blocks)


def flat(pieces):
    arrays = [a for chunk in pieces for a, _, _ in chunk]
    specs = [
        pl.BlockSpec(shape, functools.partial(lambda at, i, sc: at, at))
        for chunk in pieces
        for _, shape, at in chunk
    ]
    return arrays, specs, [len(chunk) for chunk in pieces]


def gathered(refs, counts, n, z, spans=None):
    chunks, at = [], 0
    for i, count in enumerate(counts):
        cols = slice(*spans[i]) if spans else slice(None)
        pieces = [refs[at + k][:, cols] for k in range(count)]
        if count > n:
            passed = pieces.pop()
            for k, place in ((1, 0), (n - 1, n - 1)):
                pieces[k] = jnp.where(z == place, passed, pieces[k])
        chunks.append(pieces[0] if len(pieces) == 1 else jnp.concatenate(pieces, axis=0))
        at += count
    return chunks, at


def back_kernel(n, counts, group, rels, sc_ref, *refs):
    chunks, at = gathered(refs, counts, n, sc_ref[0])
    w_refs, refs = refs[at : at + len(rels)], refs[at + len(rels) :]
    hid_ref, wt_ref, rank_ref, gh_ref, sg_ref, w_all = refs
    toks, (f, d) = wt_ref.shape[3], w_all.shape[1:]
    for rel, ref in zip(rels, w_refs):
        rows = ref.shape[2]
        start = 0 if rel is None else pl.multiple_of((sc_ref[2] ^ rel) * rows, rows)
        for e in range(group):
            w_all[e, pl.ds(start, rows), :] = ref[0, e]
    tokens = chunks[0] if len(chunks) == 1 else jnp.concatenate(chunks, axis=1)
    z = lax.dot_general(
        tokens, w_all[...].reshape(group * f, d), (((1,), (1,)), ((), ())), preferred_element_type=F32
    )
    eye = iota((toks, toks), 0) == iota((toks, toks), 1)
    slots = iota((CAP, toks), 0).astype(F32)
    for e in range(group):
        for k in range(n):
            s = lax.rem(sc_ref[0] + n - k, n)
            w_row, r_row = wt_ref[k, e], rank_ref[k, e]
            here = (slots == r_row) & (w_row > 0)
            pick = jnp.where(here, 1.0, 0.0).astype(BF)
            weigh = jnp.where(here, w_row, 0.0).astype(BF)
            zk = z[k * toks : (k + 1) * toks, e * f : (e + 1) * f]
            gh_ref[e, s] = jnp.dot(weigh, zk.astype(BF), preferred_element_type=F32).astype(BF)
            hid = lax.dot_general(
                pick, hid_ref[0, e, s, :CAP], (((0,), (0,)), ((), ())), preferred_element_type=F32
            )
            sg_col = jnp.sum(zk * hid, axis=1, keepdims=True)
            sg_ref[s, e] = jnp.sum(jnp.where(eye, sg_col, 0.0), axis=0, keepdims=True)


def backward(n, scalars, pieces, w_pieces, f, hid, wt, rank, whole):
    _, experts, band, d = w_pieces[0][1].shape
    toks = wt.shape[3]
    rels = [rel for rel, _, _ in w_pieces]
    group = 2 if experts % 2 == 0 else 1
    arrays, specs, counts = flat(pieces)
    row_spec = pl.BlockSpec((n, group, 1, toks), lambda e, sc: (0, e, 0, 0))
    return pl.pallas_call(
        functools.partial(back_kernel, n, counts, group, rels),
        out_shape=(
            jax.ShapeDtypeStruct((experts, n, CAP, 2 * f if whole else f), BF),
            jax.ShapeDtypeStruct((n, experts, 1, toks), F32),
        ),
        grid_spec=pltpu.PrefetchScalarGridSpec(
            num_scalar_prefetch=1,
            grid=(experts // group,),
            in_specs=specs
            + [
                pl.BlockSpec((1, group, band, d), functools.partial(lambda i, e, sc: (i, e, 0, 0), i))
                for _, _, i in w_pieces
            ]
            + [
                pl.BlockSpec((1, group, n, hid.shape[3], f), lambda e, sc: (0, e, 0, 0, sc[1] if whole else 0)),
                row_spec,
                row_spec,
            ],
            out_specs=(pl.BlockSpec((group, n, CAP, f), lambda e, sc: (e, 0, 0, sc[1] if whole else 0)), row_spec),
            scratch_shapes=[pltpu.VMEM((group, f, d), BF)],
        ),
        compiler_params=pltpu.CompilerParams(vmem_limit_bytes=24 << 20),
        cost_estimate=SHORT,
    )(scalars, *arrays, *[w for _, w, _ in w_pieces], hid, wt, rank)


def part_kernel(n, bands, counts, spans, sc_ref, *refs):
    own, at_own = gathered(refs, counts[0], n, sc_ref[0], spans)
    nb, at_nb = gathered(refs[at_own:], counts[1], n, sc_ref[0], spans)
    own_ref, nb_ref, *send_refs, keep_ref = refs[at_own + at_nb :]
    tokens = jnp.concatenate(
        [jnp.concatenate(c, axis=1) if len(c) > 1 else c[0] for c in (own, nb)], axis=0
    )
    hidden = jnp.concatenate([own_ref[0], nb_ref[0]], axis=1)
    total = jnp.dot(hidden, tokens, preferred_element_type=F32)
    quarter, _, band, cols = keep_ref.shape
    total = total.reshape(bands // 2, band, cols).astype(BF)
    for a in range(bands // 2):
        rel = (sc_ref[2] % (bands // 2)) ^ a
        at = rel // 2

        @pl.when(rel % 2 == 1)
        def _():
            done = 0
            for ref in send_refs:
                width = ref.shape[3]
                ref[at, 0] = total[a, :, done : done + width]
                done += width

        @pl.when(rel % 2 == 0)
        def _():
            keep_ref[at, 0] = total[a]


def partial_grad(n, bands, band, far, parts, scalars, own, nb, pieces_own, pieces_nb, spans):
    experts, f, k = own.shape
    arrays, specs, counts = flat(pieces_own)
    arrays_nb, specs_nb, counts_nb = flat(pieces_nb)
    cols = sum(stop - start for start, stop in spans)
    widths = (*parts, cols)
    half = bands // 2
    hs_spec = pl.BlockSpec((1, f // 2, k), lambda e, sc: (e, (sc[2] // half) ^ int(far), 0))
    return pl.pallas_call(
        functools.partial(part_kernel, n, bands, (counts, counts_nb), spans),
        out_shape=[jax.ShapeDtypeStruct((bands // 4, experts, band, width), BF) for width in widths],
        grid_spec=pltpu.PrefetchScalarGridSpec(
            num_scalar_prefetch=1,
            grid=(experts,),
            in_specs=specs + specs_nb + [hs_spec, hs_spec],
            out_specs=[pl.BlockSpec((bands // 4, 1, band, width), lambda e, sc: (0, e, 0, 0)) for width in widths],
        ),
        compiler_params=pltpu.CompilerParams(vmem_limit_bytes=20 << 20),
        cost_estimate=SHORT,
    )(scalars, *arrays, *arrays_nb, own, nb)


def joined_kernel(groups, *refs):
    total, at = None, 0
    for count in groups:
        parts = [ref[...].astype(F32) for ref in refs[at : at + count]]
        term = parts[0] if count == 1 else jnp.concatenate(parts, axis=3)
        total = term if total is None else total + term
        at += count
    refs[-1][...] = total.astype(BF)


def joined(terms):
    arrays = [part for term in terms for part in term]
    lead, experts, band, _ = arrays[0].shape
    d = sum(part.shape[3] for part in terms[0])
    block = lambda x: pl.BlockSpec((x.shape[0], 1, *x.shape[2:]), lambda e: (0, e, 0, 0))
    out, spec = (lead, experts, band, d), pl.BlockSpec((lead, 1, band, d), lambda e: (0, e, 0, 0))
    return pl.pallas_call(
        functools.partial(joined_kernel, [len(term) for term in terms]),
        out_shape=jax.ShapeDtypeStruct(out, BF),
        grid=(experts,),
        in_specs=[block(x) for x in arrays],
        out_specs=spec,
        compiler_params=pltpu.CompilerParams(vmem_limit_bytes=8 << 20),
        cost_estimate=SHORT,
    )(*arrays)


def finish_kernel(sc_ref, base_ref, there_ref, new_ref, old_ref, down_ref, hidden_ref):
    down_ref[0] = (base_ref[0, 0].astype(F32) + there_ref[0, 0].astype(F32)).astype(BF)
    hidden_ref[...] = new_ref[...]


def finish(scalars, base, there, new, whole):
    _, experts, band, d = base.shape
    _, n, cap, f = new.shape
    sums = pl.BlockSpec((1, 1, band, d), lambda e, sc: (0, e, 0, 0))
    return pl.pallas_call(
        finish_kernel,
        out_shape=(jax.ShapeDtypeStruct((experts, band, d), BF), jax.ShapeDtypeStruct(whole.shape, BF)),
        grid_spec=pltpu.PrefetchScalarGridSpec(
            num_scalar_prefetch=1,
            grid=(experts,),
            in_specs=[
                sums,
                sums,
                pl.BlockSpec((1, n, cap, f), lambda e, sc: (e, 0, 0, 0)),
                pl.BlockSpec(memory_space=pl.ANY),
            ],
            out_specs=(
                pl.BlockSpec((1, band, d), lambda e, sc: (e, 0, 0)),
                pl.BlockSpec((1, n, cap, f), lambda e, sc: (e, 0, 0, 1 - sc[1])),
            ),
        ),
        input_output_aliases={4: 1},
        compiler_params=pltpu.CompilerParams(vmem_limit_bytes=12 << 20),
        cost_estimate=SHORT,
    )(scalars, base, there, new, whole)


def per_device(n_dp, n, grad_out, expert_ids, route_weights, hidden_cache, w_down):
    dp, z = lax.axis_index("dp"), lax.axis_index("expert")
    bands = n_dp // 2
    upper, j = dp // bands, dp % bands
    experts, band, d = w_down.shape
    toks = grad_out.shape[0]
    f = bands * band

    def swap(x, bit):
        return lax.ppermute(x, "dp", [(i, i ^ bit) for i in range(n_dp)])

    def spread(x):
        if n != 4:
            return [x] + [
                lax.ppermute(x, "expert", [(i, (i + k) % n) for i in range(n)]) for k in range(1, n)
            ]
        two = lax.ppermute(x, "expert", [(i, (i + 2) % n) for i in range(n)])
        one = lax.ppermute(x, "expert", [(i, i + 1) for i in range(n - 1)])
        three = lax.ppermute(x, "expert", [(i + 1, i) for i in range(n - 1)])
        passed = lax.ppermute(two, "expert", [(2, 3), (1, 0)])
        return [x, one, two, three, passed]

    ids = expert_ids[None] == jnp.arange(EXPERTS, dtype=jnp.int32)[:, None, None]
    table = jnp.sum(jnp.where(ids, route_weights.astype(F32)[None], 0.0), axis=2).astype(BF)

    cut = 11 * d // 16
    table = jnp.concatenate([table[: EXPERTS // 2], table[EXPERTS // 2 :]], axis=1)
    table = jnp.pad(table, ((0, 0), (0, cut - 2 * toks)))
    blocks = spread(jnp.concatenate([grad_out[:, :cut], table], axis=0))
    w_core = swap(w_down[None], 1)
    scalars = jnp.stack([z, upper, j]).astype(jnp.int32)
    lefts = [min(left, d - f) for left in range(0, d, f)]
    outgoing = pack(scalars, hidden_cache, grad_out, lefts, f)
    incoming = swap(after(outgoing, w_core), bands)
    count = experts * n * PADDED
    hid_nb = incoming[:count].reshape(1, experts, n, PADDED, f)
    first_nb = jnp.concatenate(
        [incoming[count + i * toks : count + (i + 1) * toks, i * f - left :] for i, left in enumerate(lefts)], axis=1
    )
    first_nb, pair = first_nb[:, :cut], first_nb[:, cut:]
    w_pieces = [(0, w_down[None], 0), (1, w_core, 0)]
    bit = 2
    while bit < bands:
        far = swap(w_down[None] if bit == 2 else jnp.concatenate([a for _, a, _ in w_pieces[::2]]), bit)
        there = swap(far, 1)
        for i in range(far.shape[0]):
            w_pieces += [(w_pieces[2 * i][0] ^ bit, far, i), (w_pieces[2 * i][0] ^ bit ^ 1, there, i)]
        bit *= 2

    mine = below(n, experts, scalars, blocks)
    hs_own, wt_own, rank_own = hidden_to_tokens(n, experts, toks, scalars, mine, hidden_cache, f, True)
    rest = jnp.concatenate([grad_out[:, cut:], pair], axis=0)
    rests = spread(after(rest, *blocks))
    nb_a = swap(after(mine, incoming), bands)
    hs_nb, wt_nb, rank_nb = hidden_to_tokens(n, experts, toks, scalars, nb_a, hid_nb, f, False)

    own_pieces = [[(blocks[0], (toks, cut), (0, 0)), (mine, ((n - 1) * toks, cut), (0, 0))], [(b, (toks, d - cut), (0, 0)) for b in rests]]
    nb_pieces = [[(first_nb, (toks, cut), (0, 0)), (nb_a, ((n - 1) * toks, cut), (0, 0))], [(b, (toks, d - cut), (1, 0)) for b in rests]]

    if band % 16:
        w = jnp.zeros((experts, f, d), BF)
        for r, array, i in w_pieces:
            w = lax.dynamic_update_slice(w, array[i], (0, (j ^ r) * band, 0))
        w_pieces = [(None, w[None], 0)]

    half = d // 2
    groups = (
        (slice(0, 1), ((0, half),)),
        (slice(0, 2), ((half, cut), (0, d - cut))),
    )
    order, sums = scalars, []
    for chunks, spans in groups:
        tokens = own_pieces[chunks], nb_pieces[chunks], spans
        width = sum(stop - start for start, stop in spans) // 2
        *far, keep_far = partial_grad(n, bands, band, True, (width, width), order, hs_own, hs_nb, *tokens)
        order = after(scalars, far[0])
        sums.append([[keep_far], [swap(x, 1) for x in far]])
    going = joined([[x[i][k] for x in sums for k in ks] for i, ks in ((0, (0,)), (1, (0, 1)))])
    there = [swap(going, bands // 2)]
    gh_nb, sg_nb = backward(
        n, after(scalars, going), nb_pieces, w_pieces, f, hid_nb, wt_nb, rank_nb, False
    )
    sg_in = swap(sg_nb.reshape(n, experts, toks), bands)
    gh_own, sg_own = backward(
        n, after(scalars, sg_in), own_pieces, w_pieces, f, hidden_cache, wt_own, rank_own, True
    )
    sg = sg_own.reshape(n, experts, toks) + sg_in
    by_expert = lax.all_to_all(sg, "expert", split_axis=0, concat_axis=0, tiled=True)
    spans = ((0, cut), (0, d - cut))
    *near, keep = partial_grad(
        n, bands, band, False, (half, half), after(scalars, sg_own), hs_own, hs_nb, own_pieces, nb_pieces, spans
    )
    base = joined([[keep], [swap(x, 1) for x in near]])
    mid = bands // 8
    there = there[0]
    while mid:
        total = base.astype(F32) + there.astype(F32)
        base, there, mid = total[:mid].astype(BF), swap(total[mid:].astype(BF), 4 * mid), mid // 2
    gh_in = swap(after(gh_nb, sg_in), bands)
    grad_down, grad_hidden = finish(scalars, base, there, gh_in, gh_own)
    by_expert = by_expert.reshape(EXPERTS, 1, toks)
    chosen = expert_ids.T[None] == jnp.arange(EXPERTS, dtype=jnp.int32)[:, None, None]
    grad_probs = jnp.sum(jnp.where(chosen, by_expert, 0.0), axis=0).T
    return grad_hidden[None], grad_down, grad_probs


def solution(mesh):
    tokens = P(("dp", "expert"), None)
    cache = P("dp", "expert", None, None, None)
    weights = P("expert", "dp", None)
    return jax.shard_map(
        functools.partial(per_device, mesh.shape["dp"], mesh.shape["expert"]),
        mesh=mesh,
        in_specs=(tokens, tokens, tokens, cache, weights),
        out_specs=(cache, weights, tokens),
        check_vma=False,
    )
```

```python
import functools

import jax
import jax.numpy as jnp
from jax import lax
from jax.experimental import pallas as pl
from jax.experimental.pallas import tpu as pltpu
from jax.sharding import PartitionSpec as P

EXPERTS = 16
CAP = 72
PADDED = 80
BF = jnp.bfloat16
F32 = jnp.float32
SHORT = pl.CostEstimate(flops=1, bytes_accessed=1, transcendentals=0)


def iota(shape, dim):
    return lax.broadcasted_iota(jnp.int32, shape, dim)


def after(x, *others):
    return lax.optimization_barrier((x, *others))[0]


def hidden_kernel(n, experts, sc_ref, tab_ref, hid_ref, hst_ref, wt_ref, rank_ref):
    toks = tab_ref.shape[1]
    earlier = (iota((toks, toks), 0) < iota((toks, toks), 1)).astype(BF)
    slots = iota((CAP, toks), 0).astype(F32)
    table = tab_ref[...].astype(F32)
    rank = jnp.dot((table > 0).astype(F32).astype(BF), earlier, preferred_element_type=F32)
    for k in range(n):
        s = lax.rem(sc_ref[0] + n - k, n)
        for e in range(experts):
            at = k * experts + e
            w_row, r_row = table[at : at + 1], rank[at : at + 1]
            place = jnp.where(slots == r_row, w_row, 0.0).astype(BF)
            moved = lax.dot_general(
                hid_ref[0, e, s, :CAP], place, (((0,), (0,)), ((), ())), preferred_element_type=F32
            )
            hst_ref[e, :, k * toks : (k + 1) * toks] = moved.astype(BF)
            wt_ref[k, e] = w_row
            rank_ref[k, e] = r_row


def hidden_to_tokens(n, experts, toks, scalars, tokens, hid, f, whole):
    row = jax.ShapeDtypeStruct((n, experts, 1, toks), F32)
    row_spec = pl.BlockSpec((n, experts, 1, toks), lambda i, sc: (0, 0, 0, 0))
    lines = n * experts
    return pl.pallas_call(
        functools.partial(hidden_kernel, n, experts),
        out_shape=(jax.ShapeDtypeStruct((experts, f, n * toks), BF), row, row),
        grid_spec=pltpu.PrefetchScalarGridSpec(
            num_scalar_prefetch=1,
            grid=(1,),
            in_specs=[
                pl.BlockSpec((lines, toks), lambda i, sc: ((n - 1) * toks // lines, 0)),
                pl.BlockSpec((1, experts, n, hid.shape[3], f), lambda i, sc: (0, 0, 0, 0, sc[1] if whole else 0)),
            ],
            out_specs=(
                pl.BlockSpec((experts, f, n * toks), lambda i, sc: (0, 0, 0)),
                row_spec,
                row_spec,
            ),
        ),
        compiler_params=pltpu.CompilerParams(vmem_limit_bytes=12 << 20),
        cost_estimate=SHORT,
    )(scalars, tokens, hid)


def pack_kernel(lefts, sc_ref, hid_ref, tok_ref, out_ref):
    _, experts, n, cap, f = hid_ref.shape
    toks = tok_ref.shape[0]
    for e in range(experts):
        for s in range(n):
            at = (e * n + s) * PADDED
            out_ref[at : at + cap] = hid_ref[0, e, s]
            out_ref[at + cap : at + PADDED] = jnp.zeros((PADDED - cap, f), BF)
    for i, left in enumerate(lefts):
        at = experts * n * PADDED + i * toks
        out_ref[at : at + toks] = tok_ref[:, left : left + f]


def pack(scalars, hid, tok, lefts, f):
    _, experts, n, cap, _ = hid.shape
    rows = experts * n * PADDED + len(lefts) * tok.shape[0]
    return pl.pallas_call(
        functools.partial(pack_kernel, lefts),
        out_shape=jax.ShapeDtypeStruct((rows, f), BF),
        grid_spec=pltpu.PrefetchScalarGridSpec(
            num_scalar_prefetch=1,
            grid=(1,),
            in_specs=[
                pl.BlockSpec((1, experts, n, cap, f), lambda i, sc: (0, 0, 0, 0, 1 - sc[1])),
                pl.BlockSpec(tok.shape, lambda i, sc: (0, 0)),
            ],
            out_specs=pl.BlockSpec((rows, f), lambda i, sc: (0, 0)),
        ),
        compiler_params=pltpu.CompilerParams(vmem_limit_bytes=12 << 20),
        cost_estimate=SHORT,
    )(scalars, hid, tok)


def below_kernel(n, experts, sc_ref, *refs):
    *blocks, out_ref = refs
    z = sc_ref[0]
    toks = blocks[0].shape[0] - EXPERTS // 2
    line = iota((EXPERTS, toks), 0)

    def local(ref):
        table = ref[toks:, : 2 * toks].astype(F32)
        table = jnp.concatenate([table[:, :toks], table[:, toks:]], axis=0)
        return [
            jnp.sum(jnp.where(line == z * experts + e, table, 0.0), axis=0, keepdims=True)
            for e in range(experts)
        ]

    tables = [local(blocks[k]) for k in range(n)]
    for k in range(1, n):
        out_ref[(k - 1) * toks : k * toks] = blocks[k][:toks]
    if len(blocks) > n:
        passed = blocks[n]
        rows = local(passed)
        for k, place in ((1, 0), (n - 1, n - 1)):
            tables[k] = [jnp.where(z == place, new, old) for new, old in zip(rows, tables[k])]

            @pl.when(z == place)
            def _():
                out_ref[(k - 1) * toks : k * toks] = passed[:toks]

    rows = [row for table in tables for row in table]
    out_ref[(n - 1) * toks :, :toks] = jnp.concatenate(rows, axis=0).astype(BF)


def below(n, experts, scalars, blocks):
    rows, cols = blocks[0].shape
    toks = rows - EXPERTS // 2
    height = (n - 1) * toks + n * experts
    return pl.pallas_call(
        functools.partial(below_kernel, n, experts),
        out_shape=jax.ShapeDtypeStruct((height, cols), BF),
        grid_spec=pltpu.PrefetchScalarGridSpec(
            num_scalar_prefetch=1,
            grid=(1,),
            in_specs=[pl.BlockSpec((rows, cols), lambda i, sc: (0, 0))] * len(blocks),
            out_specs=pl.BlockSpec((height, cols), lambda i, sc: (0, 0)),
        ),
        compiler_params=pltpu.CompilerParams(vmem_limit_bytes=24 << 20),
        cost_estimate=SHORT,
    )(scalars, *blocks)


def flat(pieces):
    arrays = [a for chunk in pieces for a, _, _ in chunk]
    specs = [
        pl.BlockSpec(shape, functools.partial(lambda at, i, sc: at, at))
        for chunk in pieces
        for _, shape, at in chunk
    ]
    return arrays, specs, [len(chunk) for chunk in pieces]


def gathered(refs, counts, n, z, spans=None):
    chunks, at = [], 0
    for i, count in enumerate(counts):
        cols = slice(*spans[i]) if spans else slice(None)
        pieces = [refs[at + k][:, cols] for k in range(count)]
        if count > n:
            passed = pieces.pop()
            for k, place in ((1, 0), (n - 1, n - 1)):
                pieces[k] = jnp.where(z == place, passed, pieces[k])
        chunks.append(pieces[0] if len(pieces) == 1 else jnp.concatenate(pieces, axis=0))
        at += count
    return chunks, at


def back_kernel(n, counts, group, rels, sc_ref, *refs):
    chunks, at = gathered(refs, counts, n, sc_ref[0])
    w_refs, refs = refs[at : at + len(rels)], refs[at + len(rels) :]
    hid_ref, wt_ref, rank_ref, *added, gh_ref, sg_ref, w_all = refs
    toks, (f, d) = wt_ref.shape[3], w_all.shape[1:]
    for rel, ref in zip(rels, w_refs):
        rows = ref.shape[2]
        start = 0 if rel is None else pl.multiple_of((sc_ref[2] ^ rel) * rows, rows)
        for e in range(group):
            w_all[e, pl.ds(start, rows), :] = ref[0, e]
    tokens = chunks[0] if len(chunks) == 1 else jnp.concatenate(chunks, axis=1)
    z = lax.dot_general(
        tokens, w_all[...].reshape(group * f, d), (((1,), (1,)), ((), ())), preferred_element_type=F32
    )
    eye = iota((toks, toks), 0) == iota((toks, toks), 1)
    slots = iota((CAP, toks), 0).astype(F32)
    for e in range(group):
        for k in range(n):
            s = lax.rem(sc_ref[0] + n - k, n)
            w_row, r_row = wt_ref[k, e], rank_ref[k, e]
            here = (slots == r_row) & (w_row > 0)
            pick = jnp.where(here, 1.0, 0.0).astype(BF)
            weigh = jnp.where(here, w_row, 0.0).astype(BF)
            zk = z[k * toks : (k + 1) * toks, e * f : (e + 1) * f]
            gh_ref[e, s] = jnp.dot(weigh, zk.astype(BF), preferred_element_type=F32).astype(BF)
            hid = lax.dot_general(
                pick, hid_ref[0, e, s, :CAP], (((0,), (0,)), ((), ())), preferred_element_type=F32
            )
            sg_col = jnp.sum(zk * hid, axis=1, keepdims=True)
            sg_row = jnp.sum(jnp.where(eye, sg_col, 0.0), axis=0, keepdims=True)
            sg_ref[s, e] = sg_row + added[0][s, e] if added else sg_row


def backward(n, scalars, pieces, w_pieces, f, hid, wt, rank, *added):
    _, experts, band, d = w_pieces[0][1].shape
    toks = wt.shape[3]
    rels = [rel for rel, _, _ in w_pieces]
    group = 2 if experts % 2 == 0 else 1
    arrays, specs, counts = flat(pieces)
    whole = len(added) > 0
    row_spec = pl.BlockSpec((n, group, 1, toks), lambda e, sc: (0, e, 0, 0))
    return pl.pallas_call(
        functools.partial(back_kernel, n, counts, group, rels),
        out_shape=(
            jax.ShapeDtypeStruct((experts, n, CAP, 2 * f if whole else f), BF),
            jax.ShapeDtypeStruct((n, experts, 1, toks), F32),
        ),
        grid_spec=pltpu.PrefetchScalarGridSpec(
            num_scalar_prefetch=1,
            grid=(experts // group,),
            in_specs=specs
            + [
                pl.BlockSpec((1, group, band, d), functools.partial(lambda i, e, sc: (i, e, 0, 0), i))
                for _, _, i in w_pieces
            ]
            + [
                pl.BlockSpec((1, group, n, hid.shape[3], f), lambda e, sc: (0, e, 0, 0, sc[1] if whole else 0)),
                row_spec,
                row_spec,
                *[row_spec] * len(added),
            ],
            out_specs=(pl.BlockSpec((group, n, CAP, f), lambda e, sc: (e, 0, 0, sc[1] if whole else 0)), row_spec),
            scratch_shapes=[pltpu.VMEM((group, f, d), BF)],
        ),
        compiler_params=pltpu.CompilerParams(vmem_limit_bytes=24 << 20),
        cost_estimate=SHORT,
    )(scalars, *arrays, *[w for _, w, _ in w_pieces], hid, wt, rank, *added)


def part_kernel(n, bands, counts, spans, sc_ref, *refs):
    own, at_own = gathered(refs, counts[0], n, sc_ref[0], spans)
    nb, at_nb = gathered(refs[at_own:], counts[1], n, sc_ref[0], spans)
    own_ref, nb_ref, *send_refs, keep_ref = refs[at_own + at_nb :]
    tokens = jnp.concatenate(
        [jnp.concatenate(c, axis=1) if len(c) > 1 else c[0] for c in (own, nb)], axis=0
    )
    hidden = jnp.concatenate([own_ref[0], nb_ref[0]], axis=1)
    total = jnp.dot(hidden, tokens, preferred_element_type=F32)
    quarter, _, band, cols = keep_ref.shape
    total = total.reshape(bands // 2, band, cols).astype(BF)
    for a in range(bands // 2):
        rel = (sc_ref[2] % (bands // 2)) ^ a
        at = rel // 2

        @pl.when(rel % 2 == 1)
        def _():
            done = 0
            for ref in send_refs:
                width = ref.shape[3]
                ref[at, 0] = total[a, :, done : done + width]
                done += width

        @pl.when(rel % 2 == 0)
        def _():
            keep_ref[at, 0] = total[a]


def partial_grad(n, bands, band, far, parts, scalars, own, nb, pieces_own, pieces_nb, spans):
    experts, f, k = own.shape
    arrays, specs, counts = flat(pieces_own)
    arrays_nb, specs_nb, counts_nb = flat(pieces_nb)
    cols = sum(stop - start for start, stop in spans)
    widths = (*parts, cols)
    half = bands // 2
    hs_spec = pl.BlockSpec((1, f // 2, k), lambda e, sc: (e, (sc[2] // half) ^ int(far), 0))
    return pl.pallas_call(
        functools.partial(part_kernel, n, bands, (counts, counts_nb), spans),
        out_shape=[jax.ShapeDtypeStruct((bands // 4, experts, band, width), BF) for width in widths],
        grid_spec=pltpu.PrefetchScalarGridSpec(
            num_scalar_prefetch=1,
            grid=(experts,),
            in_specs=specs + specs_nb + [hs_spec, hs_spec],
            out_specs=[pl.BlockSpec((bands // 4, 1, band, width), lambda e, sc: (0, e, 0, 0)) for width in widths],
        ),
        compiler_params=pltpu.CompilerParams(vmem_limit_bytes=20 << 20),
        cost_estimate=SHORT,
    )(scalars, *arrays, *arrays_nb, own, nb)


def joined_kernel(groups, *refs):
    total, at = None, 0
    for count in groups:
        parts = [ref[...].astype(F32) for ref in refs[at : at + count]]
        term = parts[0] if count == 1 else jnp.concatenate(parts, axis=3)
        total = term if total is None else total + term
        at += count
    refs[-1][...] = total.astype(BF)


def joined(terms):
    arrays = [part for term in terms for part in term]
    lead, experts, band, _ = arrays[0].shape
    d = sum(part.shape[3] for part in terms[0])
    block = lambda x: pl.BlockSpec((x.shape[0], 1, *x.shape[2:]), lambda e: (0, e, 0, 0))
    out, spec = (lead, experts, band, d), pl.BlockSpec((lead, 1, band, d), lambda e: (0, e, 0, 0))
    return pl.pallas_call(
        functools.partial(joined_kernel, [len(term) for term in terms]),
        out_shape=jax.ShapeDtypeStruct(out, BF),
        grid=(experts,),
        in_specs=[block(x) for x in arrays],
        out_specs=spec,
        compiler_params=pltpu.CompilerParams(vmem_limit_bytes=8 << 20),
        cost_estimate=SHORT,
    )(*arrays)


def finish_kernel(sc_ref, base_ref, *refs):
    *there, new_ref, _, down_ref, hidden_ref = refs
    others = [ref[0, 0].astype(F32) for ref in there]
    others = others[0] if len(others) == 1 else jnp.concatenate(others, axis=1)
    down_ref[0] = (base_ref[0, 0].astype(F32) + others).astype(BF)
    hidden_ref[...] = new_ref[...]


def finish(scalars, base, there, new, whole):
    _, experts, band, d = base.shape
    _, n, cap, f = new.shape
    sums = lambda x: pl.BlockSpec((1, 1, band, x.shape[3]), lambda e, sc: (0, e, 0, 0))
    return pl.pallas_call(
        finish_kernel,
        out_shape=(jax.ShapeDtypeStruct((experts, band, d), BF), jax.ShapeDtypeStruct(whole.shape, BF)),
        grid_spec=pltpu.PrefetchScalarGridSpec(
            num_scalar_prefetch=1,
            grid=(experts,),
            in_specs=[
                *[sums(x) for x in (base, *there)],
                pl.BlockSpec((1, n, cap, f), lambda e, sc: (e, 0, 0, 0)),
                pl.BlockSpec(memory_space=pl.ANY),
            ],
            out_specs=(
                pl.BlockSpec((1, band, d), lambda e, sc: (e, 0, 0)),
                pl.BlockSpec((1, n, cap, f), lambda e, sc: (e, 0, 0, 1 - sc[1])),
            ),
        ),
        input_output_aliases={3 + len(there): 1},
        compiler_params=pltpu.CompilerParams(vmem_limit_bytes=12 << 20),
        cost_estimate=SHORT,
    )(scalars, base, *there, new, whole)


def per_device(n_dp, n, grad_out, expert_ids, route_weights, hidden_cache, w_down):
    dp, z = lax.axis_index("dp"), lax.axis_index("expert")
    bands = n_dp // 2
    upper, j = dp // bands, dp % bands
    experts, band, d = w_down.shape
    toks = grad_out.shape[0]
    f = bands * band

    def swap(x, bit):
        return lax.ppermute(x, "dp", [(i, i ^ bit) for i in range(n_dp)])

    def spread(x):
        if n != 4:
            return [x] + [
                lax.ppermute(x, "expert", [(i, (i + k) % n) for i in range(n)]) for k in range(1, n)
            ]
        two = lax.ppermute(x, "expert", [(i, (i + 2) % n) for i in range(n)])
        one = lax.ppermute(x, "expert", [(i, i + 1) for i in range(n - 1)])
        three = lax.ppermute(x, "expert", [(i + 1, i) for i in range(n - 1)])
        passed = lax.ppermute(two, "expert", [(2, 3), (1, 0)])
        return [x, one, two, three, passed]

    ids = expert_ids[None] == jnp.arange(EXPERTS, dtype=jnp.int32)[:, None, None]
    table = jnp.sum(jnp.where(ids, route_weights.astype(F32)[None], 0.0), axis=2).astype(BF)

    cut = 11 * d // 16
    table = jnp.concatenate([table[: EXPERTS // 2], table[EXPERTS // 2 :]], axis=1)
    table = jnp.pad(table, ((0, 0), (0, cut - 2 * toks)))
    blocks = spread(jnp.concatenate([grad_out[:, :cut], table], axis=0))
    w_core = swap(w_down[None], 1)
    scalars = jnp.stack([z, upper, j]).astype(jnp.int32)
    lefts = [min(left, d - f) for left in range(0, d, f)]
    outgoing = pack(scalars, hidden_cache, grad_out, lefts, f)
    incoming = swap(after(outgoing, w_core), bands)
    count = experts * n * PADDED
    hid_nb = incoming[:count].reshape(1, experts, n, PADDED, f)
    first_nb = jnp.concatenate(
        [incoming[count + i * toks : count + (i + 1) * toks, i * f - left :] for i, left in enumerate(lefts)], axis=1
    )
    first_nb, pair = first_nb[:, :cut], first_nb[:, cut:]
    w_pieces = [(0, w_down[None], 0), (1, w_core, 0)]
    bit = 2
    while bit < bands:
        far = swap(w_down[None] if bit == 2 else jnp.concatenate([a for _, a, _ in w_pieces[::2]]), bit)
        there = swap(far, 1)
        for i in range(far.shape[0]):
            w_pieces += [(w_pieces[2 * i][0] ^ bit, far, i), (w_pieces[2 * i][0] ^ bit ^ 1, there, i)]
        bit *= 2

    mine = below(n, experts, scalars, blocks)
    hs_own, wt_own, rank_own = hidden_to_tokens(n, experts, toks, scalars, mine, hidden_cache, f, True)
    rest = jnp.concatenate([grad_out[:, cut:], pair], axis=0)
    rests = spread(after(rest, *blocks))
    nb_a = swap(after(mine, incoming), bands)
    hs_nb, wt_nb, rank_nb = hidden_to_tokens(n, experts, toks, scalars, nb_a, hid_nb, f, False)

    own_pieces = [[(blocks[0], (toks, cut), (0, 0)), (mine, ((n - 1) * toks, cut), (0, 0))], [(b, (toks, d - cut), (0, 0)) for b in rests]]
    nb_pieces = [[(first_nb, (toks, cut), (0, 0)), (nb_a, ((n - 1) * toks, cut), (0, 0))], [(b, (toks, d - cut), (1, 0)) for b in rests]]

    if band % 16:
        w = jnp.zeros((experts, f, d), BF)
        for r, array, i in w_pieces:
            w = lax.dynamic_update_slice(w, array[i], (0, (j ^ r) * band, 0))
        w_pieces = [(None, w[None], 0)]

    half, first = d // 2, 7 * d // 16
    groups = (
        (slice(0, 1), ((0, first),), 1),
        (slice(0, 2), ((first, cut), (0, d - cut)), 1),
    )
    order, sums = scalars, []
    for chunks, spans, parts in groups:
        tokens = own_pieces[chunks], nb_pieces[chunks], spans
        width = sum(stop - start for start, stop in spans) // parts
        *far, keep_far = partial_grad(n, bands, band, True, (width,) * parts, order, hs_own, hs_nb, *tokens)
        order = after(scalars, far[0])
        here = [swap(after(x, *rests) if not sums else x, 1) for x in far]
        sums.append(joined([[keep_far], here]))
    there = [swap(x, bands // 2) for x in sums]
    gh_nb, sg_nb = backward(
        n, after(order, sums[0]), nb_pieces, w_pieces, f, hid_nb, wt_nb, rank_nb
    )
    sg_in = swap(sg_nb, bands)
    gh_own, sg_own = backward(
        n, after(scalars, sg_in), own_pieces, w_pieces, f, hidden_cache, wt_own, rank_own, sg_in
    )
    by_expert = lax.all_to_all(sg_own, "expert", split_axis=0, concat_axis=0, tiled=True)
    spans = ((0, cut), (0, d - cut))
    *near, keep = partial_grad(
        n, bands, band, False, (half, half), after(scalars, sg_own), hs_own, hs_nb, own_pieces, nb_pieces, spans
    )
    base = joined([[keep], [swap(after(x, there[0]), 1) for x in near]])
    mid = bands // 8
    there = there if mid == 0 else [jnp.concatenate(there, axis=3)]
    while mid:
        total = base.astype(F32) + there[0].astype(F32)
        base, there, mid = total[:mid].astype(BF), [swap(total[mid:].astype(BF), 4 * mid)], mid // 2
    gh_in = swap(after(gh_nb, sg_in), bands)
    grad_down, grad_hidden = finish(scalars, base, there, gh_in, gh_own)
    by_expert = by_expert.reshape(EXPERTS, 1, toks)
    chosen = expert_ids.T[None] == jnp.arange(EXPERTS, dtype=jnp.int32)[:, None, None]
    grad_probs = jnp.sum(jnp.where(chosen, by_expert, 0.0), axis=0).T
    return grad_hidden[None], grad_down, grad_probs


def solution(mesh):
    tokens = P(("dp", "expert"), None)
    cache = P("dp", "expert", None, None, None)
    weights = P("expert", "dp", None)
    return jax.shard_map(
        functools.partial(per_device, mesh.shape["dp"], mesh.shape["expert"]),
        mesh=mesh,
        in_specs=(tokens, tokens, tokens, cache, weights),
        out_specs=(cache, weights, tokens),
        check_vma=False,
    )
```

```python
import functools

import jax
import jax.numpy as jnp
from jax import lax
from jax.experimental import pallas as pl
from jax.experimental.pallas import tpu as pltpu
from jax.sharding import PartitionSpec as P

EXPERTS = 16
CAP = 72
PADDED = 80
BF = jnp.bfloat16
F32 = jnp.float32
SHORT = pl.CostEstimate(flops=1, bytes_accessed=1, transcendentals=0)


def iota(shape, dim):
    return lax.broadcasted_iota(jnp.int32, shape, dim)


def after(x, *others):
    return lax.optimization_barrier((x, *others))[0]


def hidden_kernel(n, experts, sc_ref, tab_ref, hid_ref, hst_ref, wt_ref, rank_ref):
    toks = tab_ref.shape[1]
    earlier = (iota((toks, toks), 0) < iota((toks, toks), 1)).astype(BF)
    slots = iota((CAP, toks), 0).astype(F32)
    table = tab_ref[...].astype(F32)
    rank = jnp.dot((table > 0).astype(F32).astype(BF), earlier, preferred_element_type=F32)
    for k in range(n):
        s = lax.rem(sc_ref[0] + n - k, n)
        for e in range(experts):
            at = k * experts + e
            w_row, r_row = table[at : at + 1], rank[at : at + 1]
            place = jnp.where(slots == r_row, w_row, 0.0).astype(BF)
            moved = lax.dot_general(
                hid_ref[0, e, s][:CAP], place, (((0,), (0,)), ((), ())), preferred_element_type=F32
            )
            hst_ref[e, :, k * toks : (k + 1) * toks] = moved.astype(BF)
            wt_ref[k, e] = w_row
            rank_ref[k, e] = r_row


def hidden_to_tokens(n, experts, toks, scalars, tokens, hid, f, whole):
    row = jax.ShapeDtypeStruct((n, experts, 1, toks), F32)
    row_spec = pl.BlockSpec((n, experts, 1, toks), lambda i, sc: (0, 0, 0, 0))
    lines = n * experts
    return pl.pallas_call(
        functools.partial(hidden_kernel, n, experts),
        out_shape=(jax.ShapeDtypeStruct((experts, f, n * toks), BF), row, row),
        grid_spec=pltpu.PrefetchScalarGridSpec(
            num_scalar_prefetch=1,
            grid=(1,),
            in_specs=[
                pl.BlockSpec((lines, toks), lambda i, sc: ((n - 1) * toks // lines, 0)),
                pl.BlockSpec((1, experts, n, hid.shape[3], f), lambda i, sc: (0, 0, 0, 0, sc[1] if whole else 0)),
            ],
            out_specs=(
                pl.BlockSpec((experts, f, n * toks), lambda i, sc: (0, 0, 0)),
                row_spec,
                row_spec,
            ),
        ),
        compiler_params=pltpu.CompilerParams(vmem_limit_bytes=12 << 20),
        cost_estimate=SHORT,
    )(scalars, tokens, hid)


def pack_kernel(lefts, sc_ref, hid_ref, tok_ref, out_ref):
    _, experts, n, cap, f = hid_ref.shape
    toks = tok_ref.shape[0]
    blank = jnp.zeros((PADDED - cap, f), BF)
    for e in range(experts):
        for s in range(n):
            at = (e * n + s) * PADDED
            out_ref[at : at + PADDED] = jnp.concatenate([hid_ref[0, e, s], blank], axis=0)
    for i, left in enumerate(lefts):
        at = experts * n * PADDED + i * toks
        out_ref[at : at + toks] = tok_ref[:, left : left + f]


def pack(scalars, hid, tok, lefts, f):
    _, experts, n, cap, _ = hid.shape
    rows = experts * n * PADDED + len(lefts) * tok.shape[0]
    return pl.pallas_call(
        functools.partial(pack_kernel, lefts),
        out_shape=jax.ShapeDtypeStruct((rows, f), BF),
        grid_spec=pltpu.PrefetchScalarGridSpec(
            num_scalar_prefetch=1,
            grid=(1,),
            in_specs=[
                pl.BlockSpec((1, experts, n, cap, f), lambda i, sc: (0, 0, 0, 0, 1 - sc[1])),
                pl.BlockSpec(tok.shape, lambda i, sc: (0, 0)),
            ],
            out_specs=pl.BlockSpec((rows, f), lambda i, sc: (0, 0)),
        ),
        compiler_params=pltpu.CompilerParams(vmem_limit_bytes=12 << 20),
        cost_estimate=SHORT,
    )(scalars, hid, tok)


def below_kernel(n, experts, sc_ref, *refs):
    *blocks, out_ref = refs
    z = sc_ref[0]
    toks = blocks[0].shape[0] - EXPERTS // 2
    line = iota((EXPERTS, toks), 0)

    def local(ref):
        table = ref[toks:, : 2 * toks].astype(F32)
        table = jnp.concatenate([table[:, :toks], table[:, toks:]], axis=0)
        return [
            jnp.sum(jnp.where(line == z * experts + e, table, 0.0), axis=0, keepdims=True)
            for e in range(experts)
        ]

    tables = [local(blocks[k]) for k in range(n)]
    for k in range(1, n):
        out_ref[(k - 1) * toks : k * toks] = blocks[k][:toks]
    if len(blocks) > n:
        passed = blocks[n]
        rows = local(passed)
        for k, place in ((1, 0), (n - 1, n - 1)):
            tables[k] = [jnp.where(z == place, new, old) for new, old in zip(rows, tables[k])]

            @pl.when(z == place)
            def _():
                out_ref[(k - 1) * toks : k * toks] = passed[:toks]

    rows = [row for table in tables for row in table]
    out_ref[(n - 1) * toks :, :toks] = jnp.concatenate(rows, axis=0).astype(BF)


def below(n, experts, scalars, blocks):
    rows, cols = blocks[0].shape
    toks = rows - EXPERTS // 2
    height = (n - 1) * toks + n * experts
    return pl.pallas_call(
        functools.partial(below_kernel, n, experts),
        out_shape=jax.ShapeDtypeStruct((height, cols), BF),
        grid_spec=pltpu.PrefetchScalarGridSpec(
            num_scalar_prefetch=1,
            grid=(1,),
            in_specs=[pl.BlockSpec((rows, cols), lambda i, sc: (0, 0))] * len(blocks),
            out_specs=pl.BlockSpec((height, cols), lambda i, sc: (0, 0)),
        ),
        compiler_params=pltpu.CompilerParams(vmem_limit_bytes=24 << 20),
        cost_estimate=SHORT,
    )(scalars, *blocks)


def flat(pieces):
    arrays = [a for chunk in pieces for a, _, _ in chunk]
    specs = [
        pl.BlockSpec(shape, functools.partial(lambda at, i, sc: at, at))
        for chunk in pieces
        for _, shape, at in chunk
    ]
    return arrays, specs, [len(chunk) for chunk in pieces]


def gathered(refs, counts, n, z, spans=None):
    chunks, at = [], 0
    for i, count in enumerate(counts):
        cols = slice(*spans[i]) if spans else slice(None)
        pieces = [refs[at + k][:, cols] for k in range(count)]
        if count > n:
            passed = pieces.pop()
            for k, place in ((1, 0), (n - 1, n - 1)):
                pieces[k] = jnp.where(z == place, passed, pieces[k])
        chunks.append(pieces[0] if len(pieces) == 1 else jnp.concatenate(pieces, axis=0))
        at += count
    return chunks, at


def back_kernel(n, counts, group, rels, sc_ref, *refs):
    chunks, at = gathered(refs, counts, n, sc_ref[0])
    w_refs, refs = refs[at : at + len(rels)], refs[at + len(rels) :]
    hid_ref, wt_ref, rank_ref, *added, gh_ref, sg_ref, w_all = refs
    toks, (f, d) = wt_ref.shape[3], w_all.shape[1:]
    for rel, ref in zip(rels, w_refs):
        rows = ref.shape[2]
        start = 0 if rel is None else pl.multiple_of((sc_ref[2] ^ rel) * rows, rows)
        for e in range(group):
            w_all[e, pl.ds(start, rows), :] = ref[0, e]
    tokens = chunks[0] if len(chunks) == 1 else jnp.concatenate(chunks, axis=1)
    z = lax.dot_general(
        tokens, w_all[...].reshape(group * f, d), (((1,), (1,)), ((), ())), preferred_element_type=F32
    )
    eye = iota((toks, toks), 0) == iota((toks, toks), 1)
    slots = iota((CAP, toks), 0).astype(F32)
    for e in range(group):
        for k in range(n):
            s = lax.rem(sc_ref[0] + n - k, n)
            w_row, r_row = wt_ref[k, e], rank_ref[k, e]
            here = (slots == r_row) & (w_row > 0)
            pick = jnp.where(here, 1.0, 0.0).astype(BF)
            weigh = jnp.where(here, w_row, 0.0).astype(BF)
            zk = z[k * toks : (k + 1) * toks, e * f : (e + 1) * f]
            gh_ref[e, s] = jnp.dot(weigh, zk.astype(BF), preferred_element_type=F32).astype(BF)
            hid = lax.dot_general(
                pick, hid_ref[0, e, s][:CAP], (((0,), (0,)), ((), ())), preferred_element_type=F32
            )
            sg_col = jnp.sum(zk * hid, axis=1, keepdims=True)
            sg_row = jnp.sum(jnp.where(eye, sg_col, 0.0), axis=0, keepdims=True)
            sg_ref[s, e] = sg_row + added[0][s, e] if added else sg_row


def backward(n, scalars, pieces, w_pieces, f, hid, wt, rank, *added):
    _, experts, band, d = w_pieces[0][1].shape
    toks = wt.shape[3]
    rels = [rel for rel, _, _ in w_pieces]
    group = 2 if experts % 2 == 0 else 1
    arrays, specs, counts = flat(pieces)
    whole = len(added) > 0
    row_spec = pl.BlockSpec((n, group, 1, toks), lambda e, sc: (0, e, 0, 0))
    return pl.pallas_call(
        functools.partial(back_kernel, n, counts, group, rels),
        out_shape=(
            jax.ShapeDtypeStruct((experts, n, CAP, 2 * f if whole else f), BF),
            jax.ShapeDtypeStruct((n, experts, 1, toks), F32),
        ),
        grid_spec=pltpu.PrefetchScalarGridSpec(
            num_scalar_prefetch=1,
            grid=(experts // group,),
            in_specs=specs
            + [
                pl.BlockSpec((1, group, band, d), functools.partial(lambda i, e, sc: (i, e, 0, 0), i))
                for _, _, i in w_pieces
            ]
            + [
                pl.BlockSpec((1, group, n, hid.shape[3], f), lambda e, sc: (0, e, 0, 0, sc[1] if whole else 0)),
                row_spec,
                row_spec,
                *[row_spec] * len(added),
            ],
            out_specs=(pl.BlockSpec((group, n, CAP, f), lambda e, sc: (e, 0, 0, sc[1] if whole else 0)), row_spec),
            scratch_shapes=[pltpu.VMEM((group, f, d), BF)],
        ),
        compiler_params=pltpu.CompilerParams(vmem_limit_bytes=24 << 20),
        cost_estimate=SHORT,
    )(scalars, *arrays, *[w for _, w, _ in w_pieces], hid, wt, rank, *added)


def part_kernel(n, bands, counts, spans, sc_ref, *refs):
    own, at_own = gathered(refs, counts[0], n, sc_ref[0], spans)
    nb, at_nb = gathered(refs[at_own:], counts[1], n, sc_ref[0], spans)
    own_ref, nb_ref, *send_refs, keep_ref = refs[at_own + at_nb :]
    tokens = jnp.concatenate(
        [jnp.concatenate(c, axis=1) if len(c) > 1 else c[0] for c in (own, nb)], axis=0
    )
    hidden = jnp.concatenate([own_ref[0], nb_ref[0]], axis=1)
    total = jnp.dot(hidden, tokens, preferred_element_type=F32)
    quarter, _, band, cols = keep_ref.shape
    total = total.reshape(bands // 2, band, cols).astype(BF)
    for a in range(bands // 2):
        rel = (sc_ref[2] % (bands // 2)) ^ a
        at = rel // 2

        @pl.when(rel % 2 == 1)
        def _():
            done = 0
            for ref in send_refs:
                width = ref.shape[3]
                ref[at, 0] = total[a, :, done : done + width]
                done += width

        @pl.when(rel % 2 == 0)
        def _():
            keep_ref[at, 0] = total[a]


def partial_grad(n, bands, band, far, parts, scalars, own, nb, pieces_own, pieces_nb, spans):
    experts, f, k = own.shape
    arrays, specs, counts = flat(pieces_own)
    arrays_nb, specs_nb, counts_nb = flat(pieces_nb)
    cols = sum(stop - start for start, stop in spans)
    widths = (*parts, cols)
    half = bands // 2
    hs_spec = pl.BlockSpec((1, f // 2, k), lambda e, sc: (e, (sc[2] // half) ^ int(far), 0))
    return pl.pallas_call(
        functools.partial(part_kernel, n, bands, (counts, counts_nb), spans),
        out_shape=[jax.ShapeDtypeStruct((bands // 4, experts, band, width), BF) for width in widths],
        grid_spec=pltpu.PrefetchScalarGridSpec(
            num_scalar_prefetch=1,
            grid=(experts,),
            in_specs=specs + specs_nb + [hs_spec, hs_spec],
            out_specs=[pl.BlockSpec((bands // 4, 1, band, width), lambda e, sc: (0, e, 0, 0)) for width in widths],
        ),
        compiler_params=pltpu.CompilerParams(vmem_limit_bytes=20 << 20),
        cost_estimate=SHORT,
    )(scalars, *arrays, *arrays_nb, own, nb)


def joined_kernel(groups, *refs):
    total, at = None, 0
    for count in groups:
        parts = [ref[...].astype(F32) for ref in refs[at : at + count]]
        term = parts[0] if count == 1 else jnp.concatenate(parts, axis=3)
        total = term if total is None else total + term
        at += count
    refs[-1][...] = total.astype(BF)


def joined(terms):
    arrays = [part for term in terms for part in term]
    lead, experts, band, _ = arrays[0].shape
    d = sum(part.shape[3] for part in terms[0])
    block = lambda x: pl.BlockSpec((x.shape[0], 1, *x.shape[2:]), lambda e: (0, e, 0, 0))
    out, spec = (lead, experts, band, d), pl.BlockSpec((lead, 1, band, d), lambda e: (0, e, 0, 0))
    return pl.pallas_call(
        functools.partial(joined_kernel, [len(term) for term in terms]),
        out_shape=jax.ShapeDtypeStruct(out, BF),
        grid=(experts,),
        in_specs=[block(x) for x in arrays],
        out_specs=spec,
        compiler_params=pltpu.CompilerParams(vmem_limit_bytes=8 << 20),
        cost_estimate=SHORT,
    )(*arrays)


def finish_kernel(sc_ref, base_ref, *refs):
    *there, new_ref, _, down_ref, hidden_ref = refs
    others = [ref[0, 0].astype(F32) for ref in there]
    others = others[0] if len(others) == 1 else jnp.concatenate(others, axis=1)
    down_ref[0] = (base_ref[0, 0].astype(F32) + others).astype(BF)
    hidden_ref[...] = new_ref[...]


def finish(scalars, base, there, new, whole):
    _, experts, band, d = base.shape
    _, n, cap, f = new.shape
    sums = lambda x: pl.BlockSpec((1, 1, band, x.shape[3]), lambda e, sc: (0, e, 0, 0))
    return pl.pallas_call(
        finish_kernel,
        out_shape=(jax.ShapeDtypeStruct((experts, band, d), BF), jax.ShapeDtypeStruct(whole.shape, BF)),
        grid_spec=pltpu.PrefetchScalarGridSpec(
            num_scalar_prefetch=1,
            grid=(experts,),
            in_specs=[
                *[sums(x) for x in (base, *there)],
                pl.BlockSpec((1, n, cap, f), lambda e, sc: (e, 0, 0, 0)),
                pl.BlockSpec(memory_space=pl.ANY),
            ],
            out_specs=(
                pl.BlockSpec((1, band, d), lambda e, sc: (e, 0, 0)),
                pl.BlockSpec((1, n, cap, f), lambda e, sc: (e, 0, 0, 1 - sc[1])),
            ),
        ),
        input_output_aliases={3 + len(there): 1},
        compiler_params=pltpu.CompilerParams(vmem_limit_bytes=12 << 20),
        cost_estimate=SHORT,
    )(scalars, base, *there, new, whole)


def per_device(n_dp, n, grad_out, expert_ids, route_weights, hidden_cache, w_down):
    dp, z = lax.axis_index("dp"), lax.axis_index("expert")
    bands = n_dp // 2
    upper, j = dp // bands, dp % bands
    experts, band, d = w_down.shape
    toks = grad_out.shape[0]
    f = bands * band

    def swap(x, bit):
        return lax.ppermute(x, "dp", [(i, i ^ bit) for i in range(n_dp)])

    def spread(x):
        if n != 4:
            return [x] + [
                lax.ppermute(x, "expert", [(i, (i + k) % n) for i in range(n)]) for k in range(1, n)
            ]
        two = lax.ppermute(x, "expert", [(i, (i + 2) % n) for i in range(n)])
        one = lax.ppermute(x, "expert", [(i, i + 1) for i in range(n - 1)])
        three = lax.ppermute(x, "expert", [(i + 1, i) for i in range(n - 1)])
        passed = lax.ppermute(two, "expert", [(2, 3), (1, 0)])
        return [x, one, two, three, passed]

    ids = expert_ids[None] == jnp.arange(EXPERTS, dtype=jnp.int32)[:, None, None]
    table = jnp.sum(jnp.where(ids, route_weights.astype(F32)[None], 0.0), axis=2).astype(BF)

    cut = 11 * d // 16
    table = jnp.concatenate([table[: EXPERTS // 2], table[EXPERTS // 2 :]], axis=1)
    table = jnp.pad(table, ((0, 0), (0, cut - 2 * toks)))
    blocks = spread(jnp.concatenate([grad_out[:, :cut], table], axis=0))
    w_core = swap(w_down[None], 1)
    scalars = jnp.stack([z, upper, j]).astype(jnp.int32)
    lefts = [min(left, d - f) for left in range(0, d, f)]
    outgoing = pack(scalars, hidden_cache, grad_out, lefts, f)
    incoming = swap(after(outgoing, w_core), bands)
    count = experts * n * PADDED
    hid_nb = incoming[:count].reshape(1, experts, n, PADDED, f)
    first_nb = jnp.concatenate(
        [incoming[count + i * toks : count + (i + 1) * toks, i * f - left :] for i, left in enumerate(lefts)], axis=1
    )
    first_nb, pair = first_nb[:, :cut], first_nb[:, cut:]
    w_pieces = [(0, w_down[None], 0), (1, w_core, 0)]
    bit = 2
    while bit < bands:
        far = swap(w_down[None] if bit == 2 else jnp.concatenate([a for _, a, _ in w_pieces[::2]]), bit)
        there = swap(far, 1)
        for i in range(far.shape[0]):
            w_pieces += [(w_pieces[2 * i][0] ^ bit, far, i), (w_pieces[2 * i][0] ^ bit ^ 1, there, i)]
        bit *= 2

    mine = below(n, experts, scalars, blocks)
    hs_own, wt_own, rank_own = hidden_to_tokens(n, experts, toks, scalars, mine, hidden_cache, f, True)
    rest = jnp.concatenate([grad_out[:, cut:], pair], axis=0)
    rests = spread(after(rest, *blocks))
    nb_a = swap(after(mine, incoming), bands)
    hs_nb, wt_nb, rank_nb = hidden_to_tokens(n, experts, toks, scalars, nb_a, hid_nb, f, False)

    own_pieces = [[(blocks[0], (toks, cut), (0, 0)), (mine, ((n - 1) * toks, cut), (0, 0))], [(b, (toks, d - cut), (0, 0)) for b in rests]]
    nb_pieces = [[(first_nb, (toks, cut), (0, 0)), (nb_a, ((n - 1) * toks, cut), (0, 0))], [(b, (toks, d - cut), (1, 0)) for b in rests]]

    if band % 16:
        w = jnp.zeros((experts, f, d), BF)
        for r, array, i in w_pieces:
            w = lax.dynamic_update_slice(w, array[i], (0, (j ^ r) * band, 0))
        w_pieces = [(None, w[None], 0)]

    half, first = d // 2, 7 * d // 16
    groups = (
        (slice(0, 1), ((0, first),), 1),
        (slice(0, 2), ((first, cut), (0, d - cut)), 1),
    )
    order, sums = scalars, []
    for chunks, spans, parts in groups:
        tokens = own_pieces[chunks], nb_pieces[chunks], spans
        width = sum(stop - start for start, stop in spans) // parts
        *far, keep_far = partial_grad(n, bands, band, True, (width,) * parts, order, hs_own, hs_nb, *tokens)
        order = after(scalars, far[0])
        here = [swap(after(x, *rests) if not sums else x, 1) for x in far]
        sums.append(joined([[keep_far], here]))
    there = [swap(x, bands // 2) for x in sums]
    gh_nb, sg_nb = backward(
        n, after(order, sums[0]), nb_pieces, w_pieces, f, hid_nb, wt_nb, rank_nb
    )
    sg_in = swap(sg_nb, bands)
    gh_own, sg_own = backward(
        n, after(scalars, sg_in), own_pieces, w_pieces, f, hidden_cache, wt_own, rank_own, sg_in
    )
    by_expert = lax.all_to_all(sg_own, "expert", split_axis=0, concat_axis=0, tiled=True)
    spans = ((0, cut), (0, d - cut))
    *near, keep = partial_grad(
        n, bands, band, False, (half, half), after(scalars, sg_own), hs_own, hs_nb, own_pieces, nb_pieces, spans
    )
    base = joined([[keep], [swap(after(x, there[0]), 1) for x in near]])
    mid = bands // 8
    there = there if mid == 0 else [jnp.concatenate(there, axis=3)]
    while mid:
        total = base.astype(F32) + there[0].astype(F32)
        base, there, mid = total[:mid].astype(BF), [swap(total[mid:].astype(BF), 4 * mid)], mid // 2
    gh_in = swap(after(gh_nb, sg_in, sums[1]), bands)
    grad_down, grad_hidden = finish(scalars, base, there, gh_in, gh_own)
    by_expert = by_expert.reshape(EXPERTS, 1, toks)
    chosen = expert_ids.T[None] == jnp.arange(EXPERTS, dtype=jnp.int32)[:, None, None]
    grad_probs = jnp.sum(jnp.where(chosen, by_expert, 0.0), axis=0).T
    return grad_hidden[None], grad_down, grad_probs


def solution(mesh):
    tokens = P(("dp", "expert"), None)
    cache = P("dp", "expert", None, None, None)
    weights = P("expert", "dp", None)
    return jax.shard_map(
        functools.partial(per_device, mesh.shape["dp"], mesh.shape["expert"]),
        mesh=mesh,
        in_specs=(tokens, tokens, tokens, cache, weights),
        out_specs=(cache, weights, tokens),
        check_vma=False,
    )
```

```python
import functools

import jax
import jax.numpy as jnp
from jax import lax
from jax.experimental import pallas as pl
from jax.experimental.pallas import tpu as pltpu
from jax.sharding import PartitionSpec as P

EXPERTS = 16
CAP = 72
PADDED = 80
BF = jnp.bfloat16
F32 = jnp.float32
SHORT = pl.CostEstimate(flops=1, bytes_accessed=1, transcendentals=0)


def iota(shape, dim):
    return lax.broadcasted_iota(jnp.int32, shape, dim)


def after(x, *others):
    return lax.optimization_barrier((x, *others))[0]


def hidden_kernel(n, experts, sc_ref, tab_ref, hid_ref, hst_ref, wt_ref, rank_ref):
    toks = tab_ref.shape[1]
    earlier = (iota((toks, toks), 0) < iota((toks, toks), 1)).astype(BF)
    slots = iota((CAP, toks), 0).astype(F32)
    table = tab_ref[...].astype(F32)
    rank = jnp.dot((table > 0).astype(F32).astype(BF), earlier, preferred_element_type=F32)
    for k in range(n):
        s = lax.rem(sc_ref[0] + n - k, n)
        for e in range(experts):
            at = k * experts + e
            w_row, r_row = table[at : at + 1], rank[at : at + 1]
            place = jnp.where(slots == r_row, w_row, 0.0).astype(BF)
            moved = lax.dot_general(
                hid_ref[0, e, s][:CAP], place, (((0,), (0,)), ((), ())), preferred_element_type=F32
            )
            hst_ref[e, :, k * toks : (k + 1) * toks] = moved.astype(BF)
            wt_ref[k, e] = w_row
            rank_ref[k, e] = r_row


def hidden_to_tokens(n, experts, toks, scalars, tokens, hid, f, whole):
    row = jax.ShapeDtypeStruct((n, experts, 1, toks), F32)
    row_spec = pl.BlockSpec((n, experts, 1, toks), lambda i, sc: (0, 0, 0, 0))
    lines = n * experts
    return pl.pallas_call(
        functools.partial(hidden_kernel, n, experts),
        out_shape=(jax.ShapeDtypeStruct((experts, f, n * toks), BF), row, row),
        grid_spec=pltpu.PrefetchScalarGridSpec(
            num_scalar_prefetch=1,
            grid=(1,),
            in_specs=[
                pl.BlockSpec((lines, toks), lambda i, sc: ((n - 1) * toks // lines, 0)),
                pl.BlockSpec((1, experts, n, hid.shape[3], f), lambda i, sc: (0, 0, 0, 0, sc[1] if whole else 0)),
            ],
            out_specs=(
                pl.BlockSpec((experts, f, n * toks), lambda i, sc: (0, 0, 0)),
                row_spec,
                row_spec,
            ),
        ),
        compiler_params=pltpu.CompilerParams(vmem_limit_bytes=12 << 20),
        cost_estimate=SHORT,
    )(scalars, tokens, hid)


def pack_kernel(lefts, sc_ref, hid_ref, tok_ref, out_ref):
    _, experts, n, cap, f = hid_ref.shape
    toks = tok_ref.shape[0]
    blank = jnp.zeros((PADDED - cap, f), BF)
    for e in range(experts):
        for s in range(n):
            at = (e * n + s) * PADDED
            out_ref[at : at + PADDED] = jnp.concatenate([hid_ref[0, e, s], blank], axis=0)
    for i, left in enumerate(lefts):
        at = experts * n * PADDED + i * toks
        out_ref[at : at + toks] = tok_ref[:, left : left + f]


def pack(scalars, hid, tok, lefts, f):
    _, experts, n, cap, _ = hid.shape
    rows = experts * n * PADDED + len(lefts) * tok.shape[0]
    return pl.pallas_call(
        functools.partial(pack_kernel, lefts),
        out_shape=jax.ShapeDtypeStruct((rows, f), BF),
        grid_spec=pltpu.PrefetchScalarGridSpec(
            num_scalar_prefetch=1,
            grid=(1,),
            in_specs=[
                pl.BlockSpec((1, experts, n, cap, f), lambda i, sc: (0, 0, 0, 0, 1 - sc[1])),
                pl.BlockSpec(tok.shape, lambda i, sc: (0, 0)),
            ],
            out_specs=pl.BlockSpec((rows, f), lambda i, sc: (0, 0)),
        ),
        compiler_params=pltpu.CompilerParams(vmem_limit_bytes=12 << 20),
        cost_estimate=SHORT,
    )(scalars, hid, tok)


def below_kernel(n, experts, sc_ref, *refs):
    *blocks, out_ref = refs
    z = sc_ref[0]
    toks = blocks[0].shape[0] - EXPERTS // 2
    line = iota((EXPERTS, toks), 0)

    def local(ref):
        table = ref[toks:, : 2 * toks].astype(F32)
        table = jnp.concatenate([table[:, :toks], table[:, toks:]], axis=0)
        return [
            jnp.sum(jnp.where(line == z * experts + e, table, 0.0), axis=0, keepdims=True)
            for e in range(experts)
        ]

    tables = [local(blocks[k]) for k in range(n)]
    for k in range(1, n):
        out_ref[(k - 1) * toks : k * toks] = blocks[k][:toks]
    if len(blocks) > n:
        passed = blocks[n]
        rows = local(passed)
        for k, place in ((1, 0), (n - 1, n - 1)):
            tables[k] = [jnp.where(z == place, new, old) for new, old in zip(rows, tables[k])]

            @pl.when(z == place)
            def _():
                out_ref[(k - 1) * toks : k * toks] = passed[:toks]

    rows = [row for table in tables for row in table]
    out_ref[(n - 1) * toks :, :toks] = jnp.concatenate(rows, axis=0).astype(BF)


def below(n, experts, scalars, blocks):
    rows, cols = blocks[0].shape
    toks = rows - EXPERTS // 2
    height = (n - 1) * toks + n * experts
    return pl.pallas_call(
        functools.partial(below_kernel, n, experts),
        out_shape=jax.ShapeDtypeStruct((height, cols), BF),
        grid_spec=pltpu.PrefetchScalarGridSpec(
            num_scalar_prefetch=1,
            grid=(1,),
            in_specs=[pl.BlockSpec((rows, cols), lambda i, sc: (0, 0))] * len(blocks),
            out_specs=pl.BlockSpec((height, cols), lambda i, sc: (0, 0)),
        ),
        compiler_params=pltpu.CompilerParams(vmem_limit_bytes=24 << 20),
        cost_estimate=SHORT,
    )(scalars, *blocks)


def flat(pieces):
    arrays = [a for chunk in pieces for a, _, _ in chunk]
    specs = [
        pl.BlockSpec(shape, functools.partial(lambda at, i, sc: at, at))
        for chunk in pieces
        for _, shape, at in chunk
    ]
    return arrays, specs, [len(chunk) for chunk in pieces]


def gathered(refs, counts, n, z, spans=None):
    chunks, at = [], 0
    for i, count in enumerate(counts):
        cols = slice(*spans[i]) if spans else slice(None)
        pieces = [refs[at + k][:, cols] for k in range(count)]
        if count > n:
            passed = pieces.pop()
            for k, place in ((1, 0), (n - 1, n - 1)):
                pieces[k] = jnp.where(z == place, passed, pieces[k])
        chunks.append(pieces[0] if len(pieces) == 1 else jnp.concatenate(pieces, axis=0))
        at += count
    return chunks, at


def back_kernel(n, counts, group, rels, sc_ref, *refs):
    chunks, at = gathered(refs, counts, n, sc_ref[0])
    w_refs, refs = refs[at : at + len(rels)], refs[at + len(rels) :]
    hid_ref, wt_ref, rank_ref, *added, gh_ref, sg_ref, w_all = refs
    toks, (f, d) = wt_ref.shape[3], w_all.shape[1:]
    for rel, ref in zip(rels, w_refs):
        rows = ref.shape[2]
        start = 0 if rel is None else pl.multiple_of((sc_ref[2] ^ rel) * rows, rows)
        for e in range(group):
            w_all[e, pl.ds(start, rows), :] = ref[0, e]
    tokens = chunks[0] if len(chunks) == 1 else jnp.concatenate(chunks, axis=1)
    z = lax.dot_general(
        tokens, w_all[...].reshape(group * f, d), (((1,), (1,)), ((), ())), preferred_element_type=F32
    )
    eye = iota((toks, toks), 0) == iota((toks, toks), 1)
    slots = iota((CAP, toks), 0).astype(F32)
    for e in range(group):
        for k in range(n):
            s = lax.rem(sc_ref[0] + n - k, n)
            w_row, r_row = wt_ref[k, e], rank_ref[k, e]
            here = (slots == r_row) & (w_row > 0)
            pick = jnp.where(here, 1.0, 0.0).astype(BF)
            weigh = jnp.where(here, w_row, 0.0).astype(BF)
            zk = z[k * toks : (k + 1) * toks, e * f : (e + 1) * f]
            gh_ref[e, s] = jnp.dot(weigh, zk.astype(BF), preferred_element_type=F32).astype(BF)
            hid = lax.dot_general(
                pick, hid_ref[0, e, s][:CAP], (((0,), (0,)), ((), ())), preferred_element_type=F32
            )
            sg_col = jnp.sum(zk * hid, axis=1, keepdims=True)
            sg_row = jnp.sum(jnp.where(eye, sg_col, 0.0), axis=0, keepdims=True)
            sg_ref[s, e] = sg_row + added[0][s, e] if added else sg_row


def backward(n, scalars, pieces, w_pieces, f, hid, wt, rank, *added):
    _, experts, band, d = w_pieces[0][1].shape
    toks = wt.shape[3]
    rels = [rel for rel, _, _ in w_pieces]
    group = 2 if experts % 2 == 0 else 1
    arrays, specs, counts = flat(pieces)
    whole = len(added) > 0
    row_spec = pl.BlockSpec((n, group, 1, toks), lambda e, sc: (0, e, 0, 0))
    return pl.pallas_call(
        functools.partial(back_kernel, n, counts, group, rels),
        out_shape=(
            jax.ShapeDtypeStruct((experts, n, CAP, 2 * f if whole else f), BF),
            jax.ShapeDtypeStruct((n, experts, 1, toks), F32),
        ),
        grid_spec=pltpu.PrefetchScalarGridSpec(
            num_scalar_prefetch=1,
            grid=(experts // group,),
            in_specs=specs
            + [
                pl.BlockSpec((1, group, band, d), functools.partial(lambda i, e, sc: (i, e, 0, 0), i))
                for _, _, i in w_pieces
            ]
            + [
                pl.BlockSpec((1, group, n, hid.shape[3], f), lambda e, sc: (0, e, 0, 0, sc[1] if whole else 0)),
                row_spec,
                row_spec,
                *[row_spec] * len(added),
            ],
            out_specs=(pl.BlockSpec((group, n, CAP, f), lambda e, sc: (e, 0, 0, sc[1] if whole else 0)), row_spec),
            scratch_shapes=[pltpu.VMEM((group, f, d), BF)],
        ),
        compiler_params=pltpu.CompilerParams(vmem_limit_bytes=24 << 20),
        cost_estimate=SHORT,
    )(scalars, *arrays, *[w for _, w, _ in w_pieces], hid, wt, rank, *added)


def part_kernel(n, bands, counts, spans, sc_ref, *refs):
    own, at_own = gathered(refs, counts[0], n, sc_ref[0], spans)
    nb, at_nb = gathered(refs[at_own:], counts[1], n, sc_ref[0], spans)
    own_ref, nb_ref, *send_refs, keep_ref = refs[at_own + at_nb :]
    tokens = jnp.concatenate(
        [jnp.concatenate(c, axis=1) if len(c) > 1 else c[0] for c in (own, nb)], axis=0
    )
    hidden = jnp.concatenate([own_ref[0], nb_ref[0]], axis=1)
    total = jnp.dot(hidden, tokens, preferred_element_type=F32)
    quarter, _, band, cols = keep_ref.shape
    total = total.reshape(bands // 2, band, cols).astype(BF)
    for a in range(bands // 2):
        rel = (sc_ref[2] % (bands // 2)) ^ a
        at = rel // 2

        @pl.when(rel % 2 == 1)
        def _():
            done = 0
            for ref in send_refs:
                width = ref.shape[3]
                ref[at, 0] = total[a, :, done : done + width]
                done += width

        @pl.when(rel % 2 == 0)
        def _():
            keep_ref[at, 0] = total[a]


def partial_grad(n, bands, band, far, parts, scalars, own, nb, pieces_own, pieces_nb, spans):
    experts, f, k = own.shape
    arrays, specs, counts = flat(pieces_own)
    arrays_nb, specs_nb, counts_nb = flat(pieces_nb)
    cols = sum(stop - start for start, stop in spans)
    widths = (*parts, cols)
    half = bands // 2
    hs_spec = pl.BlockSpec((1, f // 2, k), lambda e, sc: (e, (sc[2] // half) ^ int(far), 0))
    return pl.pallas_call(
        functools.partial(part_kernel, n, bands, (counts, counts_nb), spans),
        out_shape=[jax.ShapeDtypeStruct((bands // 4, experts, band, width), BF) for width in widths],
        grid_spec=pltpu.PrefetchScalarGridSpec(
            num_scalar_prefetch=1,
            grid=(experts,),
            in_specs=specs + specs_nb + [hs_spec, hs_spec],
            out_specs=[pl.BlockSpec((bands // 4, 1, band, width), lambda e, sc: (0, e, 0, 0)) for width in widths],
        ),
        compiler_params=pltpu.CompilerParams(vmem_limit_bytes=20 << 20),
        cost_estimate=SHORT,
    )(scalars, *arrays, *arrays_nb, own, nb)


def joined_kernel(groups, *refs):
    total, at = None, 0
    for count in groups:
        parts = [ref[...].astype(F32) for ref in refs[at : at + count]]
        term = parts[0] if count == 1 else jnp.concatenate(parts, axis=3)
        total = term if total is None else total + term
        at += count
    refs[-1][...] = total.astype(BF)


def joined(terms):
    arrays = [part for term in terms for part in term]
    lead, experts, band, _ = arrays[0].shape
    d = sum(part.shape[3] for part in terms[0])
    block = lambda x: pl.BlockSpec((x.shape[0], 1, *x.shape[2:]), lambda e: (0, e, 0, 0))
    out, spec = (lead, experts, band, d), pl.BlockSpec((lead, 1, band, d), lambda e: (0, e, 0, 0))
    return pl.pallas_call(
        functools.partial(joined_kernel, [len(term) for term in terms]),
        out_shape=jax.ShapeDtypeStruct(out, BF),
        grid=(experts,),
        in_specs=[block(x) for x in arrays],
        out_specs=spec,
        compiler_params=pltpu.CompilerParams(vmem_limit_bytes=8 << 20),
        cost_estimate=SHORT,
    )(*arrays)


def finish_kernel(sc_ref, base_ref, *refs):
    *there, new_ref, _, down_ref, hidden_ref = refs
    others = [ref[0, 0].astype(F32) for ref in there]
    others = others[0] if len(others) == 1 else jnp.concatenate(others, axis=1)
    down_ref[0] = (base_ref[0, 0].astype(F32) + others).astype(BF)
    hidden_ref[...] = new_ref[...]


def finish(scalars, base, there, new, whole):
    _, experts, band, d = base.shape
    _, n, cap, f = new.shape
    sums = lambda x: pl.BlockSpec((1, 1, band, x.shape[3]), lambda e, sc: (0, e, 0, 0))
    return pl.pallas_call(
        finish_kernel,
        out_shape=(jax.ShapeDtypeStruct((experts, band, d), BF), jax.ShapeDtypeStruct(whole.shape, BF)),
        grid_spec=pltpu.PrefetchScalarGridSpec(
            num_scalar_prefetch=1,
            grid=(experts,),
            in_specs=[
                *[sums(x) for x in (base, *there)],
                pl.BlockSpec((1, n, cap, f), lambda e, sc: (e, 0, 0, 0)),
                pl.BlockSpec(memory_space=pl.ANY),
            ],
            out_specs=(
                pl.BlockSpec((1, band, d), lambda e, sc: (e, 0, 0)),
                pl.BlockSpec((1, n, cap, f), lambda e, sc: (e, 0, 0, 1 - sc[1])),
            ),
        ),
        input_output_aliases={3 + len(there): 1},
        compiler_params=pltpu.CompilerParams(vmem_limit_bytes=12 << 20),
        cost_estimate=SHORT,
    )(scalars, base, *there, new, whole)


def per_device(n_dp, n, grad_out, expert_ids, route_weights, hidden_cache, w_down):
    dp, z = lax.axis_index("dp"), lax.axis_index("expert")
    bands = n_dp // 2
    upper, j = dp // bands, dp % bands
    experts, band, d = w_down.shape
    toks = grad_out.shape[0]
    f = bands * band

    def swap(x, bit):
        return lax.ppermute(x, "dp", [(i, i ^ bit) for i in range(n_dp)])

    def spread(x):
        if n != 4:
            return [x] + [
                lax.ppermute(x, "expert", [(i, (i + k) % n) for i in range(n)]) for k in range(1, n)
            ]
        two = lax.ppermute(x, "expert", [(i, (i + 2) % n) for i in range(n)])
        one = lax.ppermute(x, "expert", [(i, i + 1) for i in range(n - 1)])
        three = lax.ppermute(x, "expert", [(i + 1, i) for i in range(n - 1)])
        passed = lax.ppermute(two, "expert", [(2, 3), (1, 0)])
        return [x, one, two, three, passed]

    ids = expert_ids[None] == jnp.arange(EXPERTS, dtype=jnp.int32)[:, None, None]
    table = jnp.sum(jnp.where(ids, route_weights.astype(F32)[None], 0.0), axis=2).astype(BF)

    cut = 11 * d // 16
    table = jnp.concatenate([table[: EXPERTS // 2], table[EXPERTS // 2 :]], axis=1)
    table = jnp.pad(table, ((0, 0), (0, cut - 2 * toks)))
    blocks = spread(jnp.concatenate([grad_out[:, :cut], table], axis=0))
    w_core = swap(w_down[None], 1)
    scalars = jnp.stack([z, upper, j]).astype(jnp.int32)
    lefts = [min(left, d - f) for left in range(0, d, f)]
    outgoing = pack(scalars, hidden_cache, grad_out, lefts, f)
    incoming = swap(after(outgoing, w_core), bands)
    count = experts * n * PADDED
    hid_nb = incoming[:count].reshape(1, experts, n, PADDED, f)
    first_nb = jnp.concatenate(
        [incoming[count + i * toks : count + (i + 1) * toks, i * f - left :] for i, left in enumerate(lefts)], axis=1
    )
    first_nb, pair = first_nb[:, :cut], first_nb[:, cut:]
    w_pieces = [(0, w_down[None], 0), (1, w_core, 0)]
    bit = 2
    while bit < bands:
        far = swap(w_down[None] if bit == 2 else jnp.concatenate([a for _, a, _ in w_pieces[::2]]), bit)
        there = swap(far, 1)
        for i in range(far.shape[0]):
            w_pieces += [(w_pieces[2 * i][0] ^ bit, far, i), (w_pieces[2 * i][0] ^ bit ^ 1, there, i)]
        bit *= 2

    mine = below(n, experts, scalars, blocks)
    hs_own, wt_own, rank_own = hidden_to_tokens(n, experts, toks, scalars, mine, hidden_cache, f, True)
    rest = jnp.concatenate([grad_out[:, cut:], pair], axis=0)
    rests = spread(after(rest, *blocks))
    nb_a = swap(after(mine, incoming), bands)
    hs_nb, wt_nb, rank_nb = hidden_to_tokens(n, experts, toks, scalars, nb_a, hid_nb, f, False)

    own_pieces = [[(blocks[0], (toks, cut), (0, 0)), (mine, ((n - 1) * toks, cut), (0, 0))], [(b, (toks, d - cut), (0, 0)) for b in rests]]
    nb_pieces = [[(first_nb, (toks, cut), (0, 0)), (nb_a, ((n - 1) * toks, cut), (0, 0))], [(b, (toks, d - cut), (1, 0)) for b in rests]]

    if band % 16:
        w = jnp.zeros((experts, f, d), BF)
        for r, array, i in w_pieces:
            w = lax.dynamic_update_slice(w, array[i], (0, (j ^ r) * band, 0))
        w_pieces = [(None, w[None], 0)]

    half, first = d // 2, 7 * d // 16
    groups = (
        (slice(0, 1), ((0, first),), 1),
        (slice(0, 2), ((first, cut), (0, d - cut)), 1),
    )
    order, sums = scalars, []
    for chunks, spans, parts in groups:
        tokens = own_pieces[chunks], nb_pieces[chunks], spans
        width = sum(stop - start for start, stop in spans) // parts
        *far, keep_far = partial_grad(n, bands, band, True, (width,) * parts, order, hs_own, hs_nb, *tokens)
        order = after(scalars, far[0])
        here = [swap(after(x, *rests) if not sums else x, 1) for x in far]
        sums.append(joined([[keep_far], here]))
    there = [swap(x, bands // 2) for x in sums]
    gh_nb, sg_nb = backward(
        n, after(order, sums[0]), nb_pieces, w_pieces, f, hid_nb, wt_nb, rank_nb
    )
    sg_in = swap(sg_nb, bands)
    gh_own, sg_own = backward(
        n, after(scalars, sg_in), own_pieces, w_pieces, f, hidden_cache, wt_own, rank_own, sg_in
    )
    by_expert = lax.all_to_all(sg_own, "expert", split_axis=0, concat_axis=0, tiled=True)
    spans = ((0, cut), (0, d - cut))
    *near, keep = partial_grad(
        n, bands, band, False, (half, half), after(scalars, sg_nb), hs_own, hs_nb, own_pieces, nb_pieces, spans
    )
    base = joined([[keep], [swap(after(x, there[0], sg_own), 1) for x in near]])
    mid = bands // 8
    there = there if mid == 0 else [jnp.concatenate(there, axis=3)]
    while mid:
        total = base.astype(F32) + there[0].astype(F32)
        base, there, mid = total[:mid].astype(BF), [swap(total[mid:].astype(BF), 4 * mid)], mid // 2
    gh_in = swap(after(gh_nb, sg_in, sums[1], keep), bands)
    grad_down, grad_hidden = finish(scalars, base, there, gh_in, gh_own)
    by_expert = by_expert.reshape(EXPERTS, 1, toks)
    chosen = expert_ids.T[None] == jnp.arange(EXPERTS, dtype=jnp.int32)[:, None, None]
    grad_probs = jnp.sum(jnp.where(chosen, by_expert, 0.0), axis=0).T
    return grad_hidden[None], grad_down, grad_probs


def solution(mesh):
    tokens = P(("dp", "expert"), None)
    cache = P("dp", "expert", None, None, None)
    weights = P("expert", "dp", None)
    return jax.shard_map(
        functools.partial(per_device, mesh.shape["dp"], mesh.shape["expert"]),
        mesh=mesh,
        in_specs=(tokens, tokens, tokens, cache, weights),
        out_specs=(cache, weights, tokens),
        check_vma=False,
    )
```

```python
import functools

import jax
import jax.numpy as jnp
from jax import lax
from jax.experimental import pallas as pl
from jax.experimental.pallas import tpu as pltpu
from jax.sharding import PartitionSpec as P

EXPERTS = 16
CAP = 72
PADDED = 80
BF = jnp.bfloat16
F32 = jnp.float32
SHORT = pl.CostEstimate(flops=1, bytes_accessed=1, transcendentals=0)


def iota(shape, dim):
    return lax.broadcasted_iota(jnp.int32, shape, dim)


def after(x, *others):
    return lax.optimization_barrier((x, *others))[0]


def hidden_kernel(n, experts, sc_ref, tab_ref, hid_ref, hst_ref, wt_ref, rank_ref):
    toks = tab_ref.shape[1]
    earlier = (iota((toks, toks), 0) < iota((toks, toks), 1)).astype(BF)
    slots = iota((CAP, toks), 0).astype(F32)
    table = tab_ref[...].astype(F32)
    rank = jnp.dot((table > 0).astype(F32).astype(BF), earlier, preferred_element_type=F32)
    for k in range(n):
        s = lax.rem(sc_ref[0] + n - k, n)
        for e in range(experts):
            at = k * experts + e
            w_row, r_row = table[at : at + 1], rank[at : at + 1]
            place = jnp.where(slots == r_row, w_row, 0.0).astype(BF)
            moved = lax.dot_general(
                hid_ref[0, e, s][:CAP], place, (((0,), (0,)), ((), ())), preferred_element_type=F32
            )
            hst_ref[e, :, k * toks : (k + 1) * toks] = moved.astype(BF)
            wt_ref[k, e] = w_row
            rank_ref[k, e] = r_row


def hidden_to_tokens(n, experts, toks, scalars, tokens, hid, f, whole):
    row = jax.ShapeDtypeStruct((n, experts, 1, toks), F32)
    row_spec = pl.BlockSpec((n, experts, 1, toks), lambda i, sc: (0, 0, 0, 0))
    lines = n * experts
    return pl.pallas_call(
        functools.partial(hidden_kernel, n, experts),
        out_shape=(jax.ShapeDtypeStruct((experts, f, n * toks), BF), row, row),
        grid_spec=pltpu.PrefetchScalarGridSpec(
            num_scalar_prefetch=1,
            grid=(1,),
            in_specs=[
                pl.BlockSpec((lines, toks), lambda i, sc: ((n - 1) * toks // lines, 0)),
                pl.BlockSpec((1, experts, n, hid.shape[3], f), lambda i, sc: (0, 0, 0, 0, sc[1] if whole else 0)),
            ],
            out_specs=(
                pl.BlockSpec((experts, f, n * toks), lambda i, sc: (0, 0, 0)),
                row_spec,
                row_spec,
            ),
        ),
        compiler_params=pltpu.CompilerParams(vmem_limit_bytes=12 << 20),
        cost_estimate=SHORT,
    )(scalars, tokens, hid)


def pack_kernel(lefts, sc_ref, hid_ref, tok_ref, out_ref):
    _, experts, n, cap, f = hid_ref.shape
    toks = tok_ref.shape[0]
    blank = jnp.zeros((PADDED - cap, f), BF)
    for e in range(experts):
        for s in range(n):
            at = (e * n + s) * PADDED
            out_ref[at : at + PADDED] = jnp.concatenate([hid_ref[0, e, s], blank], axis=0)
    for i, left in enumerate(lefts):
        at = experts * n * PADDED + i * toks
        out_ref[at : at + toks] = tok_ref[:, left : left + f]


def pack(scalars, hid, tok, lefts, f):
    _, experts, n, cap, _ = hid.shape
    rows = experts * n * PADDED + len(lefts) * tok.shape[0]
    return pl.pallas_call(
        functools.partial(pack_kernel, lefts),
        out_shape=jax.ShapeDtypeStruct((rows, f), BF),
        grid_spec=pltpu.PrefetchScalarGridSpec(
            num_scalar_prefetch=1,
            grid=(1,),
            in_specs=[
                pl.BlockSpec((1, experts, n, cap, f), lambda i, sc: (0, 0, 0, 0, 1 - sc[1])),
                pl.BlockSpec(tok.shape, lambda i, sc: (0, 0)),
            ],
            out_specs=pl.BlockSpec((rows, f), lambda i, sc: (0, 0)),
        ),
        compiler_params=pltpu.CompilerParams(vmem_limit_bytes=12 << 20),
        cost_estimate=SHORT,
    )(scalars, hid, tok)


def below_kernel(n, experts, sc_ref, *refs):
    *blocks, out_ref = refs
    z = sc_ref[0]
    toks = blocks[0].shape[0] - EXPERTS // 2
    line = iota((EXPERTS, toks), 0)

    def local(ref):
        table = ref[toks:, : 2 * toks].astype(F32)
        table = jnp.concatenate([table[:, :toks], table[:, toks:]], axis=0)
        return [
            jnp.sum(jnp.where(line == z * experts + e, table, 0.0), axis=0, keepdims=True)
            for e in range(experts)
        ]

    tables = [local(blocks[k]) for k in range(n)]
    for k in range(1, n):
        out_ref[(k - 1) * toks : k * toks] = blocks[k][:toks]
    if len(blocks) > n:
        passed = blocks[n]
        rows = local(passed)
        for k, place in ((1, 0), (n - 1, n - 1)):
            tables[k] = [jnp.where(z == place, new, old) for new, old in zip(rows, tables[k])]

            @pl.when(z == place)
            def _():
                out_ref[(k - 1) * toks : k * toks] = passed[:toks]

    rows = [row for table in tables for row in table]
    out_ref[(n - 1) * toks :, :toks] = jnp.concatenate(rows, axis=0).astype(BF)


def below(n, experts, scalars, blocks):
    rows, cols = blocks[0].shape
    toks = rows - EXPERTS // 2
    height = (n - 1) * toks + n * experts
    return pl.pallas_call(
        functools.partial(below_kernel, n, experts),
        out_shape=jax.ShapeDtypeStruct((height, cols), BF),
        grid_spec=pltpu.PrefetchScalarGridSpec(
            num_scalar_prefetch=1,
            grid=(1,),
            in_specs=[pl.BlockSpec((rows, cols), lambda i, sc: (0, 0))] * len(blocks),
            out_specs=pl.BlockSpec((height, cols), lambda i, sc: (0, 0)),
        ),
        compiler_params=pltpu.CompilerParams(vmem_limit_bytes=24 << 20),
        cost_estimate=SHORT,
    )(scalars, *blocks)


def flat(pieces):
    arrays = [a for chunk in pieces for a, _, _ in chunk]
    specs = [
        pl.BlockSpec(shape, functools.partial(lambda at, i, sc: at, at))
        for chunk in pieces
        for _, shape, at in chunk
    ]
    return arrays, specs, [len(chunk) for chunk in pieces]


def gathered(refs, counts, n, z, spans=None):
    chunks, at = [], 0
    for i, count in enumerate(counts):
        cols = slice(*spans[i]) if spans else slice(None)
        pieces = [refs[at + k][:, cols] for k in range(count)]
        if count > n:
            passed = pieces.pop()
            for k, place in ((1, 0), (n - 1, n - 1)):
                pieces[k] = jnp.where(z == place, passed, pieces[k])
        chunks.append(pieces[0] if len(pieces) == 1 else jnp.concatenate(pieces, axis=0))
        at += count
    return chunks, at


def back_kernel(n, counts, group, rels, sc_ref, *refs):
    chunks, at = gathered(refs, counts, n, sc_ref[0])
    w_refs, refs = refs[at : at + len(rels)], refs[at + len(rels) :]
    hid_ref, wt_ref, rank_ref, *added, gh_ref, sg_ref, w_all = refs
    toks, (f, d) = wt_ref.shape[3], w_all.shape[1:]
    for rel, ref in zip(rels, w_refs):
        rows = ref.shape[2]
        start = 0 if rel is None else pl.multiple_of((sc_ref[2] ^ rel) * rows, rows)
        for e in range(group):
            w_all[e, pl.ds(start, rows), :] = ref[0, e]
    tokens = chunks[0] if len(chunks) == 1 else jnp.concatenate(chunks, axis=1)
    z = lax.dot_general(
        tokens, w_all[...].reshape(group * f, d), (((1,), (1,)), ((), ())), preferred_element_type=F32
    )
    eye = iota((toks, toks), 0) == iota((toks, toks), 1)
    slots = iota((CAP, toks), 0).astype(F32)
    for e in range(group):
        for k in range(n):
            s = lax.rem(sc_ref[0] + n - k, n)
            w_row, r_row = wt_ref[k, e], rank_ref[k, e]
            here = (slots == r_row) & (w_row > 0)
            pick = jnp.where(here, 1.0, 0.0).astype(BF)
            weigh = jnp.where(here, w_row, 0.0).astype(BF)
            zk = z[k * toks : (k + 1) * toks, e * f : (e + 1) * f]
            gh_ref[e, s] = jnp.dot(weigh, zk.astype(BF), preferred_element_type=F32).astype(BF)
            hid = lax.dot_general(
                pick, hid_ref[0, e, s][:CAP], (((0,), (0,)), ((), ())), preferred_element_type=F32
            )
            sg_col = jnp.sum(zk * hid, axis=1, keepdims=True)
            sg_row = jnp.sum(jnp.where(eye, sg_col, 0.0), axis=0, keepdims=True)
            sg_ref[s, e] = sg_row + added[0][s, e] if added else sg_row


def backward(n, scalars, pieces, w_pieces, f, hid, wt, rank, *added):
    _, experts, band, d = w_pieces[0][1].shape
    toks = wt.shape[3]
    rels = [rel for rel, _, _ in w_pieces]
    group = 2 if experts % 2 == 0 else 1
    arrays, specs, counts = flat(pieces)
    whole = len(added) > 0
    row_spec = pl.BlockSpec((n, group, 1, toks), lambda e, sc: (0, e, 0, 0))
    return pl.pallas_call(
        functools.partial(back_kernel, n, counts, group, rels),
        out_shape=(
            jax.ShapeDtypeStruct((experts, n, CAP, 2 * f if whole else f), BF),
            jax.ShapeDtypeStruct((n, experts, 1, toks), F32),
        ),
        grid_spec=pltpu.PrefetchScalarGridSpec(
            num_scalar_prefetch=1,
            grid=(experts // group,),
            in_specs=specs
            + [
                pl.BlockSpec((1, group, band, d), functools.partial(lambda i, e, sc: (i, e, 0, 0), i))
                for _, _, i in w_pieces
            ]
            + [
                pl.BlockSpec((1, group, n, hid.shape[3], f), lambda e, sc: (0, e, 0, 0, sc[1] if whole else 0)),
                row_spec,
                row_spec,
                *[row_spec] * len(added),
            ],
            out_specs=(pl.BlockSpec((group, n, CAP, f), lambda e, sc: (e, 0, 0, sc[1] if whole else 0)), row_spec),
            scratch_shapes=[pltpu.VMEM((group, f, d), BF)],
        ),
        compiler_params=pltpu.CompilerParams(vmem_limit_bytes=24 << 20),
        cost_estimate=SHORT,
    )(scalars, *arrays, *[w for _, w, _ in w_pieces], hid, wt, rank, *added)


def part_kernel(n, bands, counts, spans, sc_ref, *refs):
    own, at_own = gathered(refs, counts[0], n, sc_ref[0], spans)
    nb, at_nb = gathered(refs[at_own:], counts[1], n, sc_ref[0], spans)
    own_ref, nb_ref, *send_refs, keep_ref = refs[at_own + at_nb :]
    tokens = jnp.concatenate(
        [jnp.concatenate(c, axis=1) if len(c) > 1 else c[0] for c in (own, nb)], axis=0
    )
    hidden = jnp.concatenate([own_ref[0], nb_ref[0]], axis=1)
    total = jnp.dot(hidden, tokens, preferred_element_type=F32)
    quarter, _, band, cols = keep_ref.shape
    total = total.reshape(bands // 2, band, cols).astype(BF)
    for a in range(bands // 2):
        rel = (sc_ref[2] % (bands // 2)) ^ a
        at = rel // 2

        @pl.when(rel % 2 == 1)
        def _():
            done = 0
            for ref in send_refs:
                width = ref.shape[3]
                ref[at, 0] = total[a, :, done : done + width]
                done += width

        @pl.when(rel % 2 == 0)
        def _():
            keep_ref[at, 0] = total[a]


def partial_grad(n, bands, band, far, parts, scalars, own, nb, pieces_own, pieces_nb, spans):
    experts, f, k = own.shape
    arrays, specs, counts = flat(pieces_own)
    arrays_nb, specs_nb, counts_nb = flat(pieces_nb)
    cols = sum(stop - start for start, stop in spans)
    widths = (*parts, cols)
    half = bands // 2
    hs_spec = pl.BlockSpec((1, f // 2, k), lambda e, sc: (e, (sc[2] // half) ^ int(far), 0))
    return pl.pallas_call(
        functools.partial(part_kernel, n, bands, (counts, counts_nb), spans),
        out_shape=[jax.ShapeDtypeStruct((bands // 4, experts, band, width), BF) for width in widths],
        grid_spec=pltpu.PrefetchScalarGridSpec(
            num_scalar_prefetch=1,
            grid=(experts,),
            in_specs=specs + specs_nb + [hs_spec, hs_spec],
            out_specs=[pl.BlockSpec((bands // 4, 1, band, width), lambda e, sc: (0, e, 0, 0)) for width in widths],
        ),
        compiler_params=pltpu.CompilerParams(vmem_limit_bytes=20 << 20),
        cost_estimate=SHORT,
    )(scalars, *arrays, *arrays_nb, own, nb)


def joined_kernel(groups, *refs):
    total, at = None, 0
    for count in groups:
        parts = [ref[...].astype(F32) for ref in refs[at : at + count]]
        term = parts[0] if count == 1 else jnp.concatenate(parts, axis=3)
        total = term if total is None else total + term
        at += count
    refs[-1][...] = total.astype(BF)


def joined(terms):
    arrays = [part for term in terms for part in term]
    lead, experts, band, _ = arrays[0].shape
    d = sum(part.shape[3] for part in terms[0])
    block = lambda x: pl.BlockSpec((x.shape[0], 1, *x.shape[2:]), lambda e: (0, e, 0, 0))
    out, spec = (lead, experts, band, d), pl.BlockSpec((lead, 1, band, d), lambda e: (0, e, 0, 0))
    return pl.pallas_call(
        functools.partial(joined_kernel, [len(term) for term in terms]),
        out_shape=jax.ShapeDtypeStruct(out, BF),
        grid=(experts,),
        in_specs=[block(x) for x in arrays],
        out_specs=spec,
        compiler_params=pltpu.CompilerParams(vmem_limit_bytes=8 << 20),
        cost_estimate=SHORT,
    )(*arrays)


def finish_kernel(sc_ref, base_ref, *refs):
    *there, new_ref, _, down_ref, hidden_ref = refs
    others = [ref[0].astype(F32) for ref in there]
    others = others[0] if len(others) == 1 else jnp.concatenate(others, axis=2)
    down_ref[...] = (base_ref[0].astype(F32) + others).astype(BF)
    hidden_ref[...] = new_ref[...]


def finish(scalars, base, there, new, whole):
    _, experts, band, d = base.shape
    _, n, cap, f = new.shape
    group = 2 if experts % 2 == 0 else 1
    sums = lambda x: pl.BlockSpec((1, group, band, x.shape[3]), lambda e, sc: (0, e, 0, 0))
    return pl.pallas_call(
        finish_kernel,
        out_shape=(jax.ShapeDtypeStruct((experts, band, d), BF), jax.ShapeDtypeStruct(whole.shape, BF)),
        grid_spec=pltpu.PrefetchScalarGridSpec(
            num_scalar_prefetch=1,
            grid=(experts // group,),
            in_specs=[
                *[sums(x) for x in (base, *there)],
                pl.BlockSpec((group, n, cap, f), lambda e, sc: (e, 0, 0, 0)),
                pl.BlockSpec(memory_space=pl.ANY),
            ],
            out_specs=(
                pl.BlockSpec((group, band, d), lambda e, sc: (e, 0, 0)),
                pl.BlockSpec((group, n, cap, f), lambda e, sc: (e, 0, 0, 1 - sc[1])),
            ),
        ),
        input_output_aliases={3 + len(there): 1},
        compiler_params=pltpu.CompilerParams(vmem_limit_bytes=12 << 20),
        cost_estimate=SHORT,
    )(scalars, base, *there, new, whole)


def per_device(n_dp, n, grad_out, expert_ids, route_weights, hidden_cache, w_down):
    dp, z = lax.axis_index("dp"), lax.axis_index("expert")
    bands = n_dp // 2
    upper, j = dp // bands, dp % bands
    experts, band, d = w_down.shape
    toks = grad_out.shape[0]
    f = bands * band

    def swap(x, bit):
        return lax.ppermute(x, "dp", [(i, i ^ bit) for i in range(n_dp)])

    def spread(x):
        if n != 4:
            return [x] + [
                lax.ppermute(x, "expert", [(i, (i + k) % n) for i in range(n)]) for k in range(1, n)
            ]
        two = lax.ppermute(x, "expert", [(i, (i + 2) % n) for i in range(n)])
        one = lax.ppermute(x, "expert", [(i, i + 1) for i in range(n - 1)])
        three = lax.ppermute(x, "expert", [(i + 1, i) for i in range(n - 1)])
        passed = lax.ppermute(two, "expert", [(2, 3), (1, 0)])
        return [x, one, two, three, passed]

    ids = expert_ids[None] == jnp.arange(EXPERTS, dtype=jnp.int32)[:, None, None]
    table = jnp.sum(jnp.where(ids, route_weights.astype(F32)[None], 0.0), axis=2).astype(BF)

    cut = 11 * d // 16
    table = jnp.concatenate([table[: EXPERTS // 2], table[EXPERTS // 2 :]], axis=1)
    table = jnp.pad(table, ((0, 0), (0, cut - 2 * toks)))
    blocks = spread(jnp.concatenate([grad_out[:, :cut], table], axis=0))
    w_core = swap(w_down[None], 1)
    scalars = jnp.stack([z, upper, j]).astype(jnp.int32)
    lefts = [min(left, d - f) for left in range(0, d, f)]
    outgoing = pack(scalars, hidden_cache, grad_out, lefts, f)
    incoming = swap(after(outgoing, w_core), bands)
    count = experts * n * PADDED
    hid_nb = incoming[:count].reshape(1, experts, n, PADDED, f)
    first_nb = jnp.concatenate(
        [incoming[count + i * toks : count + (i + 1) * toks, i * f - left :] for i, left in enumerate(lefts)], axis=1
    )
    first_nb, pair = first_nb[:, :cut], first_nb[:, cut:]
    w_pieces = [(0, w_down[None], 0), (1, w_core, 0)]
    bit = 2
    while bit < bands:
        far = swap(w_down[None] if bit == 2 else jnp.concatenate([a for _, a, _ in w_pieces[::2]]), bit)
        there = swap(far, 1)
        for i in range(far.shape[0]):
            w_pieces += [(w_pieces[2 * i][0] ^ bit, far, i), (w_pieces[2 * i][0] ^ bit ^ 1, there, i)]
        bit *= 2

    mine = below(n, experts, scalars, blocks)
    hs_own, wt_own, rank_own = hidden_to_tokens(n, experts, toks, scalars, mine, hidden_cache, f, True)
    rest = jnp.concatenate([grad_out[:, cut:], pair], axis=0)
    rests = spread(after(rest, *blocks))
    nb_a = swap(after(mine, incoming), bands)
    hs_nb, wt_nb, rank_nb = hidden_to_tokens(n, experts, toks, scalars, nb_a, hid_nb, f, False)

    own_pieces = [[(blocks[0], (toks, cut), (0, 0)), (mine, ((n - 1) * toks, cut), (0, 0))], [(b, (toks, d - cut), (0, 0)) for b in rests]]
    nb_pieces = [[(first_nb, (toks, cut), (0, 0)), (nb_a, ((n - 1) * toks, cut), (0, 0))], [(b, (toks, d - cut), (1, 0)) for b in rests]]

    if band % 16:
        w = jnp.zeros((experts, f, d), BF)
        for r, array, i in w_pieces:
            w = lax.dynamic_update_slice(w, array[i], (0, (j ^ r) * band, 0))
        w_pieces = [(None, w[None], 0)]

    half, first = d // 2, 7 * d // 16
    groups = (
        (slice(0, 1), ((0, first),), 1),
        (slice(0, 2), ((first, cut), (0, d - cut)), 1),
    )
    order, sums = scalars, []
    for chunks, spans, parts in groups:
        tokens = own_pieces[chunks], nb_pieces[chunks], spans
        width = sum(stop - start for start, stop in spans) // parts
        *far, keep_far = partial_grad(n, bands, band, True, (width,) * parts, order, hs_own, hs_nb, *tokens)
        order = after(scalars, far[0])
        here = [swap(after(x, *rests) if not sums else x, 1) for x in far]
        sums.append(joined([[keep_far], here]))
    there = [swap(x, bands // 2) for x in sums]
    gh_nb, sg_nb = backward(
        n, after(order, sums[0]), nb_pieces, w_pieces, f, hid_nb, wt_nb, rank_nb
    )
    sg_in = swap(sg_nb, bands)
    gh_own, sg_own = backward(
        n, after(scalars, sg_in), own_pieces, w_pieces, f, hidden_cache, wt_own, rank_own, sg_in
    )
    by_expert = lax.all_to_all(sg_own, "expert", split_axis=0, concat_axis=0, tiled=True)
    spans = ((0, cut), (0, d - cut))
    *near, keep = partial_grad(
        n, bands, band, False, (half, half), after(scalars, sg_nb), hs_own, hs_nb, own_pieces, nb_pieces, spans
    )
    base = joined([[keep], [swap(after(x, there[0], sg_own), 1) for x in near]])
    mid = bands // 8
    there = there if mid == 0 else [jnp.concatenate(there, axis=3)]
    while mid:
        total = base.astype(F32) + there[0].astype(F32)
        base, there, mid = total[:mid].astype(BF), [swap(total[mid:].astype(BF), 4 * mid)], mid // 2
    gh_in = swap(after(gh_nb, sg_in, sums[1], keep), bands)
    grad_down, grad_hidden = finish(scalars, base, there, gh_in, gh_own)
    by_expert = by_expert.reshape(EXPERTS, 1, toks)
    chosen = expert_ids.T[None] == jnp.arange(EXPERTS, dtype=jnp.int32)[:, None, None]
    grad_probs = jnp.sum(jnp.where(chosen, by_expert, 0.0), axis=0).T
    return grad_hidden[None], grad_down, grad_probs


def solution(mesh):
    tokens = P(("dp", "expert"), None)
    cache = P("dp", "expert", None, None, None)
    weights = P("expert", "dp", None)
    return jax.shard_map(
        functools.partial(per_device, mesh.shape["dp"], mesh.shape["expert"]),
        mesh=mesh,
        in_specs=(tokens, tokens, tokens, cache, weights),
        out_specs=(cache, weights, tokens),
        check_vma=False,
    )
```
